32 devices in a mesh: groups: 2 (over y), tm: 4 (over z), comp: 2 (over core), panel: 2 (over x).
Axes of the slice: x: 2, y: 2, z: 4, core: 2. Of those that a mesh axis runs over, the one named last changes fastest.
Arguments:
- orbit_angles: float32 [2, 8192], P(None, ('groups', 'tm')), parts along dimension 1, may hold values from -3.15 to 3.15, as said below
- gap_mask: int32 [8192], P(('groups', 'tm')), parts along dimension 0, may hold values 0 or 1
- column_index: int32 [2, 512], P(None, 'panel'), may hold values from -280 to 280, as said below
- lat_coeffs: bfloat16 [2, 640, 512], P('comp', None, 'panel'), may hold values from -6 to 6
- psd_table: int32 [2, 2049], P('comp'), may hold values from 1024 to 32752, as said below
Outputs:
- normals: float32 [1024, 512], P(('groups', 'tm'), 'panel'), parts along dimension 0
The draws below stay inside these ranges and needn't reach their ends.
There are 2 independent parts, one for each index of `groups`. The reference program is written for one: setup_inputs(seed, part) draws one part's arguments, and reference() takes and returns one part's arrays. A program takes and returns all parts, laid end to end along the dimension named above; an argument that names none is the same for every part. Nothing has to cross between parts.
Inputs may be any that keep to these rules, and one draw needn't show every extreme that they name: orbit_angles holds colatitude in its first row and longitude in its second. `column_index`: the first row holds each unknown's degree, the second its order; a degree is at least 2 and at least the order's magnitude; a negative order stands for the sine term in longitude. `psd_table`: entry g of a component's row is its noise power at frequency g (and 4096 - g), times 8192.
All inputs are finite; a program needn't handle non-finite values. No bound on the sum of `gap_mask` on one device may be relied on, other than what follows from the above.
Results may differ from the reference program's by a relative error of at most 0.0016.
Values may be sent and summed in bfloat16 or wider, within the bound.
A program may use at most 64 MiB of HBM per device.

```python
import math
import jax
import jax.numpy as jnp
from jax import lax

DEG = 280
KLAT = 320
UNKNOWNS = 512
TIME_DEV = 1024
SAMPLES = 4096
COMPS = 2


def draw_orbit_angles(key, part):
    key_orbit, key_earth, key_node, key_jitter = jax.random.split(key, 4)
    epochs = jnp.arange(SAMPLES, dtype=jnp.int32)
    period = 5383
    incline = 1.6878
    orbit_start = jax.random.randint(key_orbit, (), 0, period)
    earth_start = jax.random.randint(key_earth, (), 0, 86164)
    ascending = jax.random.uniform(key_node, (), jnp.float32, -math.pi, math.pi)
    lat_argument = ((epochs + orbit_start) % period).astype(jnp.float32) * (2.0 * math.pi / period)
    earth_turn = ((epochs + earth_start) % 86164).astype(jnp.float32) * (2.0 * math.pi / 86164.0)
    colatitude = jnp.arccos(jnp.sin(incline) * jnp.sin(lat_argument))
    colatitude = colatitude + 0.002 * jax.random.normal(key_jitter, (SAMPLES,), jnp.float32)
    raw_lon = ascending - earth_turn + jnp.arctan2(jnp.cos(incline) * jnp.sin(lat_argument), jnp.cos(lat_argument))
    longitude = jnp.arctan2(jnp.sin(raw_lon), jnp.cos(raw_lon))
    return jnp.stack([colatitude, longitude]).astype(jnp.float32)


def draw_column_index(key, part):
    key_order, key_degree, key_pick = jax.random.split(key, 3)
    orders = jax.random.randint(key_order, (UNKNOWNS,), -DEG, DEG + 1)
    lowest = jnp.maximum(jnp.abs(orders), 2)
    spans = DEG + 1 - lowest
    degree = lowest + jax.random.randint(key_degree, (UNKNOWNS,), 0, 1048576) % spans
    picked = jax.random.permutation(key_pick, UNKNOWNS)
    orders = orders.at[picked[0]].set(DEG).at[picked[1]].set(-DEG)
    degree = degree.at[picked[0]].set(DEG).at[picked[1]].set(DEG)
    return jnp.stack([degree, orders]).astype(jnp.int32)


def draw_psd_table(key, part):
    key_mant, key_expo = jax.random.split(key)
    grid_shape = (COMPS, SAMPLES // 2 + 1)
    mantissa = jax.random.randint(key_mant, grid_shape, 1024, 2048)
    exponent = jax.random.randint(key_expo, grid_shape, 0, 5)
    return jnp.left_shift(mantissa, exponent).astype(jnp.int32)


def set_ends(result, own_key, smallest, largest):
    longest = result.shape.index(max(result.shape))
    spots = []
    for shift in (0, 1):
        where = [jax.random.randint(jax.random.fold_in(own_key, axis), (), 0, length) for axis, length in enumerate(result.shape)]
        where[longest] = (where[longest] + shift) % result.shape[longest]
        spots.append(tuple(where))
    return result.at[spots[0]].set(smallest).at[spots[1]].set(largest)


def shard_levels(rng, dims, pieces, low, high):
    factor_of = 1.0
    for axis_at, shards_of in pieces:
        heights = jax.random.uniform(jax.random.fold_in(jax.random.fold_in(rng, 6), axis_at), (shards_of,), jnp.float32, low / len(pieces), high / len(pieces))
        factor_of = factor_of * jnp.repeat(jnp.exp(heights), dims[axis_at] // shards_of).reshape((-1,) + (1,) * (len(dims) - 1 - axis_at))
    return factor_of


def bell_draw(own_key, extent, deviation, reach, cuts=(), held_as=jnp.bfloat16):
    level = shard_levels(own_key, extent, cuts, -0.22, 0.18) if cuts else 1.0
    result = jax.random.normal(own_key, extent, jnp.float32) * deviation * level
    return jnp.minimum(jnp.maximum(result, -reach), reach).astype(held_as)


def setup_inputs(seed: int = 0, part: int = 0) -> dict:
    keys = jax.random.split(jax.random.key(seed), 6)
    own_keys = jax.random.split(jax.random.fold_in(keys[5], part), 6)
    orbit_angles = draw_orbit_angles(jax.random.fold_in(jax.random.fold_in(keys[5], part), 71), part)
    gap_mask = set_ends((jax.random.randint(own_keys[1], (SAMPLES,), 0, 16) < 15).astype(jnp.int32), jax.random.fold_in(own_keys[1], 1), 0, 1)
    column_index = draw_column_index(jax.random.fold_in(keys[5], 71), part)
    lat_coeffs = bell_draw(keys[3], (COMPS, 2 * KLAT, UNKNOWNS), 1.0, 6.0, ((0, 2), (2, 2)))
    psd_table = draw_psd_table(jax.random.fold_in(keys[5], 71), part)
    return dict(orbit_angles=orbit_angles, gap_mask=gap_mask, column_index=column_index, lat_coeffs=lat_coeffs, psd_table=psd_table)


def synthesize(angles, keep_rows, column_index, coeffs):
    terms_lat = coeffs.shape[0] // 2
    colatitude = angles[0]
    longit = angles[1]
    wavenumbers = jnp.arange(terms_lat, dtype=jnp.float32)
    phases = colatitude[:, None] * wavenumbers[None, :]
    basis_rows = jnp.concatenate([jnp.cos(phases), jnp.sin(phases)], axis=1).astype(jnp.bfloat16)
    degree = column_index[0]
    orders = column_index[1]
    levels = jnp.arange(2 * terms_lat, dtype=jnp.int32) % terms_lat
    allowed = levels[:, None] <= degree[None, :]
    masked = jnp.where(allowed, coeffs, jnp.zeros_like(coeffs))
    latitude = jnp.dot(basis_rows, masked, preferred_element_type=jnp.float32)
    lon_phase = longit[:, None] * jnp.abs(orders).astype(jnp.float32)[None, :]
    lon_wave = jnp.where(orders[None, :] >= 0, jnp.cos(lon_phase), jnp.sin(lon_phase))
    norm_scale = 1.0 / jnp.sqrt(degree.astype(jnp.float32) + 1.0)
    return latitude * lon_wave * (keep_rows[:, None] * norm_scale[None, :])

def reference(orbit_angles, gap_mask, column_index, lat_coeffs, psd_table):
    samples = orbit_angles.shape[1]
    keep_rows = gap_mask.astype(jnp.float32)
    frequency = jnp.arange(samples, dtype=jnp.int32)
    folded = jnp.minimum(frequency, samples - frequency)
    starts = jnp.arange(samples // TIME_DEV, dtype=jnp.int32) * TIME_DEV
    normals = jnp.zeros((UNKNOWNS, UNKNOWNS), jnp.float32)
    for comp_index in range(COMPS):
        coeffs = lat_coeffs[comp_index]

        def block_design(start_row):
            angles = lax.dynamic_slice_in_dim(orbit_angles, start_row, TIME_DEV, 1)
            keep_part = lax.dynamic_slice_in_dim(keep_rows, start_row, TIME_DEV, 0)
            return synthesize(angles, keep_part, column_index, coeffs)
        design = lax.map(block_design, starts).reshape(samples, UNKNOWNS)
        spectrum = jnp.fft.fft(design, axis=0) / samples
        spec_real = jnp.real(spectrum).astype(jnp.bfloat16)
        spec_imag = jnp.imag(spectrum).astype(jnp.bfloat16)
        inverse_psd = 8192.0 / psd_table[comp_index][folded].astype(jnp.float32)
        weighted_real = (spec_real.astype(jnp.float32) * inverse_psd[:, None]).astype(jnp.bfloat16)
        weighted_imag = (spec_imag.astype(jnp.float32) * inverse_psd[:, None]).astype(jnp.bfloat16)
        normals = normals + jnp.dot(spec_real.T, weighted_real, preferred_element_type=jnp.float32)
        normals = normals + jnp.dot(spec_imag.T, weighted_imag, preferred_element_type=jnp.float32)
    return normals
```

```python
import functools
import math

import jax
import jax.numpy as jnp
from jax import lax
from jax.experimental import pallas as pl
from jax.experimental.pallas import tpu as pltpu
from jax.sharding import PartitionSpec as P

SPLIT = 64


def synthesize(angles, keep_rows, column_index, coeffs):
    terms_lat = coeffs.shape[0] // 2
    colatitude = angles[0]
    longit = angles[1]
    wavenumbers = jnp.arange(terms_lat, dtype=jnp.float32)
    phases = colatitude[:, None] * wavenumbers[None, :]
    basis_rows = jnp.concatenate([jnp.cos(phases), jnp.sin(phases)], axis=1).astype(jnp.bfloat16)
    degree = column_index[0]
    orders = column_index[1]
    levels = jnp.arange(2 * terms_lat, dtype=jnp.int32) % terms_lat
    allowed = levels[:, None] <= degree[None, :]
    masked = jnp.where(allowed, coeffs, jnp.zeros_like(coeffs))
    latitude = jnp.dot(basis_rows, masked, preferred_element_type=jnp.float32)
    lon_phase = longit[:, None] * jnp.abs(orders).astype(jnp.float32)[None, :]
    lon_wave = jnp.where(orders[None, :] >= 0, jnp.cos(lon_phase), jnp.sin(lon_phase))
    norm_scale = 1.0 / jnp.sqrt(degree.astype(jnp.float32) + 1.0)
    return latitude * lon_wave * (keep_rows[:, None] * norm_scale[None, :])


def phase_tables(row_index, col_index, length):
    product = row_index[:, None] * col_index[None, :] % length
    angle_grid = product.astype(jnp.float32) * (2.0 * math.pi / length)
    return (jnp.cos(angle_grid), jnp.sin(angle_grid))


def dft_tables(length):
    indices = jnp.arange(length, dtype=jnp.int32)
    return phase_tables(indices, indices, length)


def rotate(real_part, imag_part, outer_index, inner_index, length):
    index_grid = outer_index[:, None] * inner_index[None, :] % length
    angle_grid = index_grid.astype(jnp.float32) * (2.0 * math.pi / length)
    cosine = jnp.cos(angle_grid)[:, :, None]
    sine_grid = jnp.sin(angle_grid)[:, :, None]
    return (real_part * cosine + imag_part * sine_grid, imag_part * cosine - real_part * sine_grid)


def precise_dot(left_side, right_side):
    return jnp.dot(
        left_side, right_side, precision=lax.Precision.HIGHEST, preferred_element_type=jnp.float32
    )


def transform(cos_table, sin_table, real_part, imag_part):
    new_real = precise_dot(cos_table, real_part) + precise_dot(sin_table, imag_part)
    new_imag = precise_dot(cos_table, imag_part) - precise_dot(sin_table, real_part)
    return (new_real, new_imag)


def four_step(real_in, imag_in, samples):
    length = real_in.shape[0]
    columns = real_in.shape[1]
    outer_count = SPLIT
    inner_count = length // SPLIT
    real_part = real_in.reshape(outer_count, inner_count * columns)
    imag_part = imag_in.reshape(outer_count, inner_count * columns)
    cos_outer, sin_outer = dft_tables(outer_count)
    real_part, imag_part = transform(cos_outer, sin_outer, real_part, imag_part)
    real_part = real_part.reshape(outer_count, inner_count, columns)
    imag_part = imag_part.reshape(outer_count, inner_count, columns)
    real_part, imag_part = rotate(
        real_part,
        imag_part,
        jnp.arange(outer_count, dtype=jnp.int32),
        jnp.arange(inner_count, dtype=jnp.int32),
        length,
    )
    real_part = jnp.transpose(real_part, (1, 0, 2)).reshape(inner_count, outer_count * columns)
    imag_part = jnp.transpose(imag_part, (1, 0, 2)).reshape(inner_count, outer_count * columns)
    cos_inner, sin_inner = dft_tables(inner_count)
    real_part, imag_part = transform(cos_inner, sin_inner, real_part, imag_part)
    return (
        real_part.reshape(length, columns) / samples,
        imag_part.reshape(length, columns) / samples,
    )


def local_transform(received, samples):
    real_part, imag_part = four_step(received[0, 0], received[1, 0], samples)
    return (real_part.astype(jnp.bfloat16), imag_part.astype(jnp.bfloat16))


def noise_weighted(spectra, psd_row, frequency, samples):
    folded = jnp.minimum(frequency, samples - frequency)
    inverse_psd = 8192.0 / jnp.take(psd_row, folded).astype(jnp.float32)
    return (spectra.astype(jnp.float32) * inverse_psd[None, :, None]).astype(jnp.bfloat16)


def settle(partial_value, sum_dim):
    summed = lax.psum_scatter(partial_value, "tm", scatter_dimension=sum_dim, tiled=True)
    return lax.psum(summed, "comp")


def body(orbit_angles, gap_mask, column_index, lat_coeffs, psd_table):
    devices_tm = lax.axis_size("tm")
    epochs = orbit_angles.shape[1]
    block_len = epochs // devices_tm
    samples = epochs * devices_tm
    columns = lat_coeffs.shape[2]
    coeffs = lat_coeffs[0]
    keep_rows = gap_mask.astype(jnp.float32)
    packed = jnp.concatenate([orbit_angles, keep_rows[None]], axis=0)[:, None, :]
    received = lax.all_to_all(packed, "tm", split_axis=2, concat_axis=1, tiled=True)
    flat_orbit = received.reshape(3, devices_tm * block_len)
    spread = synthesize(flat_orbit[0:2], flat_orbit[2], column_index, coeffs).reshape(
        devices_tm, block_len, columns
    )
    position = lax.axis_index("tm")
    local_epoch = position * block_len + jnp.arange(block_len, dtype=jnp.int32)
    cos_outer, sin_outer = dft_tables(devices_tm)
    flat_design = spread.reshape(devices_tm, block_len * columns)
    real_part = precise_dot(cos_outer, flat_design).reshape(devices_tm, block_len, columns)
    imag_part = -precise_dot(sin_outer, flat_design).reshape(devices_tm, block_len, columns)
    real_part, imag_part = rotate(
        real_part, imag_part, jnp.arange(devices_tm, dtype=jnp.int32), local_epoch, samples
    )
    twisted = jnp.stack([real_part, imag_part])
    spec_real, spec_imag = local_transform(
        lax.all_to_all(twisted, "tm", split_axis=1, concat_axis=2, tiled=True), samples
    )
    spectra = jnp.stack([spec_real, spec_imag])
    psd_row = psd_table[0]
    contract = (((0, 1), (0, 1)), ((), ()))
    frequency = position + devices_tm * jnp.arange(epochs, dtype=jnp.int32)
    weighted = noise_weighted(spectra, psd_row, frequency, samples)
    partial_value = lax.dot_general(
        lax.all_gather(spectra, "panel", axis=2, tiled=True),
        weighted,
        contract,
        preferred_element_type=jnp.float32,
    )
    return settle(partial_value, 0)


RADIX = 16
SINE_LON = (6.283164044168851, -41.33714234995496, 81.34076808172247, -70.99342472149007)
SINE_FINE = (
    6.283185160088548,
    -41.3416550311802,
    81.60100405747373,
    -76.54978191007581,
    39.53670300634923,
)
CLASSES = (1, 2, 13, 4, 5, 6, 9)
MESH = pl.DeviceIdType.MESH


def cos_turns(turns, terms=SINE_FINE):
    offset = turns - jnp.floor(turns + 0.5)
    near = 0.25 - jnp.abs(offset)
    square = near * near
    total = terms[-1]
    for term in terms[-2::-1]:
        total = total * square + term
    return total * near


def iota(shape, dim):
    return lax.broadcasted_iota(jnp.int32, shape, dim)


def put_split(high_ref, low_ref, where, value):
    high = value.astype(jnp.bfloat16)
    high_ref[where] = high
    low_ref[where] = (value - high.astype(jnp.float32)).astype(jnp.bfloat16)


def frequency_weights(psd_ref, wts_ref, samples):
    length = samples // RADIX
    half = length // 2
    power = jnp.concatenate([psd_ref[:, half * i : half * (i + 1)] for i in range(RADIX)], axis=0)
    spread = (iota((RADIX, half), 0) == iota((RADIX, half), 1) // (half // RADIX)).astype(jnp.bfloat16)
    keep = iota((half, half), 0) // RADIX == iota((half, half), 1) % (half // RADIX)
    pick_up = (iota((RADIX, half), 1) % RADIX == iota((RADIX, half), 0)).astype(jnp.bfloat16)
    pick_down = (iota((RADIX, half), 1) % RADIX == (RADIX - iota((RADIX, half), 0)) % RADIX).astype(
        jnp.bfloat16
    )
    flip = (iota((half, half), 0) + iota((half, half), 1) == half - 1).astype(jnp.bfloat16)
    up = jnp.zeros((RADIX, half), jnp.float32)
    down = jnp.zeros((RADIX, half), jnp.float32)
    for digits, unit in ((power // 256, 256.0), (power % 256, 1.0)):
        digits = digits.astype(jnp.float32).astype(jnp.bfloat16)
        moved = lax.dot_general(
            digits, spread, (((0,), (0,)), ((), ())), preferred_element_type=jnp.float32
        )
        moved = jnp.where(keep, moved, 0.0).astype(jnp.bfloat16)
        up = up + unit * jnp.dot(pick_up, moved, preferred_element_type=jnp.float32)
        back = jnp.dot(pick_down, moved, preferred_element_type=jnp.float32).astype(jnp.bfloat16)
        down = down + unit * jnp.dot(back, flip, preferred_element_type=jnp.float32)
    up = 2.0 * (8192.0 / up)
    down = 2.0 * (8192.0 / down)
    last = 8192.0 / psd_ref[:, samples // 2 : samples // 2 + 1].astype(jnp.float32)
    first = iota((1, half), 1) == 0
    wts_ref[0:1, 0:half] = jnp.where(first, 0.5 * up[0:1], up[0:1])
    wts_ref[0:1, half:length] = jnp.where(first, last, up[0:1])
    wts_ref[1:2, 0:half] = up[RADIX // 2 : RADIX // 2 + 1]
    wts_ref[1:2, half:length] = up[RADIX // 2 : RADIX // 2 + 1]
    for slot, cls in enumerate(CLASSES):
        for at in (0, length):
            wts_ref[slot + 2 : slot + 3, at : at + half] = up[cls : cls + 1]
            wts_ref[slot + 2 : slot + 3, at + half : at + length] = down[cls : cls + 1]


def butterflies(d):
    r = math.sqrt(0.5)
    even, odd_r, odd_i, alt = [], [], [], []
    for q in range(4):
        s02, m02 = d[q] + d[q + 8], d[q] - d[q + 8]
        s13, m13 = d[q + 4] + d[q + 12], d[q + 4] - d[q + 12]
        even.append(s02 + s13)
        alt.append(s02 - s13)
        odd_r.append(m02)
        odd_i.append(-m13)
    e02, e13 = even[0] + even[2], even[1] + even[3]
    zero, eight = e02 + e13, e02 - e13
    four = (even[0] - even[2], even[3] - even[1])
    p, q = r * (alt[1] - alt[3]), r * (alt[1] + alt[3])
    two = (alt[0] + p, -(alt[2] + q))
    six = (alt[0] - p, alt[2] - q)
    br, bi = [odd_r[0]], [odd_i[0]]
    for q in (1, 2, 3):
        c, s = math.cos(math.pi * q / 8), math.sin(math.pi * q / 8)
        if q == 2:
            br.append(r * (odd_r[q] + odd_i[q]))
            bi.append(r * (odd_i[q] - odd_r[q]))
        else:
            br.append(c * odd_r[q] + s * odd_i[q])
            bi.append(c * odd_i[q] - s * odd_r[q])
    sr, si = br[0] + br[2], bi[0] + bi[2]
    tr, ti = br[1] + br[3], bi[1] + bi[3]
    ur, ui = br[0] - br[2], bi[0] - bi[2]
    vr, vi = br[1] - br[3], bi[1] - bi[3]
    one, nine = (sr + tr, si + ti), (sr - tr, si - ti)
    five, thirteen = (ur + vi, ui - vr), (ur - vi, ui + vr)
    return zero, eight, (one, two, thirteen, four, five, six, nine)


def kernel(
    devices_tm,
    angles_ref,
    mask_ref,
    columns_ref,
    coeffs_ref,
    psd_ref,
    own_ref,
    other_ref,
    orbit,
    far_coeffs,
    far_columns,
    coeffs_t,
    column_t,
    basis_a,
    basis_b,
    design,
    real_hi,
    real_lo,
    pair_hi,
    pair_lo,
    mat_real_hi,
    mat_real_lo,
    mat_hi,
    mat_lo,
    twiddle,
    wts,
    total,
    send_sem,
    recv_sem,
    side_send,
    side_recv,
):
    block = angles_ref.shape[1]
    samples = block * devices_tm
    length = samples // RADIX
    half = length // 2
    terms = coeffs_ref.shape[1]
    terms_lat = terms // 2
    columns = coeffs_ref.shape[2]
    rows = own_ref.shape[0]
    everyone = rows + columns
    me = lax.axis_index("tm")
    panel = lax.axis_index("panel")
    comp = lax.axis_index("comp")

    barrier = pltpu.get_barrier_semaphore()
    peers = [lax.rem(me + k, devices_tm) for k in range(1, devices_tm)]
    for peer in peers:
        pl.semaphore_signal(barrier, inc=1, device_id={"tm": peer}, device_id_type=MESH)
    pl.semaphore_signal(barrier, inc=1, device_id={"panel": 1 - panel}, device_id_type=MESH)
    pl.semaphore_signal(barrier, inc=1, device_id={"comp": 1 - comp}, device_id_type=MESH)

    orbit[me, 0:2, :] = angles_ref[...] * (0.5 / math.pi)
    orbit[me, 2:3, :] = mask_ref[...].astype(jnp.float32)
    pl.semaphore_wait(barrier, devices_tm + 1)

    def send_orbit(k, slot, peer):
        return pltpu.make_async_remote_copy(
            src_ref=orbit.at[slot],
            dst_ref=orbit.at[slot],
            send_sem=send_sem.at[k],
            recv_sem=recv_sem.at[slot],
            device_id={"tm": peer},
            device_id_type=MESH,
        )

    for k, peer in enumerate(peers):
        send_orbit(k, me, peer).start()
    first_row = me * rows
    lanes = pl.ds(pl.multiple_of(lax.rem(first_row, columns), rows), rows)
    send_coeffs = pltpu.make_async_remote_copy(
        src_ref=coeffs_ref.at[0, :, lanes],
        dst_ref=far_coeffs,
        send_sem=side_send.at[0],
        recv_sem=side_recv.at[0],
        device_id={"panel": 1 - panel},
        device_id_type=MESH,
    )
    send_columns = pltpu.make_async_remote_copy(
        src_ref=columns_ref.at[:, lanes],
        dst_ref=far_columns,
        send_sem=side_send.at[1],
        recv_sem=side_recv.at[1],
        device_id={"panel": 1 - panel},
        device_id_type=MESH,
    )
    send_coeffs.start()
    send_columns.start()

    scale = 1.0 / samples
    index = iota((length, length), 0) * iota((length, length), 1) % length
    turns = index.astype(jnp.float32) * (1.0 / length)
    cosine, sine = cos_turns(turns) * scale, cos_turns(turns - 0.25) * scale
    put_split(mat_hi, mat_lo, (slice(0, length), slice(0, length)), cosine)
    put_split(mat_hi, mat_lo, (slice(0, length), slice(length, 2 * length)), -sine)
    put_split(mat_hi, mat_lo, (slice(length, 2 * length), slice(0, length)), sine)
    put_split(mat_hi, mat_lo, (slice(length, 2 * length), slice(length, 2 * length)), cosine)
    sign = (1 - 2 * (iota((length, half), 0) % 2)).astype(jnp.float32) * scale
    nyquist = jnp.where(iota((length, half), 1) == 0, sign, -sine[:, :half])
    put_split(mat_real_hi, mat_real_lo, (0, slice(None), slice(0, half)), cosine[:, :half])
    put_split(mat_real_hi, mat_real_lo, (0, slice(None), slice(half, length)), nyquist)
    index = iota((length, half), 0) * (RADIX // 2 + RADIX * iota((length, half), 1)) % samples
    turns = index.astype(jnp.float32) * (1.0 / samples)
    put_split(mat_real_hi, mat_real_lo, (1, slice(None), slice(0, half)), cos_turns(turns) * scale)
    put_split(
        mat_real_hi,
        mat_real_lo,
        (1, slice(None), slice(half, length)),
        cos_turns(turns - 0.25) * -scale,
    )
    for slot, cls in enumerate(CLASSES):
        turns = (cls * iota((1, length), 1) % samples).astype(jnp.float32) * (1.0 / samples)
        twiddle[2 * slot : 2 * slot + 1, :] = cos_turns(turns)
        twiddle[2 * slot + 1 : 2 * slot + 2, :] = cos_turns(turns - 0.25)
    frequency_weights(psd_ref, wts, samples)

    def place(at, coeffs, index_rows):
        width = coeffs.shape[1]
        level = iota((terms, width), 0) % terms_lat
        masked = jnp.where(level <= index_rows[0:1, :], coeffs, 0.0)
        coeffs_t[at : at + width, :] = jnp.transpose(masked).astype(jnp.bfloat16)
        orders = index_rows[1:2, :]
        shift = jnp.where(orders >= 0, 0.0, 0.25)
        norm = 1.0 / jnp.sqrt(index_rows[0:1, :].astype(jnp.float32) + 1.0)
        packed = jnp.concatenate(
            [jnp.abs(orders).astype(jnp.float32), shift, norm, jnp.zeros((5, width), jnp.float32)], axis=0
        )
        column_t[at : at + width, 0:8] = jnp.transpose(packed)

    place(0, coeffs_ref[0].astype(jnp.float32), columns_ref[...])
    send_coeffs.wait()
    send_columns.wait()
    mine = first_row // columns == panel
    near = coeffs_ref[0, :, lanes].astype(jnp.float32)
    place(
        columns,
        jnp.where(mine, near, far_coeffs[...].astype(jnp.float32)),
        jnp.where(mine, columns_ref[:, lanes], far_columns[...]),
    )
    for k, peer in enumerate(peers):
        send_orbit(k, me, peer).wait_send()
    for k, peer in enumerate(peers):
        send_orbit(k, peer, peer).wait_recv()

    per_device = block // length

    def epoch_rows(chunk):
        where = pl.ds(pl.multiple_of(lax.rem(chunk, per_device) * length, length), length)
        return orbit[chunk // per_device, :, where]

    def fill_basis(chunk, basis):
        part = epoch_rows(chunk)
        theta, keep = part[0:1], part[2:3]
        turns = iota((16, length), 0).astype(jnp.float32) * theta
        cosine, sine = cos_turns(turns) * keep, cos_turns(turns - 0.25) * keep
        step_c, step_s = cos_turns(16.0 * theta), cos_turns(16.0 * theta - 0.25)
        for at in range(0, terms_lat, 16):
            basis[at : at + 16, :] = cosine.astype(jnp.bfloat16)
            basis[terms_lat + at : terms_lat + at + 16, :] = sine.astype(jnp.bfloat16)
            cosine, sine = cosine * step_c - sine * step_s, sine * step_c + cosine * step_s

    def fill_design(chunk, basis):
        longit = epoch_rows(chunk)[1:2]
        for at in range(0, everyone, 128):
            latitude = jnp.dot(coeffs_t[at : at + 128, :], basis[...], preferred_element_type=jnp.float32)
            order = column_t[at : at + 128, 0:1]
            shift = column_t[at : at + 128, 1:2]
            norm = column_t[at : at + 128, 2:3]
            wave = cos_turns(order * longit - shift, SINE_LON)
            design[chunk, at : at + 128, :] = latitude * wave * norm

    fill_basis(0, basis_a)

    def two_chunks(i, carry):
        fill_basis(2 * i + 1, basis_b)
        fill_design(2 * i, basis_a)
        fill_basis(lax.rem(2 * i + 2, RADIX), basis_a)
        fill_design(2 * i + 1, basis_b)
        return carry

    lax.fori_loop(0, RADIX // 2, two_chunks, 0)

    def fold(i, carry):
        at = pl.ds(pl.multiple_of(i * 16, 16), 16)
        for lane in range(0, length, 128):
            where = slice(lane, lane + 128)
            zero, eight, pairs = butterflies([design[q, at, where] for q in range(RADIX)])
            put_split(real_hi, real_lo, (0, at, where), zero)
            put_split(real_hi, real_lo, (1, at, where), eight)
            for slot, (real, imag) in enumerate(pairs):
                c = twiddle[2 * slot : 2 * slot + 1, where]
                s = twiddle[2 * slot + 1 : 2 * slot + 2, where]
                put_split(pair_hi, pair_lo, (slot, at, where), real * c + imag * s)
                past = slice(length + lane, length + lane + 128)
                put_split(pair_hi, pair_lo, (slot, at, past), imag * c - real * s)
        return carry

    lax.fori_loop(0, everyone // 16, fold, 0)

    def gram(high, low, mat_high, mat_low, weight):
        spectra = (
            jnp.dot(high, mat_high, preferred_element_type=jnp.float32)
            + jnp.dot(low, mat_high, preferred_element_type=jnp.float32)
            + jnp.dot(high, mat_low, preferred_element_type=jnp.float32)
        ).astype(jnp.bfloat16)
        weighted = (spectra[:columns].astype(jnp.float32) * weight).astype(jnp.bfloat16)
        return lax.dot_general(
            spectra[columns:], weighted, (((1,), (1,)), ((), ())), preferred_element_type=jnp.float32
        )

    total[...] = gram(
        real_hi[0], real_lo[0], mat_real_hi[0], mat_real_lo[0], wts[0:1, 0:length]
    ) + gram(real_hi[1], real_lo[1], mat_real_hi[1], mat_real_lo[1], wts[1:2, 0:length])

    def one_class(slot, carry):
        total[...] += gram(
            pair_hi[slot], pair_lo[slot], mat_hi[...], mat_lo[...], wts[pl.ds(slot + 2, 1), :]
        )
        return carry

    lax.fori_loop(0, len(CLASSES), one_class, 0)
    swap = pltpu.make_async_remote_copy(
        src_ref=total,
        dst_ref=other_ref,
        send_sem=side_send.at[2],
        recv_sem=side_recv.at[2],
        device_id={"comp": 1 - comp},
        device_id_type=MESH,
    )
    swap.start()
    own_ref[...] = total[...]
    swap.wait()


def fused(orbit_angles, gap_mask, column_index, lat_coeffs, psd_table):
    devices_tm = lax.axis_size("tm")
    block = orbit_angles.shape[1]
    samples = devices_tm * block
    length = samples // RADIX
    terms, columns = lat_coeffs.shape[1:]
    rows = columns * lax.axis_size("panel") // devices_tm
    everyone = rows + columns
    f32, bf16 = jnp.float32, jnp.bfloat16
    vmem = pl.BlockSpec(memory_space=pltpu.VMEM)
    count = len(CLASSES)
    own, other = pl.pallas_call(
        functools.partial(kernel, devices_tm),
        out_shape=[jax.ShapeDtypeStruct((rows, columns), f32)] * 2,
        in_specs=[vmem] * 5,
        out_specs=[vmem] * 2,
        scratch_shapes=[
            pltpu.VMEM((devices_tm, 8, block), f32),
            pltpu.VMEM((terms, rows), bf16),
            pltpu.VMEM((2, rows), jnp.int32),
            pltpu.VMEM((everyone, terms), bf16),
            pltpu.VMEM((everyone, 128), f32),
            pltpu.VMEM((terms, length), bf16),
            pltpu.VMEM((terms, length), bf16),
            pltpu.VMEM((RADIX, everyone, length), f32),
            pltpu.VMEM((2, everyone, length), bf16),
            pltpu.VMEM((2, everyone, length), bf16),
            pltpu.VMEM((count, everyone, 2 * length), bf16),
            pltpu.VMEM((count, everyone, 2 * length), bf16),
            pltpu.VMEM((2, length, length), bf16),
            pltpu.VMEM((2, length, length), bf16),
            pltpu.VMEM((2 * length, 2 * length), bf16),
            pltpu.VMEM((2 * length, 2 * length), bf16),
            pltpu.VMEM((2 * count, length), f32),
            pltpu.VMEM((16, 2 * length), f32),
            pltpu.VMEM((rows, columns), f32),
            pltpu.SemaphoreType.DMA((devices_tm,)),
            pltpu.SemaphoreType.DMA((devices_tm,)),
            pltpu.SemaphoreType.DMA((3,)),
            pltpu.SemaphoreType.DMA((3,)),
        ],
        compiler_params=pltpu.CompilerParams(
            collective_id=0, has_side_effects=True, vmem_limit_bytes=48 * 1024 * 1024
        ),
    )(orbit_angles, gap_mask.reshape(1, block), column_index, lat_coeffs, psd_table)
    return own + other


def choose(orbit_angles, gap_mask, column_index, lat_coeffs, psd_table):
    devices_tm, panels = lax.axis_size("tm"), lax.axis_size("panel")
    samples = devices_tm * orbit_angles.shape[1]
    columns = lat_coeffs.shape[2]
    rows = columns * panels // devices_tm
    fits = (
        samples == 4096
        and orbit_angles.shape[1] % 256 == 0
        and panels == 2
        and lax.axis_size("comp") == 2
        and rows % 128 == 0
        and columns % rows == 0
        and lat_coeffs.shape[1] % 32 == 0
        and (rows + columns) * lat_coeffs.shape[1] <= 512 * 1024
    )
    step = fused if fits else body
    return step(orbit_angles, gap_mask, column_index, lat_coeffs, psd_table)


def solution(mesh):
    return jax.shard_map(
        choose,
        mesh=mesh,
        in_specs=(
            P(None, ("groups", "tm")),
            P(("groups", "tm")),
            P(None, "panel"),
            P("comp", None, "panel"),
            P("comp", None),
        ),
        out_specs=P(("groups", "tm"), "panel"),
        check_vma=False,
    )
```

```python
import functools
import math

import jax
import jax.numpy as jnp
from jax import lax
from jax.experimental import pallas as pl
from jax.experimental.pallas import tpu as pltpu
from jax.sharding import PartitionSpec as P

SPLIT = 64


def synthesize(angles, keep_rows, column_index, coeffs):
    terms_lat = coeffs.shape[0] // 2
    colatitude = angles[0]
    longit = angles[1]
    wavenumbers = jnp.arange(terms_lat, dtype=jnp.float32)
    phases = colatitude[:, None] * wavenumbers[None, :]
    basis_rows = jnp.concatenate([jnp.cos(phases), jnp.sin(phases)], axis=1).astype(jnp.bfloat16)
    degree = column_index[0]
    orders = column_index[1]
    levels = jnp.arange(2 * terms_lat, dtype=jnp.int32) % terms_lat
    allowed = levels[:, None] <= degree[None, :]
    masked = jnp.where(allowed, coeffs, jnp.zeros_like(coeffs))
    latitude = jnp.dot(basis_rows, masked, preferred_element_type=jnp.float32)
    lon_phase = longit[:, None] * jnp.abs(orders).astype(jnp.float32)[None, :]
    lon_wave = jnp.where(orders[None, :] >= 0, jnp.cos(lon_phase), jnp.sin(lon_phase))
    norm_scale = 1.0 / jnp.sqrt(degree.astype(jnp.float32) + 1.0)
    return latitude * lon_wave * (keep_rows[:, None] * norm_scale[None, :])


def phase_tables(row_index, col_index, length):
    product = row_index[:, None] * col_index[None, :] % length
    angle_grid = product.astype(jnp.float32) * (2.0 * math.pi / length)
    return (jnp.cos(angle_grid), jnp.sin(angle_grid))


def dft_tables(length):
    indices = jnp.arange(length, dtype=jnp.int32)
    return phase_tables(indices, indices, length)


def rotate(real_part, imag_part, outer_index, inner_index, length):
    index_grid = outer_index[:, None] * inner_index[None, :] % length
    angle_grid = index_grid.astype(jnp.float32) * (2.0 * math.pi / length)
    cosine = jnp.cos(angle_grid)[:, :, None]
    sine_grid = jnp.sin(angle_grid)[:, :, None]
    return (real_part * cosine + imag_part * sine_grid, imag_part * cosine - real_part * sine_grid)


def precise_dot(left_side, right_side):
    return jnp.dot(
        left_side, right_side, precision=lax.Precision.HIGHEST, preferred_element_type=jnp.float32
    )


def transform(cos_table, sin_table, real_part, imag_part):
    new_real = precise_dot(cos_table, real_part) + precise_dot(sin_table, imag_part)
    new_imag = precise_dot(cos_table, imag_part) - precise_dot(sin_table, real_part)
    return (new_real, new_imag)


def four_step(real_in, imag_in, samples):
    length = real_in.shape[0]
    columns = real_in.shape[1]
    outer_count = SPLIT
    inner_count = length // SPLIT
    real_part = real_in.reshape(outer_count, inner_count * columns)
    imag_part = imag_in.reshape(outer_count, inner_count * columns)
    cos_outer, sin_outer = dft_tables(outer_count)
    real_part, imag_part = transform(cos_outer, sin_outer, real_part, imag_part)
    real_part = real_part.reshape(outer_count, inner_count, columns)
    imag_part = imag_part.reshape(outer_count, inner_count, columns)
    real_part, imag_part = rotate(
        real_part,
        imag_part,
        jnp.arange(outer_count, dtype=jnp.int32),
        jnp.arange(inner_count, dtype=jnp.int32),
        length,
    )
    real_part = jnp.transpose(real_part, (1, 0, 2)).reshape(inner_count, outer_count * columns)
    imag_part = jnp.transpose(imag_part, (1, 0, 2)).reshape(inner_count, outer_count * columns)
    cos_inner, sin_inner = dft_tables(inner_count)
    real_part, imag_part = transform(cos_inner, sin_inner, real_part, imag_part)
    return (
        real_part.reshape(length, columns) / samples,
        imag_part.reshape(length, columns) / samples,
    )


def local_transform(received, samples):
    real_part, imag_part = four_step(received[0, 0], received[1, 0], samples)
    return (real_part.astype(jnp.bfloat16), imag_part.astype(jnp.bfloat16))


def noise_weighted(spectra, psd_row, frequency, samples):
    folded = jnp.minimum(frequency, samples - frequency)
    inverse_psd = 8192.0 / jnp.take(psd_row, folded).astype(jnp.float32)
    return (spectra.astype(jnp.float32) * inverse_psd[None, :, None]).astype(jnp.bfloat16)


def settle(partial_value, sum_dim):
    summed = lax.psum_scatter(partial_value, "tm", scatter_dimension=sum_dim, tiled=True)
    return lax.psum(summed, "comp")


def body(orbit_angles, gap_mask, column_index, lat_coeffs, psd_table):
    devices_tm = lax.axis_size("tm")
    epochs = orbit_angles.shape[1]
    block_len = epochs // devices_tm
    samples = epochs * devices_tm
    columns = lat_coeffs.shape[2]
    coeffs = lat_coeffs[0]
    keep_rows = gap_mask.astype(jnp.float32)
    packed = jnp.concatenate([orbit_angles, keep_rows[None]], axis=0)[:, None, :]
    received = lax.all_to_all(packed, "tm", split_axis=2, concat_axis=1, tiled=True)
    flat_orbit = received.reshape(3, devices_tm * block_len)
    spread = synthesize(flat_orbit[0:2], flat_orbit[2], column_index, coeffs).reshape(
        devices_tm, block_len, columns
    )
    position = lax.axis_index("tm")
    local_epoch = position * block_len + jnp.arange(block_len, dtype=jnp.int32)
    cos_outer, sin_outer = dft_tables(devices_tm)
    flat_design = spread.reshape(devices_tm, block_len * columns)
    real_part = precise_dot(cos_outer, flat_design).reshape(devices_tm, block_len, columns)
    imag_part = -precise_dot(sin_outer, flat_design).reshape(devices_tm, block_len, columns)
    real_part, imag_part = rotate(
        real_part, imag_part, jnp.arange(devices_tm, dtype=jnp.int32), local_epoch, samples
    )
    twisted = jnp.stack([real_part, imag_part])
    spec_real, spec_imag = local_transform(
        lax.all_to_all(twisted, "tm", split_axis=1, concat_axis=2, tiled=True), samples
    )
    spectra = jnp.stack([spec_real, spec_imag])
    psd_row = psd_table[0]
    contract = (((0, 1), (0, 1)), ((), ()))
    frequency = position + devices_tm * jnp.arange(epochs, dtype=jnp.int32)
    weighted = noise_weighted(spectra, psd_row, frequency, samples)
    partial_value = lax.dot_general(
        lax.all_gather(spectra, "panel", axis=2, tiled=True),
        weighted,
        contract,
        preferred_element_type=jnp.float32,
    )
    return settle(partial_value, 0)


RADIX = 16
SINE_LON = (6.283164044168851, -41.33714234995496, 81.34076808172247, -70.99342472149007)
SINE_FINE = (
    6.283185160088548,
    -41.3416550311802,
    81.60100405747373,
    -76.54978191007581,
    39.53670300634923,
)
CLASSES = (1, 2, 13, 4, 5, 6, 9)
MESH = pl.DeviceIdType.MESH


def cos_turns(turns, terms=SINE_FINE):
    offset = turns - jnp.round(turns)
    near = 0.25 - jnp.abs(offset)
    square = near * near
    total = terms[-1]
    for term in terms[-2::-1]:
        total = total * square + term
    return total * near


def iota(shape, dim):
    return lax.broadcasted_iota(jnp.int32, shape, dim)


def split(value):
    high = value.astype(jnp.bfloat16)
    return high, (value - high.astype(jnp.float32)).astype(jnp.bfloat16)


def put_matrix(ref, slot, at, value, lanes):
    high, low = split(value)
    third = ref.shape[1] // 3
    for block, part in ((0, high), (1, high), (2, low)):
        start = block * third + at
        ref[slot, start : start + value.shape[0], lanes] = part


def put_rows(ref, slot, rows, at, value):
    high, low = split(value)
    past = ref.shape[2] // 2 + at
    ref[slot, rows, at : at + value.shape[1]] = high
    ref[slot, rows, past : past + value.shape[1]] = low


def frequency_weights(psd_ref, wts_ref, samples):
    length = samples // RADIX
    half = length // 2
    power = jnp.concatenate([psd_ref[:, half * i : half * (i + 1)] for i in range(RADIX)], axis=0)
    spread = (iota((RADIX, half), 0) == iota((RADIX, half), 1) >> 3).astype(jnp.bfloat16)
    keep = (iota((half, half), 0) >> 4) == (iota((half, half), 1) & (half // RADIX - 1))
    pick_up = ((iota((RADIX, half), 1) & (RADIX - 1)) == iota((RADIX, half), 0)).astype(jnp.bfloat16)
    pick_down = ((iota((RADIX, half), 1) + iota((RADIX, half), 0)) & (RADIX - 1) == 0).astype(
        jnp.bfloat16
    )
    flip = (iota((half, half), 0) + iota((half, half), 1) == half - 1).astype(jnp.bfloat16)
    up = jnp.zeros((RADIX, half), jnp.float32)
    down = jnp.zeros((RADIX, half), jnp.float32)
    for digits, unit in ((power >> 8, 256.0), (power & 255, 1.0)):
        digits = digits.astype(jnp.float32).astype(jnp.bfloat16)
        moved = lax.dot_general(
            digits, spread, (((0,), (0,)), ((), ())), preferred_element_type=jnp.float32
        )
        moved = jnp.where(keep, moved, 0.0).astype(jnp.bfloat16)
        up = up + unit * jnp.dot(pick_up, moved, preferred_element_type=jnp.float32)
        back = jnp.dot(pick_down, moved, preferred_element_type=jnp.float32).astype(jnp.bfloat16)
        down = down + unit * jnp.dot(back, flip, preferred_element_type=jnp.float32)
    up = 2.0 * (8192.0 / up)
    down = 2.0 * (8192.0 / down)
    last = 8192.0 / psd_ref[:, samples // 2 : samples // 2 + 1].astype(jnp.float32)
    first = iota((1, half), 1) == 0
    wts_ref[0:1, 0:half] = jnp.where(first, 0.5 * up[0:1], up[0:1])
    wts_ref[0:1, half:length] = jnp.where(first, last, up[0:1])
    wts_ref[1:2, 0:half] = up[RADIX // 2 : RADIX // 2 + 1]
    wts_ref[1:2, half:length] = up[RADIX // 2 : RADIX // 2 + 1]
    for slot, cls in enumerate(CLASSES):
        for at in (0, length):
            wts_ref[slot + 2 : slot + 3, at : at + half] = up[cls : cls + 1]
            wts_ref[slot + 2 : slot + 3, at + half : at + length] = down[cls : cls + 1]


def butterflies(d):
    r = math.sqrt(0.5)
    even, odd_r, odd_i, alt = [], [], [], []
    for q in range(4):
        s02, m02 = d[q] + d[q + 8], d[q] - d[q + 8]
        s13, m13 = d[q + 4] + d[q + 12], d[q + 4] - d[q + 12]
        even.append(s02 + s13)
        alt.append(s02 - s13)
        odd_r.append(m02)
        odd_i.append(-m13)
    e02, e13 = even[0] + even[2], even[1] + even[3]
    zero, eight = e02 + e13, e02 - e13
    four = (even[0] - even[2], even[3] - even[1])
    p, q = r * (alt[1] - alt[3]), r * (alt[1] + alt[3])
    two = (alt[0] + p, -(alt[2] + q))
    six = (alt[0] - p, alt[2] - q)
    br, bi = [odd_r[0]], [odd_i[0]]
    for q in (1, 2, 3):
        c, s = math.cos(math.pi * q / 8), math.sin(math.pi * q / 8)
        if q == 2:
            br.append(r * (odd_r[q] + odd_i[q]))
            bi.append(r * (odd_i[q] - odd_r[q]))
        else:
            br.append(c * odd_r[q] + s * odd_i[q])
            bi.append(c * odd_i[q] - s * odd_r[q])
    sr, si = br[0] + br[2], bi[0] + bi[2]
    tr, ti = br[1] + br[3], bi[1] + bi[3]
    ur, ui = br[0] - br[2], bi[0] - bi[2]
    vr, vi = br[1] - br[3], bi[1] - bi[3]
    one, nine = (sr + tr, si + ti), (sr - tr, si - ti)
    five, thirteen = (ur + vi, ui - vr), (ur - vi, ui + vr)
    return zero, eight, (one, two, thirteen, four, five, six, nine)


def kernel(
    devices_tm,
    angles_hbm,
    mask_hbm,
    columns_hbm,
    coeffs_hbm,
    psd_hbm,
    own_ref,
    other_ref,
    angles_ref,
    mask_ref,
    columns_ref,
    coeffs_ref,
    psd_ref,
    orbit,
    far_coeffs,
    far_columns,
    coeffs_t,
    column_t,
    basis_a,
    basis_b,
    design,
    real,
    pair,
    mat_real,
    mat,
    twiddle,
    wts,
    total,
    send_sem,
    recv_sem,
    side_send,
    side_recv,
    load_sem,
):
    block = angles_ref.shape[1]
    samples = block * devices_tm
    length = samples // RADIX
    half = length // 2
    terms = coeffs_ref.shape[1]
    terms_lat = terms // 2
    columns = coeffs_ref.shape[2]
    rows = own_ref.shape[0]
    everyone = rows + columns
    me = lax.axis_index("tm")
    panel = lax.axis_index("panel")
    comp = lax.axis_index("comp")

    loads = [
        pltpu.make_async_copy(source, held, load_sem.at[i])
        for i, (source, held) in enumerate(
            (
                (angles_hbm, angles_ref),
                (mask_hbm, mask_ref),
                (columns_hbm, columns_ref),
                (coeffs_hbm, coeffs_ref),
                (psd_hbm, psd_ref),
            )
        )
    ]
    for load in loads:
        load.start()
    barrier = pltpu.get_barrier_semaphore()
    peers = [lax.rem(me + k, devices_tm) for k in range(1, devices_tm)]
    for peer in peers:
        pl.semaphore_signal(barrier, inc=1, device_id={"tm": peer}, device_id_type=MESH)
    pl.semaphore_signal(barrier, inc=1, device_id={"panel": 1 - panel}, device_id_type=MESH)
    pl.semaphore_signal(barrier, inc=1, device_id={"comp": 1 - comp}, device_id_type=MESH)

    loads[0].wait()
    loads[1].wait()
    orbit[me, 0:2, :] = angles_ref[...] * (0.5 / math.pi)
    orbit[me, 2:3, :] = mask_ref[...].astype(jnp.float32)
    pl.semaphore_wait(barrier, devices_tm + 1)

    def send_orbit(k, slot, peer):
        return pltpu.make_async_remote_copy(
            src_ref=orbit.at[slot],
            dst_ref=orbit.at[slot],
            send_sem=send_sem.at[k],
            recv_sem=recv_sem.at[slot],
            device_id={"tm": peer},
            device_id_type=MESH,
        )

    for k, peer in enumerate(peers):
        send_orbit(k, me, peer).start()
    first_row = me * rows
    lanes = pl.ds(pl.multiple_of(lax.rem(first_row, columns), rows), rows)
    send_coeffs = pltpu.make_async_remote_copy(
        src_ref=coeffs_hbm.at[0, :, lanes],
        dst_ref=far_coeffs,
        send_sem=side_send.at[0],
        recv_sem=side_recv.at[0],
        device_id={"panel": 1 - panel},
        device_id_type=MESH,
    )
    send_columns = pltpu.make_async_remote_copy(
        src_ref=columns_hbm.at[:, lanes],
        dst_ref=far_columns,
        send_sem=side_send.at[1],
        recv_sem=side_recv.at[1],
        device_id={"panel": 1 - panel},
        device_id_type=MESH,
    )
    send_coeffs.start()
    send_columns.start()

    scale = 1.0 / samples
    index = iota((length, length), 0) * iota((length, length), 1) & (length - 1)
    turns = index.astype(jnp.float32) * (1.0 / length)
    cosine, sine = cos_turns(turns) * scale, cos_turns(turns - 0.25) * scale
    left, right = slice(0, length), slice(length, 2 * length)
    put_matrix(mat, 0, 0, cosine, left)
    put_matrix(mat, 0, 0, -sine, right)
    put_matrix(mat, 0, length, sine, left)
    put_matrix(mat, 0, length, cosine, right)
    left, right = slice(0, half), slice(half, length)
    sign = (1 - 2 * ((iota((length, half), 0) & 1))).astype(jnp.float32) * scale
    nyquist = jnp.where(iota((length, half), 1) == 0, sign, -sine[:, :half])
    put_matrix(mat_real, 0, 0, cosine[:, :half], left)
    put_matrix(mat_real, 0, 0, nyquist, right)
    index = iota((length, half), 0) * (RADIX // 2 + RADIX * iota((length, half), 1)) & (samples - 1)
    turns = index.astype(jnp.float32) * (1.0 / samples)
    put_matrix(mat_real, 1, 0, cos_turns(turns) * scale, left)
    put_matrix(mat_real, 1, 0, cos_turns(turns - 0.25) * -scale, right)
    for slot, cls in enumerate(CLASSES):
        turns = (cls * iota((1, length), 1) & (samples - 1)).astype(jnp.float32) * (1.0 / samples)
        twiddle[2 * slot : 2 * slot + 1, :] = cos_turns(turns)
        twiddle[2 * slot + 1 : 2 * slot + 2, :] = cos_turns(turns - 0.25)
    loads[4].wait()
    frequency_weights(psd_ref, wts, samples)

    def place(at, coeffs, index_rows):
        width = coeffs.shape[1]
        level = iota((terms, width), 0)
        level = jnp.where(level < terms_lat, level, level - terms_lat)
        masked = jnp.where(level <= index_rows[0:1, :], coeffs, 0.0)
        coeffs_t[at : at + width, :] = jnp.transpose(masked).astype(jnp.bfloat16)
        orders = index_rows[1:2, :]
        shift = jnp.where(orders >= 0, 0.0, 0.25)
        norm = 1.0 / jnp.sqrt(index_rows[0:1, :].astype(jnp.float32) + 1.0)
        packed = jnp.concatenate(
            [jnp.abs(orders).astype(jnp.float32), shift]
            + [norm * term for term in SINE_LON]
            + [jnp.zeros((2, width), jnp.float32)],
            axis=0,
        )
        turned = jnp.transpose(packed)
        for i in range(2 + len(SINE_LON)):
            column_t[i, at : at + width, :] = jnp.broadcast_to(turned[:, i : i + 1], (width, 128))

    loads[2].wait()
    loads[3].wait()
    place(0, coeffs_ref[0].astype(jnp.float32), columns_ref[...])
    send_coeffs.wait()
    send_columns.wait()
    mine = first_row // columns == panel
    near = coeffs_ref[0, :, lanes].astype(jnp.float32)
    place(
        columns,
        jnp.where(mine, near, far_coeffs[...].astype(jnp.float32)),
        jnp.where(mine, columns_ref[:, lanes], far_columns[...]),
    )
    for k, peer in enumerate(peers):
        send_orbit(k, me, peer).wait_send()
    for k, peer in enumerate(peers):
        send_orbit(k, peer, peer).wait_recv()

    per_device = block // length

    def epoch_rows(chunk):
        where = pl.ds(pl.multiple_of(lax.rem(chunk, per_device) * length, length), length)
        return orbit[chunk // per_device, :, where]

    def fill_basis(chunk, basis):
        part = epoch_rows(chunk)
        theta, keep = part[0:1], part[2:3]
        turns = iota((16, length), 0).astype(jnp.float32) * theta
        cosine, sine = cos_turns(turns) * keep, cos_turns(turns - 0.25) * keep
        step_c, step_s = cos_turns(16.0 * theta), cos_turns(16.0 * theta - 0.25)
        for at in range(0, terms_lat, 16):
            basis[at : at + 16, :] = cosine.astype(jnp.bfloat16)
            basis[terms_lat + at : terms_lat + at + 16, :] = sine.astype(jnp.bfloat16)
            cosine, sine = cosine * step_c - sine * step_s, sine * step_c + cosine * step_s

    def fill_design(chunk, basis):
        longit = epoch_rows(chunk)[1:2]
        latitude = jnp.dot(coeffs_t[...], basis[...], preferred_element_type=jnp.float32)
        terms_lon = [column_t[2 + i] for i in range(len(SINE_LON))]
        for lane in range(0, length, 128):
            lanes = slice(lane, lane + 128)
            wave = cos_turns(column_t[0] * longit[:, lanes] - column_t[1], terms_lon)
            design[chunk, :, lanes] = latitude[:, lanes] * wave

    fill_basis(0, basis_a)

    def two_chunks(i, carry):
        fill_basis(2 * i + 1, basis_b)
        fill_design(2 * i, basis_a)
        fill_basis(lax.rem(2 * i + 2, RADIX), basis_a)
        fill_design(2 * i + 1, basis_b)
        return carry

    lax.fori_loop(0, RADIX // 2, two_chunks, 0)

    def fold(i, carry):
        at = pl.ds(pl.multiple_of(i * 16, 16), 16)
        for lane in range(0, length, 128):
            where = slice(lane, lane + 128)
            zero, eight, pairs = butterflies([design[q, at, where] for q in range(RADIX)])
            put_rows(real, 0, at, lane, zero)
            put_rows(real, 1, at, lane, eight)
            for slot, (re, im) in enumerate(pairs):
                c = twiddle[2 * slot : 2 * slot + 1, where]
                s = twiddle[2 * slot + 1 : 2 * slot + 2, where]
                put_rows(pair, slot, at, lane, re * c + im * s)
                put_rows(pair, slot, at, length + lane, im * c - re * s)
        return carry

    lax.fori_loop(0, everyone // 16, fold, 0)

    def gram(parts, matrix, weight):
        high = parts[:, : parts.shape[1] // 2]
        spectra = jnp.dot(
            jnp.concatenate([parts, high], axis=1), matrix, preferred_element_type=jnp.float32
        ).astype(jnp.bfloat16)
        weighted = (spectra[:columns].astype(jnp.float32) * weight).astype(jnp.bfloat16)
        return lax.dot_general(
            spectra[columns:], weighted, (((1,), (1,)), ((), ())), preferred_element_type=jnp.float32
        )

    total[...] = gram(real[0], mat_real[0], wts[0:1, 0:length]) + gram(
        real[1], mat_real[1], wts[1:2, 0:length]
    )

    def one_class(slot, carry):
        total[...] += gram(pair[slot], mat[0], wts[pl.ds(slot + 2, 1), :])
        return carry

    lax.fori_loop(0, len(CLASSES), one_class, 0)
    swap = pltpu.make_async_remote_copy(
        src_ref=total,
        dst_ref=other_ref,
        send_sem=side_send.at[2],
        recv_sem=side_recv.at[2],
        device_id={"comp": 1 - comp},
        device_id_type=MESH,
    )
    swap.start()
    own_ref[...] = total[...]
    swap.wait()


def fused(orbit_angles, gap_mask, column_index, lat_coeffs, psd_table):
    devices_tm = lax.axis_size("tm")
    block = orbit_angles.shape[1]
    samples = devices_tm * block
    length = samples // RADIX
    terms, columns = lat_coeffs.shape[1:]
    rows = columns * lax.axis_size("panel") // devices_tm
    everyone = rows + columns
    f32, bf16 = jnp.float32, jnp.bfloat16
    vmem = pl.BlockSpec(memory_space=pltpu.VMEM)
    count = len(CLASSES)
    own, other = pl.pallas_call(
        functools.partial(kernel, devices_tm),
        out_shape=[jax.ShapeDtypeStruct((rows, columns), f32)] * 2,
        in_specs=[pl.BlockSpec(memory_space=pltpu.HBM)] * 5,
        out_specs=[vmem] * 2,
        scratch_shapes=[
            pltpu.VMEM(orbit_angles.shape, f32),
            pltpu.VMEM((1, block), jnp.int32),
            pltpu.VMEM(column_index.shape, jnp.int32),
            pltpu.VMEM(lat_coeffs.shape, bf16),
            pltpu.VMEM(psd_table.shape, jnp.int32),
            pltpu.VMEM((devices_tm, 8, block), f32),
            pltpu.VMEM((terms, rows), bf16),
            pltpu.VMEM((2, rows), jnp.int32),
            pltpu.VMEM((everyone, terms), bf16),
            pltpu.VMEM((2 + len(SINE_LON), everyone, 128), f32),
            pltpu.VMEM((terms, length), bf16),
            pltpu.VMEM((terms, length), bf16),
            pltpu.VMEM((RADIX, everyone, length), f32),
            pltpu.VMEM((2, everyone, 2 * length), bf16),
            pltpu.VMEM((count, everyone, 4 * length), bf16),
            pltpu.VMEM((2, 3 * length, length), bf16),
            pltpu.VMEM((1, 6 * length, 2 * length), bf16),
            pltpu.VMEM((2 * count, length), f32),
            pltpu.VMEM((16, 2 * length), f32),
            pltpu.VMEM((rows, columns), f32),
            pltpu.SemaphoreType.DMA((devices_tm,)),
            pltpu.SemaphoreType.DMA((devices_tm,)),
            pltpu.SemaphoreType.DMA((3,)),
            pltpu.SemaphoreType.DMA((3,)),
            pltpu.SemaphoreType.DMA((5,)),
        ],
        compiler_params=pltpu.CompilerParams(
            collective_id=0, has_side_effects=True, vmem_limit_bytes=63 * 1024 * 1024
        ),
    )(orbit_angles, gap_mask.reshape(1, block), column_index, lat_coeffs, psd_table)
    return own + other


def choose(orbit_angles, gap_mask, column_index, lat_coeffs, psd_table):
    devices_tm, panels = lax.axis_size("tm"), lax.axis_size("panel")
    samples = devices_tm * orbit_angles.shape[1]
    columns = lat_coeffs.shape[2]
    rows = columns * panels // devices_tm
    fits = (
        samples == 4096
        and orbit_angles.shape[1] % 256 == 0
        and panels == 2
        and lax.axis_size("comp") == 2
        and rows % 128 == 0
        and columns % rows == 0
        and lat_coeffs.shape[1] % 32 == 0
        and (rows + columns) * lat_coeffs.shape[1] <= 512 * 1024
    )
    step = fused if fits else body
    return step(orbit_angles, gap_mask, column_index, lat_coeffs, psd_table)


def solution(mesh):
    return jax.shard_map(
        choose,
        mesh=mesh,
        in_specs=(
            P(None, ("groups", "tm")),
            P(("groups", "tm")),
            P(None, "panel"),
            P("comp", None, "panel"),
            P("comp", None),
        ),
        out_specs=P(("groups", "tm"), "panel"),
        check_vma=False,
    )
```

```python
import functools
import math

import jax
import jax.numpy as jnp
import numpy as np
from jax import lax
from jax.experimental import pallas as pl
from jax.experimental.pallas import tpu as pltpu
from jax.sharding import PartitionSpec as P

SPLIT = 64


def synthesize(angles, keep_rows, column_index, coeffs):
    terms_lat = coeffs.shape[0] // 2
    colatitude = angles[0]
    longit = angles[1]
    wavenumbers = jnp.arange(terms_lat, dtype=jnp.float32)
    phases = colatitude[:, None] * wavenumbers[None, :]
    basis_rows = jnp.concatenate([jnp.cos(phases), jnp.sin(phases)], axis=1).astype(jnp.bfloat16)
    degree = column_index[0]
    orders = column_index[1]
    levels = jnp.arange(2 * terms_lat, dtype=jnp.int32) % terms_lat
    allowed = levels[:, None] <= degree[None, :]
    masked = jnp.where(allowed, coeffs, jnp.zeros_like(coeffs))
    latitude = jnp.dot(basis_rows, masked, preferred_element_type=jnp.float32)
    lon_phase = longit[:, None] * jnp.abs(orders).astype(jnp.float32)[None, :]
    lon_wave = jnp.where(orders[None, :] >= 0, jnp.cos(lon_phase), jnp.sin(lon_phase))
    norm_scale = 1.0 / jnp.sqrt(degree.astype(jnp.float32) + 1.0)
    return latitude * lon_wave * (keep_rows[:, None] * norm_scale[None, :])


def phase_tables(row_index, col_index, length):
    product = row_index[:, None] * col_index[None, :] % length
    angle_grid = product.astype(jnp.float32) * (2.0 * math.pi / length)
    return (jnp.cos(angle_grid), jnp.sin(angle_grid))


def dft_tables(length):
    indices = jnp.arange(length, dtype=jnp.int32)
    return phase_tables(indices, indices, length)


def rotate(real_part, imag_part, outer_index, inner_index, length):
    index_grid = outer_index[:, None] * inner_index[None, :] % length
    angle_grid = index_grid.astype(jnp.float32) * (2.0 * math.pi / length)
    cosine = jnp.cos(angle_grid)[:, :, None]
    sine_grid = jnp.sin(angle_grid)[:, :, None]
    return (real_part * cosine + imag_part * sine_grid, imag_part * cosine - real_part * sine_grid)


def precise_dot(left_side, right_side):
    return jnp.dot(
        left_side, right_side, precision=lax.Precision.HIGHEST, preferred_element_type=jnp.float32
    )


def transform(cos_table, sin_table, real_part, imag_part):
    new_real = precise_dot(cos_table, real_part) + precise_dot(sin_table, imag_part)
    new_imag = precise_dot(cos_table, imag_part) - precise_dot(sin_table, real_part)
    return (new_real, new_imag)


def four_step(real_in, imag_in, samples):
    length = real_in.shape[0]
    columns = real_in.shape[1]
    outer_count = SPLIT
    inner_count = length // SPLIT
    real_part = real_in.reshape(outer_count, inner_count * columns)
    imag_part = imag_in.reshape(outer_count, inner_count * columns)
    cos_outer, sin_outer = dft_tables(outer_count)
    real_part, imag_part = transform(cos_outer, sin_outer, real_part, imag_part)
    real_part = real_part.reshape(outer_count, inner_count, columns)
    imag_part = imag_part.reshape(outer_count, inner_count, columns)
    real_part, imag_part = rotate(
        real_part,
        imag_part,
        jnp.arange(outer_count, dtype=jnp.int32),
        jnp.arange(inner_count, dtype=jnp.int32),
        length,
    )
    real_part = jnp.transpose(real_part, (1, 0, 2)).reshape(inner_count, outer_count * columns)
    imag_part = jnp.transpose(imag_part, (1, 0, 2)).reshape(inner_count, outer_count * columns)
    cos_inner, sin_inner = dft_tables(inner_count)
    real_part, imag_part = transform(cos_inner, sin_inner, real_part, imag_part)
    return (
        real_part.reshape(length, columns) / samples,
        imag_part.reshape(length, columns) / samples,
    )


def local_transform(received, samples):
    real_part, imag_part = four_step(received[0, 0], received[1, 0], samples)
    return (real_part.astype(jnp.bfloat16), imag_part.astype(jnp.bfloat16))


def noise_weighted(spectra, psd_row, frequency, samples):
    folded = jnp.minimum(frequency, samples - frequency)
    inverse_psd = 8192.0 / jnp.take(psd_row, folded).astype(jnp.float32)
    return (spectra.astype(jnp.float32) * inverse_psd[None, :, None]).astype(jnp.bfloat16)


def settle(partial_value, sum_dim):
    summed = lax.psum_scatter(partial_value, "tm", scatter_dimension=sum_dim, tiled=True)
    return lax.psum(summed, "comp")


def body(orbit_angles, gap_mask, column_index, lat_coeffs, psd_table):
    devices_tm = lax.axis_size("tm")
    epochs = orbit_angles.shape[1]
    block_len = epochs // devices_tm
    samples = epochs * devices_tm
    columns = lat_coeffs.shape[2]
    coeffs = lat_coeffs[0]
    keep_rows = gap_mask.astype(jnp.float32)
    packed = jnp.concatenate([orbit_angles, keep_rows[None]], axis=0)[:, None, :]
    received = lax.all_to_all(packed, "tm", split_axis=2, concat_axis=1, tiled=True)
    flat_orbit = received.reshape(3, devices_tm * block_len)
    spread = synthesize(flat_orbit[0:2], flat_orbit[2], column_index, coeffs).reshape(
        devices_tm, block_len, columns
    )
    position = lax.axis_index("tm")
    local_epoch = position * block_len + jnp.arange(block_len, dtype=jnp.int32)
    cos_outer, sin_outer = dft_tables(devices_tm)
    flat_design = spread.reshape(devices_tm, block_len * columns)
    real_part = precise_dot(cos_outer, flat_design).reshape(devices_tm, block_len, columns)
    imag_part = -precise_dot(sin_outer, flat_design).reshape(devices_tm, block_len, columns)
    real_part, imag_part = rotate(
        real_part, imag_part, jnp.arange(devices_tm, dtype=jnp.int32), local_epoch, samples
    )
    twisted = jnp.stack([real_part, imag_part])
    spec_real, spec_imag = local_transform(
        lax.all_to_all(twisted, "tm", split_axis=1, concat_axis=2, tiled=True), samples
    )
    spectra = jnp.stack([spec_real, spec_imag])
    psd_row = psd_table[0]
    contract = (((0, 1), (0, 1)), ((), ()))
    frequency = position + devices_tm * jnp.arange(epochs, dtype=jnp.int32)
    weighted = noise_weighted(spectra, psd_row, frequency, samples)
    partial_value = lax.dot_general(
        lax.all_gather(spectra, "panel", axis=2, tiled=True),
        weighted,
        contract,
        preferred_element_type=jnp.float32,
    )
    return settle(partial_value, 0)


RADIX = 16
SINE_LON = (6.283164044168851, -41.33714234995496, 81.34076808172247, -70.99342472149007)
SINE_FINE = (
    6.283185160088548,
    -41.3416550311802,
    81.60100405747373,
    -76.54978191007581,
    39.53670300634923,
)
CLASSES = (2, 4, 6, 1, 5, 9, 13)
EVEN = 3
MESH = pl.DeviceIdType.MESH


def cos_turns(turns, terms=SINE_FINE):
    offset = turns - jnp.round(turns)
    near = 0.25 - jnp.abs(offset)
    square = near * near
    total = terms[-1]
    for term in terms[-2::-1]:
        total = total * square + term
    return total * near


def iota(shape, dim):
    return lax.broadcasted_iota(jnp.int32, shape, dim)


def split(value):
    high = value.astype(jnp.bfloat16)
    return high, (value - high.astype(jnp.float32)).astype(jnp.bfloat16)


def tables(length):
    samples = RADIX * length
    half = length // 2

    def waves(product):
        angle = (product % samples) * (2.0 * np.pi / samples)
        return np.cos(angle), np.sin(angle)

    count = np.arange(length)
    cosine, sine = waves(RADIX * np.outer(count, count))
    zero = np.concatenate([cosine[:, :half], -sine[:, :half]], axis=1)
    zero[:, half] = 1 - 2 * (count % 2)
    eight = np.concatenate(waves(np.outer(count, RADIX // 2 + RADIX * count[:half])), axis=1)
    eight[:, half:] *= -1
    turn = [wave for cls in CLASSES for wave in waves(cls * count)]
    square = np.stack([cosine, sine, zero, eight]) / samples
    return square.astype(np.float32), np.stack(turn).astype(np.float32)


def put_matrix(ref, at, value, lanes):
    high, low = split(value)
    third = ref.shape[0] // 3
    for block, part in ((0, high), (1, high), (2, low)):
        start = block * third + at
        ref[start : start + value.shape[0], lanes] = part


def put_rows(ref, slot, rows, at, value):
    high, low = split(value)
    past = ref.shape[2] // 2 + at
    ref[slot, rows, at : at + value.shape[1]] = high
    ref[slot, rows, past : past + value.shape[1]] = low


def frequency_weights(psd_ref, wts_ref, samples):
    length = samples // RADIX
    half = length // 2
    power = jnp.concatenate([psd_ref[:, half * i : half * (i + 1)] for i in range(RADIX)], axis=0)
    spread = (iota((RADIX, half), 0) == iota((RADIX, half), 1) >> 3).astype(jnp.bfloat16)
    keep = (iota((half, half), 0) >> 4) == (iota((half, half), 1) & (half // RADIX - 1))
    pick_up = ((iota((RADIX, half), 1) & (RADIX - 1)) == iota((RADIX, half), 0)).astype(jnp.bfloat16)
    pick_down = ((iota((RADIX, half), 1) + iota((RADIX, half), 0)) & (RADIX - 1) == 0).astype(
        jnp.bfloat16
    )
    flip = (iota((half, half), 0) + iota((half, half), 1) == half - 1).astype(jnp.bfloat16)
    up = jnp.zeros((RADIX, half), jnp.float32)
    down = jnp.zeros((RADIX, half), jnp.float32)
    for digits, unit in ((power >> 8, 256.0), (power & 255, 1.0)):
        digits = digits.astype(jnp.float32).astype(jnp.bfloat16)
        moved = lax.dot_general(
            digits, spread, (((0,), (0,)), ((), ())), preferred_element_type=jnp.float32
        )
        moved = jnp.where(keep, moved, 0.0).astype(jnp.bfloat16)
        up = up + unit * jnp.dot(pick_up, moved, preferred_element_type=jnp.float32)
        back = jnp.dot(pick_down, moved, preferred_element_type=jnp.float32).astype(jnp.bfloat16)
        down = down + unit * jnp.dot(back, flip, preferred_element_type=jnp.float32)
    up = 2.0 * (8192.0 / up)
    down = 2.0 * (8192.0 / down)
    last = 8192.0 / psd_ref[:, samples // 2 : samples // 2 + 1].astype(jnp.float32)
    first = iota((1, half), 1) == 0
    wts_ref[0:1, 0:half] = jnp.where(first, 0.5 * up[0:1], up[0:1])
    wts_ref[0:1, half:length] = jnp.where(first, last, up[0:1])
    wts_ref[1:2, 0:half] = up[RADIX // 2 : RADIX // 2 + 1]
    wts_ref[1:2, half:length] = up[RADIX // 2 : RADIX // 2 + 1]
    for slot, cls in enumerate(CLASSES):
        for at in (0, length):
            wts_ref[slot + 2 : slot + 3, at : at + half] = up[cls : cls + 1]
            wts_ref[slot + 2 : slot + 3, at + half : at + length] = down[cls : cls + 1]


def even_classes(d):
    r = math.sqrt(0.5)
    even, alt = [], []
    for q in range(4):
        first, second = d(q) + d(q + 8), d(q + 4) + d(q + 12)
        even.append(first + second)
        alt.append(first - second)
    e02, e13 = even[0] + even[2], even[1] + even[3]
    four = (even[0] - even[2], even[3] - even[1])
    p, q = r * (alt[1] - alt[3]), r * (alt[1] + alt[3])
    two = (alt[0] + p, -(alt[2] + q))
    six = (alt[0] - p, alt[2] - q)
    return (e02 + e13, e02 - e13), (two, four, six)


def odd_classes(d):
    br, bi = [], []
    for q in range(4):
        real, imag = d(q) - d(q + 8), d(q + 12) - d(q + 4)
        c, s = math.cos(math.pi * q / 8), math.sin(math.pi * q / 8)
        if q == 2:
            real, imag = c * (real + imag), c * (imag - real)
        elif q:
            real, imag = c * real + s * imag, c * imag - s * real
        br.append(real)
        bi.append(imag)
    sr, si = br[0] + br[2], bi[0] + bi[2]
    tr, ti = br[1] + br[3], bi[1] + bi[3]
    ur, ui = br[0] - br[2], bi[0] - bi[2]
    vr, vi = br[1] - br[3], bi[1] - bi[3]
    return (sr + tr, si + ti), (ur + vi, ui - vr), (sr - tr, si - ti), (ur - vi, ui + vr)


def kernel(
    devices_tm,
    angles_hbm,
    mask_hbm,
    columns_hbm,
    coeffs_hbm,
    psd_hbm,
    square_hbm,
    twiddle_hbm,
    own_ref,
    other_ref,
    angles_ref,
    mask_ref,
    columns_ref,
    coeffs_ref,
    psd_ref,
    orbit,
    far_coeffs,
    far_columns,
    coeffs_t,
    column_t,
    basis_a,
    basis_b,
    design,
    real,
    pair_even,
    pair_odd,
    mat_real,
    mat,
    square,
    twiddle,
    wts,
    total,
    send_sem,
    recv_sem,
    side_send,
    side_recv,
    load_sem,
):
    block = angles_ref.shape[1]
    samples = block * devices_tm
    length = samples // RADIX
    half = length // 2
    terms = coeffs_ref.shape[1]
    terms_lat = terms // 2
    columns = coeffs_ref.shape[2]
    rows = own_ref.shape[0]
    everyone = rows + columns
    me = lax.axis_index("tm")
    panel = lax.axis_index("panel")
    comp = lax.axis_index("comp")

    loads = [
        pltpu.make_async_copy(source, held, load_sem.at[i])
        for i, (source, held) in enumerate(
            (
                (angles_hbm, angles_ref),
                (mask_hbm, mask_ref),
                (columns_hbm, columns_ref),
                (coeffs_hbm, coeffs_ref),
                (psd_hbm, psd_ref),
                (twiddle_hbm, twiddle),
                (square_hbm, square),
            )
        )
    ]
    for load in loads:
        load.start()
    barrier = pltpu.get_barrier_semaphore()
    peers = [lax.rem(me + k, devices_tm) for k in range(1, devices_tm)]
    for peer in peers:
        pl.semaphore_signal(barrier, inc=1, device_id={"tm": peer}, device_id_type=MESH)
    pl.semaphore_signal(barrier, inc=1, device_id={"panel": 1 - panel}, device_id_type=MESH)
    pl.semaphore_signal(barrier, inc=1, device_id={"comp": 1 - comp}, device_id_type=MESH)

    loads[0].wait()
    loads[1].wait()
    orbit[me, 0:2, :] = angles_ref[...] * (0.5 / math.pi)
    orbit[me, 2:3, :] = mask_ref[...].astype(jnp.float32)
    pl.semaphore_wait(barrier, devices_tm + 1)

    def send_orbit(k, slot, peer):
        return pltpu.make_async_remote_copy(
            src_ref=orbit.at[slot],
            dst_ref=orbit.at[slot],
            send_sem=send_sem.at[k],
            recv_sem=recv_sem.at[slot],
            device_id={"tm": peer},
            device_id_type=MESH,
        )

    for k, peer in enumerate(peers):
        send_orbit(k, me, peer).start()
    first_row = me * rows
    lanes = pl.ds(pl.multiple_of(lax.rem(first_row, columns), rows), rows)
    send_coeffs = pltpu.make_async_remote_copy(
        src_ref=coeffs_hbm.at[0, :, lanes],
        dst_ref=far_coeffs,
        send_sem=side_send.at[0],
        recv_sem=side_recv.at[0],
        device_id={"panel": 1 - panel},
        device_id_type=MESH,
    )
    send_columns = pltpu.make_async_remote_copy(
        src_ref=columns_hbm.at[:, lanes],
        dst_ref=far_columns,
        send_sem=side_send.at[1],
        recv_sem=side_recv.at[1],
        device_id={"panel": 1 - panel},
        device_id_type=MESH,
    )
    send_coeffs.start()
    send_columns.start()

    loads[6].wait()
    left, right = slice(0, length), slice(length, 2 * length)
    put_matrix(mat, 0, square[0], left)
    put_matrix(mat, 0, -square[1], right)
    put_matrix(mat, length, square[1], left)
    put_matrix(mat, length, square[0], right)
    put_matrix(mat_real.at[0], 0, square[2], left)
    put_matrix(mat_real.at[1], 0, square[3], left)
    loads[4].wait()
    frequency_weights(psd_ref, wts, samples)

    def place(at, coeffs, index_rows):
        width = coeffs.shape[1]
        level = iota((terms, width), 0)
        level = jnp.where(level < terms_lat, level, level - terms_lat)
        masked = jnp.where(level <= index_rows[0:1, :], coeffs, 0.0)
        coeffs_t[at : at + width, :] = jnp.transpose(masked).astype(jnp.bfloat16)
        orders = index_rows[1:2, :]
        shift = jnp.where(orders >= 0, 0.0, 0.25)
        norm = 1.0 / jnp.sqrt(index_rows[0:1, :].astype(jnp.float32) + 1.0)
        packed = jnp.concatenate(
            [jnp.abs(orders).astype(jnp.float32), shift]
            + [norm * term for term in SINE_LON]
            + [jnp.zeros((2, width), jnp.float32)],
            axis=0,
        )
        turned = jnp.transpose(packed)
        for i in range(2 + len(SINE_LON)):
            column_t[i, at : at + width, :] = jnp.broadcast_to(turned[:, i : i + 1], (width, 128))

    loads[2].wait()
    loads[3].wait()
    place(0, coeffs_ref[0].astype(jnp.float32), columns_ref[...])
    send_coeffs.wait()
    send_columns.wait()
    mine = first_row // columns == panel
    near = coeffs_ref[0, :, lanes].astype(jnp.float32)
    place(
        columns,
        jnp.where(mine, near, far_coeffs[...].astype(jnp.float32)),
        jnp.where(mine, columns_ref[:, lanes], far_columns[...]),
    )
    for k, peer in enumerate(peers):
        send_orbit(k, me, peer).wait_send()
    for k, peer in enumerate(peers):
        send_orbit(k, peer, peer).wait_recv()

    per_device = block // length

    def epoch_rows(chunk):
        where = pl.ds(pl.multiple_of(lax.rem(chunk, per_device) * length, length), length)
        return orbit[chunk // per_device, :, where]

    def fill_basis(chunk, basis):
        part = epoch_rows(chunk)
        theta, keep = part[0:1], part[2:3]
        turns = iota((16, length), 0).astype(jnp.float32) * theta
        cosine, sine = cos_turns(turns) * keep, cos_turns(turns - 0.25) * keep
        step_c, step_s = cos_turns(16.0 * theta), cos_turns(16.0 * theta - 0.25)
        for at in range(0, terms_lat, 16):
            basis[at : at + 16, :] = cosine.astype(jnp.bfloat16)
            basis[terms_lat + at : terms_lat + at + 16, :] = sine.astype(jnp.bfloat16)
            cosine, sine = cosine * step_c - sine * step_s, sine * step_c + cosine * step_s

    def fill_design(chunk, basis):
        longit = epoch_rows(chunk)[1:2]
        latitude = jnp.dot(coeffs_t[...], basis[...], preferred_element_type=jnp.float32)
        terms_lon = [column_t[2 + i] for i in range(len(SINE_LON))]
        for lane in range(0, length, 128):
            lanes = slice(lane, lane + 128)
            wave = cos_turns(column_t[0] * longit[:, lanes] - column_t[1], terms_lon)
            design[chunk, :, lanes] = latitude[:, lanes] * wave

    fill_basis(0, basis_a)

    def two_chunks(i, carry):
        fill_basis(2 * i + 1, basis_b)
        fill_design(2 * i, basis_a)
        fill_basis(lax.rem(2 * i + 2, RADIX), basis_a)
        fill_design(2 * i + 1, basis_b)
        return carry

    lax.fori_loop(0, RADIX // 2, two_chunks, 0)

    def turn(slot, pair, at, lane, value):
        re, im = value
        c = twiddle[2 * slot : 2 * slot + 1, lane : lane + 128]
        s = twiddle[2 * slot + 1 : 2 * slot + 2, lane : lane + 128]
        place_at = slot if slot < EVEN else slot - EVEN
        put_rows(pair, place_at, at, lane, re * c + im * s)
        put_rows(pair, place_at, at, length + lane, im * c - re * s)

    def fold_even(i, carry):
        at = pl.ds(pl.multiple_of(i * 16, 16), 16)
        for lane in range(0, length, 128):
            plain, pairs = even_classes(lambda q: design[q, at, lane : lane + 128])
            for slot, value in enumerate(plain):
                put_rows(real, slot, at, lane, value)
            for slot, value in enumerate(pairs):
                turn(slot, pair_even, at, lane, value)
        return carry

    def fold_odd(i):
        at = pl.ds(pl.multiple_of(i * 16, 16), 16)
        for lane in range(0, length, 128):
            for slot, value in enumerate(odd_classes(lambda q: design[q, at, lane : lane + 128])):
                turn(EVEN + slot, pair_odd, at, lane, value)

    loads[5].wait()
    lax.fori_loop(0, everyone // 16, fold_even, 0)

    def gram(parts, matrix, weight):
        high = parts[:, : parts.shape[1] // 2]
        spectra = jnp.dot(
            jnp.concatenate([parts, high], axis=1), matrix, preferred_element_type=jnp.float32
        ).astype(jnp.bfloat16)
        weighted = (spectra[:columns].astype(jnp.float32) * weight).astype(jnp.bfloat16)
        return lax.dot_general(
            spectra[columns:], weighted, (((1,), (1,)), ((), ())), preferred_element_type=jnp.float32
        )

    total[...] = jnp.zeros_like(total)
    units = everyone // 16 // EVEN

    def even_step(slot, carry):
        total[...] += gram(pair_even[slot], mat[...], wts[pl.ds(slot + 2, 1), :])
        for unit in range(units):
            fold_odd(slot * units + unit)
        return carry

    def odd_step(slot, carry):
        total[...] += gram(pair_odd[slot], mat[...], wts[pl.ds(slot + 2 + EVEN, 1), :])
        return carry

    lax.fori_loop(0, EVEN, even_step, 0)
    lax.fori_loop(0, len(CLASSES) - EVEN, odd_step, 0)
    for slot in range(2):
        total[...] += gram(real[slot], mat_real[slot], wts[slot : slot + 1, 0:length])
    swap = pltpu.make_async_remote_copy(
        src_ref=total,
        dst_ref=other_ref,
        send_sem=side_send.at[2],
        recv_sem=side_recv.at[2],
        device_id={"comp": 1 - comp},
        device_id_type=MESH,
    )
    swap.start()
    own_ref[...] = total[...]
    swap.wait()


def fused(orbit_angles, gap_mask, column_index, lat_coeffs, psd_table):
    devices_tm = lax.axis_size("tm")
    block = orbit_angles.shape[1]
    samples = devices_tm * block
    length = samples // RADIX
    terms, columns = lat_coeffs.shape[1:]
    rows = columns * lax.axis_size("panel") // devices_tm
    everyone = rows + columns
    f32, bf16 = jnp.float32, jnp.bfloat16
    vmem = pl.BlockSpec(memory_space=pltpu.VMEM)
    count = len(CLASSES)
    own, other = pl.pallas_call(
        functools.partial(kernel, devices_tm),
        out_shape=[jax.ShapeDtypeStruct((rows, columns), f32)] * 2,
        in_specs=[pl.BlockSpec(memory_space=pltpu.HBM)] * 7,
        out_specs=[vmem] * 2,
        scratch_shapes=[
            pltpu.VMEM(orbit_angles.shape, f32),
            pltpu.VMEM((1, block), jnp.int32),
            pltpu.VMEM(column_index.shape, jnp.int32),
            pltpu.VMEM(lat_coeffs.shape, bf16),
            pltpu.VMEM(psd_table.shape, jnp.int32),
            pltpu.VMEM((devices_tm, 8, block), f32),
            pltpu.VMEM((terms, rows), bf16),
            pltpu.VMEM((2, rows), jnp.int32),
            pltpu.VMEM((everyone, terms), bf16),
            pltpu.VMEM((2 + len(SINE_LON), everyone, 128), f32),
            pltpu.VMEM((terms, length), bf16),
            pltpu.VMEM((terms, length), bf16),
            pltpu.VMEM((RADIX, everyone, length), f32),
            pltpu.VMEM((2, everyone, 2 * length), bf16),
            pltpu.VMEM((EVEN, everyone, 4 * length), bf16),
            pltpu.VMEM((count - EVEN, everyone, 4 * length), bf16),
            pltpu.VMEM((2, 3 * length, length), bf16),
            pltpu.VMEM((6 * length, 2 * length), bf16),
            pltpu.VMEM((4, length, length), f32),
            pltpu.VMEM((2 * count, length), f32),
            pltpu.VMEM((16, 2 * length), f32),
            pltpu.VMEM((rows, columns), f32),
            pltpu.SemaphoreType.DMA((devices_tm,)),
            pltpu.SemaphoreType.DMA((devices_tm,)),
            pltpu.SemaphoreType.DMA((3,)),
            pltpu.SemaphoreType.DMA((3,)),
            pltpu.SemaphoreType.DMA((7,)),
        ],
        compiler_params=pltpu.CompilerParams(
            collective_id=0, has_side_effects=True, vmem_limit_bytes=63 * 1024 * 1024
        ),
    )(orbit_angles, gap_mask.reshape(1, block), column_index, lat_coeffs, psd_table, *tables(length))
    return own + other


def choose(orbit_angles, gap_mask, column_index, lat_coeffs, psd_table):
    devices_tm, panels = lax.axis_size("tm"), lax.axis_size("panel")
    samples = devices_tm * orbit_angles.shape[1]
    columns = lat_coeffs.shape[2]
    rows = columns * panels // devices_tm
    fits = (
        samples == 4096
        and orbit_angles.shape[1] % 256 == 0
        and panels == 2
        and lax.axis_size("comp") == 2
        and rows % 128 == 0
        and columns % rows == 0
        and lat_coeffs.shape[1] % 32 == 0
        and (rows + columns) * lat_coeffs.shape[1] <= 512 * 1024
    )
    step = fused if fits else body
    return step(orbit_angles, gap_mask, column_index, lat_coeffs, psd_table)


def solution(mesh):
    return jax.shard_map(
        choose,
        mesh=mesh,
        in_specs=(
            P(None, ("groups", "tm")),
            P(("groups", "tm")),
            P(None, "panel"),
            P("comp", None, "panel"),
            P("comp", None),
        ),
        out_specs=P(("groups", "tm"), "panel"),
        check_vma=False,
    )
```

```python
import functools
import math

import jax
import jax.numpy as jnp
import numpy as np
from jax import lax
from jax.experimental import pallas as pl
from jax.experimental.pallas import tpu as pltpu
from jax.sharding import PartitionSpec as P

SPLIT = 64


def synthesize(angles, keep_rows, column_index, coeffs):
    terms_lat = coeffs.shape[0] // 2
    colatitude = angles[0]
    longit = angles[1]
    wavenumbers = jnp.arange(terms_lat, dtype=jnp.float32)
    phases = colatitude[:, None] * wavenumbers[None, :]
    basis_rows = jnp.concatenate([jnp.cos(phases), jnp.sin(phases)], axis=1).astype(jnp.bfloat16)
    degree = column_index[0]
    orders = column_index[1]
    levels = jnp.arange(2 * terms_lat, dtype=jnp.int32) % terms_lat
    allowed = levels[:, None] <= degree[None, :]
    masked = jnp.where(allowed, coeffs, jnp.zeros_like(coeffs))
    latitude = jnp.dot(basis_rows, masked, preferred_element_type=jnp.float32)
    lon_phase = longit[:, None] * jnp.abs(orders).astype(jnp.float32)[None, :]
    lon_wave = jnp.where(orders[None, :] >= 0, jnp.cos(lon_phase), jnp.sin(lon_phase))
    norm_scale = 1.0 / jnp.sqrt(degree.astype(jnp.float32) + 1.0)
    return latitude * lon_wave * (keep_rows[:, None] * norm_scale[None, :])


def phase_tables(row_index, col_index, length):
    product = row_index[:, None] * col_index[None, :] % length
    angle_grid = product.astype(jnp.float32) * (2.0 * math.pi / length)
    return (jnp.cos(angle_grid), jnp.sin(angle_grid))


def dft_tables(length):
    indices = jnp.arange(length, dtype=jnp.int32)
    return phase_tables(indices, indices, length)


def rotate(real_part, imag_part, outer_index, inner_index, length):
    index_grid = outer_index[:, None] * inner_index[None, :] % length
    angle_grid = index_grid.astype(jnp.float32) * (2.0 * math.pi / length)
    cosine = jnp.cos(angle_grid)[:, :, None]
    sine_grid = jnp.sin(angle_grid)[:, :, None]
    return (real_part * cosine + imag_part * sine_grid, imag_part * cosine - real_part * sine_grid)


def precise_dot(left_side, right_side):
    return jnp.dot(
        left_side, right_side, precision=lax.Precision.HIGHEST, preferred_element_type=jnp.float32
    )


def transform(cos_table, sin_table, real_part, imag_part):
    new_real = precise_dot(cos_table, real_part) + precise_dot(sin_table, imag_part)
    new_imag = precise_dot(cos_table, imag_part) - precise_dot(sin_table, real_part)
    return (new_real, new_imag)


def four_step(real_in, imag_in, samples):
    length = real_in.shape[0]
    columns = real_in.shape[1]
    outer_count = SPLIT
    inner_count = length // SPLIT
    real_part = real_in.reshape(outer_count, inner_count * columns)
    imag_part = imag_in.reshape(outer_count, inner_count * columns)
    cos_outer, sin_outer = dft_tables(outer_count)
    real_part, imag_part = transform(cos_outer, sin_outer, real_part, imag_part)
    real_part = real_part.reshape(outer_count, inner_count, columns)
    imag_part = imag_part.reshape(outer_count, inner_count, columns)
    real_part, imag_part = rotate(
        real_part,
        imag_part,
        jnp.arange(outer_count, dtype=jnp.int32),
        jnp.arange(inner_count, dtype=jnp.int32),
        length,
    )
    real_part = jnp.transpose(real_part, (1, 0, 2)).reshape(inner_count, outer_count * columns)
    imag_part = jnp.transpose(imag_part, (1, 0, 2)).reshape(inner_count, outer_count * columns)
    cos_inner, sin_inner = dft_tables(inner_count)
    real_part, imag_part = transform(cos_inner, sin_inner, real_part, imag_part)
    return (
        real_part.reshape(length, columns) / samples,
        imag_part.reshape(length, columns) / samples,
    )


def local_transform(received, samples):
    real_part, imag_part = four_step(received[0, 0], received[1, 0], samples)
    return (real_part.astype(jnp.bfloat16), imag_part.astype(jnp.bfloat16))


def noise_weighted(spectra, psd_row, frequency, samples):
    folded = jnp.minimum(frequency, samples - frequency)
    inverse_psd = 8192.0 / jnp.take(psd_row, folded).astype(jnp.float32)
    return (spectra.astype(jnp.float32) * inverse_psd[None, :, None]).astype(jnp.bfloat16)


def settle(partial_value, sum_dim):
    summed = lax.psum_scatter(partial_value, "tm", scatter_dimension=sum_dim, tiled=True)
    return lax.psum(summed, "comp")


def body(orbit_angles, gap_mask, column_index, lat_coeffs, psd_table):
    devices_tm = lax.axis_size("tm")
    epochs = orbit_angles.shape[1]
    block_len = epochs // devices_tm
    samples = epochs * devices_tm
    columns = lat_coeffs.shape[2]
    coeffs = lat_coeffs[0]
    keep_rows = gap_mask.astype(jnp.float32)
    packed = jnp.concatenate([orbit_angles, keep_rows[None]], axis=0)[:, None, :]
    received = lax.all_to_all(packed, "tm", split_axis=2, concat_axis=1, tiled=True)
    flat_orbit = received.reshape(3, devices_tm * block_len)
    spread = synthesize(flat_orbit[0:2], flat_orbit[2], column_index, coeffs).reshape(
        devices_tm, block_len, columns
    )
    position = lax.axis_index("tm")
    local_epoch = position * block_len + jnp.arange(block_len, dtype=jnp.int32)
    cos_outer, sin_outer = dft_tables(devices_tm)
    flat_design = spread.reshape(devices_tm, block_len * columns)
    real_part = precise_dot(cos_outer, flat_design).reshape(devices_tm, block_len, columns)
    imag_part = -precise_dot(sin_outer, flat_design).reshape(devices_tm, block_len, columns)
    real_part, imag_part = rotate(
        real_part, imag_part, jnp.arange(devices_tm, dtype=jnp.int32), local_epoch, samples
    )
    twisted = jnp.stack([real_part, imag_part])
    spec_real, spec_imag = local_transform(
        lax.all_to_all(twisted, "tm", split_axis=1, concat_axis=2, tiled=True), samples
    )
    spectra = jnp.stack([spec_real, spec_imag])
    psd_row = psd_table[0]
    contract = (((0, 1), (0, 1)), ((), ()))
    frequency = position + devices_tm * jnp.arange(epochs, dtype=jnp.int32)
    weighted = noise_weighted(spectra, psd_row, frequency, samples)
    partial_value = lax.dot_general(
        lax.all_gather(spectra, "panel", axis=2, tiled=True),
        weighted,
        contract,
        preferred_element_type=jnp.float32,
    )
    return settle(partial_value, 0)


RADIX = 16
SINE_LON = (6.283164044168851, -41.33714234995496, 81.34076808172247, -70.99342472149007)
SINE_FINE = (
    6.283185160088548,
    -41.3416550311802,
    81.60100405747373,
    -76.54978191007581,
    39.53670300634923,
)
CLASSES = (2, 4, 6, 1, 5, 9, 13)
EVEN = 3
ROUNDER = 1.5 * 2.0**23
MESH = pl.DeviceIdType.MESH


def cos_turns(turns, terms=SINE_FINE):
    offset = turns - ((turns + ROUNDER) - ROUNDER)
    near = 0.25 - jnp.abs(offset)
    square = near * near
    total = terms[-1]
    for term in terms[-2::-1]:
        total = total * square + term
    return total * near


def iota(shape, dim):
    return lax.broadcasted_iota(jnp.int32, shape, dim)


def split(value):
    high = value.astype(jnp.bfloat16)
    return high, (value - high.astype(jnp.float32)).astype(jnp.bfloat16)


def tables(length):
    samples = RADIX * length
    half = length // 2

    def waves(product):
        angle = (product % samples) * (2.0 * np.pi / samples)
        return np.cos(angle), np.sin(angle)

    count = np.arange(length)
    cosine, sine = waves(RADIX * np.outer(count, count))
    zero = np.concatenate([cosine[:, :half], -sine[:, :half]], axis=1)
    zero[:, half] = 1 - 2 * (count % 2)
    eight = np.concatenate(waves(np.outer(count, RADIX // 2 + RADIX * count[:half])), axis=1)
    eight[:, half:] *= -1
    turn = [wave for cls in CLASSES for wave in waves(cls * count)]
    square = np.stack([cosine, sine, zero, eight]) / samples
    return square.astype(np.float32), np.stack(turn).astype(np.float32)


def put_matrix(ref, at, value, lanes):
    high, low = split(value)
    third = ref.shape[0] // 3
    for block, part in ((0, high), (1, high), (2, low)):
        start = block * third + at
        ref[start : start + value.shape[0], lanes] = part


def put_rows(ref, slot, rows, at, value):
    high, low = split(value)
    past = ref.shape[2] // 2 + at
    ref[slot, rows, at : at + value.shape[1]] = high
    ref[slot, rows, past : past + value.shape[1]] = low


def frequency_weights(psd_ref, wts_ref, samples):
    length = samples // RADIX
    half = length // 2
    power = jnp.concatenate([psd_ref[:, half * i : half * (i + 1)] for i in range(RADIX)], axis=0)
    spread = (iota((RADIX, half), 0) == iota((RADIX, half), 1) >> 3).astype(jnp.bfloat16)
    keep = (iota((half, half), 0) >> 4) == (iota((half, half), 1) & (half // RADIX - 1))
    pick_up = ((iota((RADIX, half), 1) & (RADIX - 1)) == iota((RADIX, half), 0)).astype(jnp.bfloat16)
    pick_down = ((iota((RADIX, half), 1) + iota((RADIX, half), 0)) & (RADIX - 1) == 0).astype(
        jnp.bfloat16
    )
    flip = (iota((half, half), 0) + iota((half, half), 1) == half - 1).astype(jnp.bfloat16)
    up = jnp.zeros((RADIX, half), jnp.float32)
    down = jnp.zeros((RADIX, half), jnp.float32)
    for digits, unit in ((power >> 8, 256.0), (power & 255, 1.0)):
        digits = digits.astype(jnp.float32).astype(jnp.bfloat16)
        moved = lax.dot_general(
            digits, spread, (((0,), (0,)), ((), ())), preferred_element_type=jnp.float32
        )
        moved = jnp.where(keep, moved, 0.0).astype(jnp.bfloat16)
        up = up + unit * jnp.dot(pick_up, moved, preferred_element_type=jnp.float32)
        back = jnp.dot(pick_down, moved, preferred_element_type=jnp.float32).astype(jnp.bfloat16)
        down = down + unit * jnp.dot(back, flip, preferred_element_type=jnp.float32)
    up = 2.0 * (8192.0 / up)
    down = 2.0 * (8192.0 / down)
    last = 8192.0 / psd_ref[:, samples // 2 : samples // 2 + 1].astype(jnp.float32)
    first = iota((1, half), 1) == 0
    wts_ref[0:1, 0:half] = jnp.where(first, 0.5 * up[0:1], up[0:1])
    wts_ref[0:1, half:length] = jnp.where(first, last, up[0:1])
    wts_ref[1:2, 0:half] = up[RADIX // 2 : RADIX // 2 + 1]
    wts_ref[1:2, half:length] = up[RADIX // 2 : RADIX // 2 + 1]
    for slot, cls in enumerate(CLASSES):
        for at in (0, length):
            wts_ref[slot + 2 : slot + 3, at : at + half] = up[cls : cls + 1]
            wts_ref[slot + 2 : slot + 3, at + half : at + length] = down[cls : cls + 1]


def even_classes(d):
    r = math.sqrt(0.5)
    even, alt = [], []
    for q in range(4):
        first, second = d(q) + d(q + 8), d(q + 4) + d(q + 12)
        even.append(first + second)
        alt.append(first - second)
    e02, e13 = even[0] + even[2], even[1] + even[3]
    four = (even[0] - even[2], even[3] - even[1])
    p, q = r * (alt[1] - alt[3]), r * (alt[1] + alt[3])
    two = (alt[0] + p, -(alt[2] + q))
    six = (alt[0] - p, alt[2] - q)
    return (e02 + e13, e02 - e13), (two, four, six)


def odd_classes(d):
    br, bi = [], []
    for q in range(4):
        real, imag = d(q) - d(q + 8), d(q + 12) - d(q + 4)
        c, s = math.cos(math.pi * q / 8), math.sin(math.pi * q / 8)
        if q == 2:
            real, imag = c * (real + imag), c * (imag - real)
        elif q:
            real, imag = c * real + s * imag, c * imag - s * real
        br.append(real)
        bi.append(imag)
    sr, si = br[0] + br[2], bi[0] + bi[2]
    tr, ti = br[1] + br[3], bi[1] + bi[3]
    ur, ui = br[0] - br[2], bi[0] - bi[2]
    vr, vi = br[1] - br[3], bi[1] - bi[3]
    return (sr + tr, si + ti), (ur + vi, ui - vr), (sr - tr, si - ti), (ur - vi, ui + vr)


def kernel(
    devices_tm,
    angles_hbm,
    mask_hbm,
    columns_hbm,
    coeffs_hbm,
    psd_hbm,
    square_hbm,
    twiddle_hbm,
    own_ref,
    other_ref,
    columns_ref,
    coeffs_ref,
    psd_ref,
    orbit,
    flags,
    far_coeffs,
    far_columns,
    coeffs_t,
    column_t,
    basis_a,
    basis_b,
    design,
    real,
    pair_even,
    pair_odd,
    mat_real,
    mat,
    square,
    twiddle,
    wts,
    total,
    send_sem,
    recv_sem,
    side_send,
    side_recv,
    load_sem,
):
    block = angles_hbm.shape[1]
    samples = block * devices_tm
    length = samples // RADIX
    half = length // 2
    terms = coeffs_ref.shape[1]
    terms_lat = terms // 2
    columns = coeffs_ref.shape[2]
    rows = own_ref.shape[0]
    everyone = rows + columns
    me = lax.axis_index("tm")
    panel = lax.axis_index("panel")
    comp = lax.axis_index("comp")

    barrier = pltpu.get_barrier_semaphore()
    peers = [lax.rem(me + k, devices_tm) for k in range(1, devices_tm)]
    for peer in peers:
        pl.semaphore_signal(barrier, inc=1, device_id={"tm": peer}, device_id_type=MESH)
    pl.semaphore_signal(barrier, inc=1, device_id={"panel": 1 - panel}, device_id_type=MESH)
    pl.semaphore_signal(barrier, inc=1, device_id={"comp": 1 - comp}, device_id_type=MESH)

    loads = [
        pltpu.make_async_copy(source, held, load_sem.at[i])
        for i, (source, held) in enumerate(
            (
                (angles_hbm, orbit.at[me]),
                (mask_hbm, flags.at[me]),
                (columns_hbm, columns_ref),
                (coeffs_hbm, coeffs_ref),
                (psd_hbm, psd_ref),
                (twiddle_hbm, twiddle),
                (square_hbm, square),
            )
        )
    ]
    for load in loads:
        load.start()
    pl.semaphore_wait(barrier, devices_tm + 1)

    def send_orbit(k, slot, peer):
        return [
            pltpu.make_async_remote_copy(
                src_ref=source,
                dst_ref=held.at[slot],
                send_sem=send_sem.at[i, k],
                recv_sem=recv_sem.at[i, slot],
                device_id={"tm": peer},
                device_id_type=MESH,
            )
            for i, (source, held) in enumerate(((angles_hbm, orbit), (mask_hbm, flags)))
        ]

    for k, peer in enumerate(peers):
        for copy in send_orbit(k, me, peer):
            copy.start()
    first_row = me * rows
    lanes = pl.ds(pl.multiple_of(lax.rem(first_row, columns), rows), rows)
    send_coeffs = pltpu.make_async_remote_copy(
        src_ref=coeffs_hbm.at[0, :, lanes],
        dst_ref=far_coeffs,
        send_sem=side_send.at[0],
        recv_sem=side_recv.at[0],
        device_id={"panel": 1 - panel},
        device_id_type=MESH,
    )
    send_columns = pltpu.make_async_remote_copy(
        src_ref=columns_hbm.at[:, lanes],
        dst_ref=far_columns,
        send_sem=side_send.at[1],
        recv_sem=side_recv.at[1],
        device_id={"panel": 1 - panel},
        device_id_type=MESH,
    )
    send_coeffs.start()
    send_columns.start()

    loads[6].wait()
    left, right = slice(0, length), slice(length, 2 * length)
    put_matrix(mat, 0, square[0], left)
    put_matrix(mat, 0, -square[1], right)
    put_matrix(mat, length, square[1], left)
    put_matrix(mat, length, square[0], right)
    put_matrix(mat_real.at[0], 0, square[2], left)
    put_matrix(mat_real.at[1], 0, square[3], left)
    loads[4].wait()
    frequency_weights(psd_ref, wts, samples)

    def place(at, coeffs, index_rows):
        width = coeffs.shape[1]
        level = iota((terms, width), 0)
        level = jnp.where(level < terms_lat, level, level - terms_lat)
        masked = jnp.where(level <= index_rows[0:1, :], coeffs, 0.0)
        coeffs_t[at : at + width, :] = jnp.transpose(masked).astype(jnp.bfloat16)
        orders = index_rows[1:2, :]
        shift = jnp.where(orders >= 0, 0.0, 0.25)
        norm = 1.0 / jnp.sqrt(index_rows[0:1, :].astype(jnp.float32) + 1.0)
        packed = jnp.concatenate(
            [jnp.abs(orders).astype(jnp.float32), shift]
            + [norm * term for term in SINE_LON]
            + [jnp.zeros((2, width), jnp.float32)],
            axis=0,
        )
        turned = jnp.transpose(packed)
        for i in range(2 + len(SINE_LON)):
            column_t[i, at : at + width, :] = jnp.broadcast_to(turned[:, i : i + 1], (width, 128))

    loads[2].wait()
    loads[3].wait()
    place(0, coeffs_ref[0].astype(jnp.float32), columns_ref[...])
    send_coeffs.wait()
    send_columns.wait()
    mine = first_row // columns == panel
    near = coeffs_ref[0, :, lanes].astype(jnp.float32)
    place(
        columns,
        jnp.where(mine, near, far_coeffs[...].astype(jnp.float32)),
        jnp.where(mine, columns_ref[:, lanes], far_columns[...]),
    )
    loads[0].wait()
    loads[1].wait()
    for k, peer in enumerate(peers):
        for copy in send_orbit(k, me, peer):
            copy.wait_send()
        for copy in send_orbit(k, peer, peer):
            copy.wait_recv()

    per_device = block // length

    def epoch_lanes(chunk):
        at = lax.rem(chunk, per_device) * length
        return chunk // per_device, pl.ds(pl.multiple_of(at, length), length)

    def fill_basis(chunk, basis):
        holder, lanes = epoch_lanes(chunk)
        theta = orbit[holder, 0:1, lanes] * (0.5 / math.pi)
        keep = flags[holder, :, lanes].astype(jnp.float32)
        turns = iota((16, length), 0).astype(jnp.float32) * theta
        cosine, sine = cos_turns(turns) * keep, cos_turns(turns - 0.25) * keep
        step_c, step_s = cos_turns(16.0 * theta), cos_turns(16.0 * theta - 0.25)
        for at in range(0, terms_lat, 16):
            basis[at : at + 16, :] = cosine.astype(jnp.bfloat16)
            basis[terms_lat + at : terms_lat + at + 16, :] = sine.astype(jnp.bfloat16)
            cosine, sine = cosine * step_c - sine * step_s, sine * step_c + cosine * step_s

    def fill_design(chunk, basis):
        holder, lanes = epoch_lanes(chunk)
        longit = orbit[holder, 1:2, lanes] * (0.5 / math.pi)
        latitude = jnp.dot(coeffs_t[...], basis[...], preferred_element_type=jnp.float32)
        terms_lon = [column_t[2 + i] for i in range(len(SINE_LON))]
        for lane in range(0, length, 128):
            where = slice(lane, lane + 128)
            wave = cos_turns(column_t[0] * longit[:, where] - column_t[1], terms_lon)
            design[chunk, :, where] = latitude[:, where] * wave

    fill_basis(0, basis_a)

    def two_chunks(i, carry):
        fill_basis(2 * i + 1, basis_b)
        fill_design(2 * i, basis_a)
        fill_basis(lax.rem(2 * i + 2, RADIX), basis_a)
        fill_design(2 * i + 1, basis_b)
        return carry

    lax.fori_loop(0, RADIX // 2, two_chunks, 0)

    def turn(slot, pair, at, lane, value):
        re, im = value
        c = twiddle[2 * slot : 2 * slot + 1, lane : lane + 128]
        s = twiddle[2 * slot + 1 : 2 * slot + 2, lane : lane + 128]
        place_at = slot if slot < EVEN else slot - EVEN
        put_rows(pair, place_at, at, lane, re * c + im * s)
        put_rows(pair, place_at, at, length + lane, im * c - re * s)

    def fold_even(i, carry):
        at = pl.ds(pl.multiple_of(i * 16, 16), 16)
        for lane in range(0, length, 128):
            plain, pairs = even_classes(lambda q: design[q, at, lane : lane + 128])
            for slot, value in enumerate(plain):
                put_rows(real, slot, at, lane, value)
            for slot, value in enumerate(pairs):
                turn(slot, pair_even, at, lane, value)
        return carry

    def fold_odd(i):
        at = pl.ds(pl.multiple_of(i * 16, 16), 16)
        for lane in range(0, length, 128):
            for slot, value in enumerate(odd_classes(lambda q: design[q, at, lane : lane + 128])):
                turn(EVEN + slot, pair_odd, at, lane, value)

    loads[5].wait()
    lax.fori_loop(0, everyone // 16, fold_even, 0)

    def gram(parts, matrix, weight):
        high = parts[:, : parts.shape[1] // 2]
        spectra = jnp.dot(
            jnp.concatenate([parts, high], axis=1), matrix, preferred_element_type=jnp.float32
        ).astype(jnp.bfloat16)
        weighted = (spectra[:columns].astype(jnp.float32) * weight).astype(jnp.bfloat16)
        total[...] += lax.dot_general(
            spectra[columns:], weighted, (((1,), (1,)), ((), ())), preferred_element_type=jnp.float32
        )

    total[...] = jnp.zeros_like(total)
    units = everyone // 16 // EVEN

    def even_step(slot, carry):
        for part in range(2):
            lanes = slice(part * length, (part + 1) * length)
            gram(pair_even[slot], mat[:, lanes], wts[pl.ds(slot + 2, 1), lanes])
            for unit in range(part * units // 2, (part + 1) * units // 2):
                fold_odd(slot * units + unit)
        return carry

    def odd_step(slot, carry):
        for part in range(2):
            lanes = slice(part * length, (part + 1) * length)
            gram(pair_odd[slot], mat[:, lanes], wts[pl.ds(slot + 2 + EVEN, 1), lanes])
        return carry

    lax.fori_loop(0, EVEN, even_step, 0)
    lax.fori_loop(0, len(CLASSES) - EVEN, odd_step, 0)
    for slot in range(2):
        gram(real[slot], mat_real[slot], wts[slot : slot + 1, 0:length])
    swap = pltpu.make_async_remote_copy(
        src_ref=total,
        dst_ref=other_ref,
        send_sem=side_send.at[2],
        recv_sem=side_recv.at[2],
        device_id={"comp": 1 - comp},
        device_id_type=MESH,
    )
    swap.start()
    own_ref[...] = total[...]
    swap.wait()


def fused(orbit_angles, gap_mask, column_index, lat_coeffs, psd_table):
    devices_tm = lax.axis_size("tm")
    block = orbit_angles.shape[1]
    samples = devices_tm * block
    length = samples // RADIX
    terms, columns = lat_coeffs.shape[1:]
    rows = columns * lax.axis_size("panel") // devices_tm
    everyone = rows + columns
    f32, bf16 = jnp.float32, jnp.bfloat16
    vmem = pl.BlockSpec(memory_space=pltpu.VMEM)
    count = len(CLASSES)
    own, other = pl.pallas_call(
        functools.partial(kernel, devices_tm),
        out_shape=[jax.ShapeDtypeStruct((rows, columns), f32)] * 2,
        in_specs=[pl.BlockSpec(memory_space=pltpu.HBM)] * 7,
        out_specs=[vmem] * 2,
        scratch_shapes=[
            pltpu.VMEM(column_index.shape, jnp.int32),
            pltpu.VMEM(lat_coeffs.shape, bf16),
            pltpu.VMEM(psd_table.shape, jnp.int32),
            pltpu.VMEM((devices_tm, 2, block), f32),
            pltpu.VMEM((devices_tm, 1, block), jnp.int32),
            pltpu.VMEM((terms, rows), bf16),
            pltpu.VMEM((2, rows), jnp.int32),
            pltpu.VMEM((everyone, terms), bf16),
            pltpu.VMEM((2 + len(SINE_LON), everyone, 128), f32),
            pltpu.VMEM((terms, length), bf16),
            pltpu.VMEM((terms, length), bf16),
            pltpu.VMEM((RADIX, everyone, length), f32),
            pltpu.VMEM((2, everyone, 2 * length), bf16),
            pltpu.VMEM((EVEN, everyone, 4 * length), bf16),
            pltpu.VMEM((count - EVEN, everyone, 4 * length), bf16),
            pltpu.VMEM((2, 3 * length, length), bf16),
            pltpu.VMEM((6 * length, 2 * length), bf16),
            pltpu.VMEM((4, length, length), f32),
            pltpu.VMEM((2 * count, length), f32),
            pltpu.VMEM((16, 2 * length), f32),
            pltpu.VMEM((rows, columns), f32),
            pltpu.SemaphoreType.DMA((2, devices_tm)),
            pltpu.SemaphoreType.DMA((2, devices_tm)),
            pltpu.SemaphoreType.DMA((3,)),
            pltpu.SemaphoreType.DMA((3,)),
            pltpu.SemaphoreType.DMA((7,)),
        ],
        compiler_params=pltpu.CompilerParams(
            collective_id=0, has_side_effects=True, vmem_limit_bytes=63 * 1024 * 1024
        ),
    )(orbit_angles, gap_mask.reshape(1, block), column_index, lat_coeffs, psd_table, *tables(length))
    return own + other


def choose(orbit_angles, gap_mask, column_index, lat_coeffs, psd_table):
    devices_tm, panels = lax.axis_size("tm"), lax.axis_size("panel")
    samples = devices_tm * orbit_angles.shape[1]
    columns = lat_coeffs.shape[2]
    rows = columns * panels // devices_tm
    fits = (
        samples == 4096
        and orbit_angles.shape[1] % 256 == 0
        and panels == 2
        and lax.axis_size("comp") == 2
        and rows % 128 == 0
        and columns % rows == 0
        and lat_coeffs.shape[1] % 32 == 0
        and (rows + columns) * lat_coeffs.shape[1] <= 512 * 1024
    )
    step = fused if fits else body
    return step(orbit_angles, gap_mask, column_index, lat_coeffs, psd_table)


def solution(mesh):
    return jax.shard_map(
        choose,
        mesh=mesh,
        in_specs=(
            P(None, ("groups", "tm")),
            P(("groups", "tm")),
            P(None, "panel"),
            P("comp", None, "panel"),
            P("comp", None),
        ),
        out_specs=P(("groups", "tm"), "panel"),
        check_vma=False,
    )
```

```python
import functools
import math

import jax
import jax.numpy as jnp
import numpy as np
from jax import lax
from jax.experimental import pallas as pl
from jax.experimental.pallas import tpu as pltpu
from jax.sharding import PartitionSpec as P

SPLIT = 64


def synthesize(angles, keep_rows, column_index, coeffs):
    terms_lat = coeffs.shape[0] // 2
    colatitude = angles[0]
    longit = angles[1]
    wavenumbers = jnp.arange(terms_lat, dtype=jnp.float32)
    phases = colatitude[:, None] * wavenumbers[None, :]
    basis_rows = jnp.concatenate([jnp.cos(phases), jnp.sin(phases)], axis=1).astype(jnp.bfloat16)
    degree = column_index[0]
    orders = column_index[1]
    levels = jnp.arange(2 * terms_lat, dtype=jnp.int32) % terms_lat
    allowed = levels[:, None] <= degree[None, :]
    masked = jnp.where(allowed, coeffs, jnp.zeros_like(coeffs))
    latitude = jnp.dot(basis_rows, masked, preferred_element_type=jnp.float32)
    lon_phase = longit[:, None] * jnp.abs(orders).astype(jnp.float32)[None, :]
    lon_wave = jnp.where(orders[None, :] >= 0, jnp.cos(lon_phase), jnp.sin(lon_phase))
    norm_scale = 1.0 / jnp.sqrt(degree.astype(jnp.float32) + 1.0)
    return latitude * lon_wave * (keep_rows[:, None] * norm_scale[None, :])


def phase_tables(row_index, col_index, length):
    product = row_index[:, None] * col_index[None, :] % length
    angle_grid = product.astype(jnp.float32) * (2.0 * math.pi / length)
    return (jnp.cos(angle_grid), jnp.sin(angle_grid))


def dft_tables(length):
    indices = jnp.arange(length, dtype=jnp.int32)
    return phase_tables(indices, indices, length)


def rotate(real_part, imag_part, outer_index, inner_index, length):
    index_grid = outer_index[:, None] * inner_index[None, :] % length
    angle_grid = index_grid.astype(jnp.float32) * (2.0 * math.pi / length)
    cosine = jnp.cos(angle_grid)[:, :, None]
    sine_grid = jnp.sin(angle_grid)[:, :, None]
    return (real_part * cosine + imag_part * sine_grid, imag_part * cosine - real_part * sine_grid)


def precise_dot(left_side, right_side):
    return jnp.dot(
        left_side, right_side, precision=lax.Precision.HIGHEST, preferred_element_type=jnp.float32
    )


def transform(cos_table, sin_table, real_part, imag_part):
    new_real = precise_dot(cos_table, real_part) + precise_dot(sin_table, imag_part)
    new_imag = precise_dot(cos_table, imag_part) - precise_dot(sin_table, real_part)
    return (new_real, new_imag)


def four_step(real_in, imag_in, samples):
    length = real_in.shape[0]
    columns = real_in.shape[1]
    outer_count = SPLIT
    inner_count = length // SPLIT
    real_part = real_in.reshape(outer_count, inner_count * columns)
    imag_part = imag_in.reshape(outer_count, inner_count * columns)
    cos_outer, sin_outer = dft_tables(outer_count)
    real_part, imag_part = transform(cos_outer, sin_outer, real_part, imag_part)
    real_part = real_part.reshape(outer_count, inner_count, columns)
    imag_part = imag_part.reshape(outer_count, inner_count, columns)
    real_part, imag_part = rotate(
        real_part,
        imag_part,
        jnp.arange(outer_count, dtype=jnp.int32),
        jnp.arange(inner_count, dtype=jnp.int32),
        length,
    )
    real_part = jnp.transpose(real_part, (1, 0, 2)).reshape(inner_count, outer_count * columns)
    imag_part = jnp.transpose(imag_part, (1, 0, 2)).reshape(inner_count, outer_count * columns)
    cos_inner, sin_inner = dft_tables(inner_count)
    real_part, imag_part = transform(cos_inner, sin_inner, real_part, imag_part)
    return (
        real_part.reshape(length, columns) / samples,
        imag_part.reshape(length, columns) / samples,
    )


def local_transform(received, samples):
    real_part, imag_part = four_step(received[0, 0], received[1, 0], samples)
    return (real_part.astype(jnp.bfloat16), imag_part.astype(jnp.bfloat16))


def noise_weighted(spectra, psd_row, frequency, samples):
    folded = jnp.minimum(frequency, samples - frequency)
    inverse_psd = 8192.0 / jnp.take(psd_row, folded).astype(jnp.float32)
    return (spectra.astype(jnp.float32) * inverse_psd[None, :, None]).astype(jnp.bfloat16)


def settle(partial_value, sum_dim):
    summed = lax.psum_scatter(partial_value, "tm", scatter_dimension=sum_dim, tiled=True)
    return lax.psum(summed, "comp")


def body(orbit_angles, gap_mask, column_index, lat_coeffs, psd_table):
    devices_tm = lax.axis_size("tm")
    epochs = orbit_angles.shape[1]
    block_len = epochs // devices_tm
    samples = epochs * devices_tm
    columns = lat_coeffs.shape[2]
    coeffs = lat_coeffs[0]
    keep_rows = gap_mask.astype(jnp.float32)
    packed = jnp.concatenate([orbit_angles, keep_rows[None]], axis=0)[:, None, :]
    received = lax.all_to_all(packed, "tm", split_axis=2, concat_axis=1, tiled=True)
    flat_orbit = received.reshape(3, devices_tm * block_len)
    spread = synthesize(flat_orbit[0:2], flat_orbit[2], column_index, coeffs).reshape(
        devices_tm, block_len, columns
    )
    position = lax.axis_index("tm")
    local_epoch = position * block_len + jnp.arange(block_len, dtype=jnp.int32)
    cos_outer, sin_outer = dft_tables(devices_tm)
    flat_design = spread.reshape(devices_tm, block_len * columns)
    real_part = precise_dot(cos_outer, flat_design).reshape(devices_tm, block_len, columns)
    imag_part = -precise_dot(sin_outer, flat_design).reshape(devices_tm, block_len, columns)
    real_part, imag_part = rotate(
        real_part, imag_part, jnp.arange(devices_tm, dtype=jnp.int32), local_epoch, samples
    )
    twisted = jnp.stack([real_part, imag_part])
    spec_real, spec_imag = local_transform(
        lax.all_to_all(twisted, "tm", split_axis=1, concat_axis=2, tiled=True), samples
    )
    spectra = jnp.stack([spec_real, spec_imag])
    psd_row = psd_table[0]
    contract = (((0, 1), (0, 1)), ((), ()))
    frequency = position + devices_tm * jnp.arange(epochs, dtype=jnp.int32)
    weighted = noise_weighted(spectra, psd_row, frequency, samples)
    partial_value = lax.dot_general(
        lax.all_gather(spectra, "panel", axis=2, tiled=True),
        weighted,
        contract,
        preferred_element_type=jnp.float32,
    )
    return settle(partial_value, 0)


RADIX = 16
SINE_LON = (6.283164044168851, -41.33714234995496, 81.34076808172247, -70.99342472149007)
SINE_FINE = (
    6.283185160088548,
    -41.3416550311802,
    81.60100405747373,
    -76.54978191007581,
    39.53670300634923,
)
CLASSES = (2, 4, 6, 1, 5, 9, 13)
EVEN = 3
ROUNDER = 1.5 * 2.0**23
MESH = pl.DeviceIdType.MESH


def cos_turns(turns, terms=SINE_FINE):
    offset = turns - ((turns + ROUNDER) - ROUNDER)
    near = 0.25 - jnp.abs(offset)
    square = near * near
    total = terms[-1]
    for term in terms[-2::-1]:
        total = total * square + term
    return total * near


def iota(shape, dim):
    return lax.broadcasted_iota(jnp.int32, shape, dim)


def split(value):
    high = value.astype(jnp.bfloat16)
    return high, (value - high.astype(jnp.float32)).astype(jnp.bfloat16)


def tables(length):
    samples = RADIX * length
    half = length // 2

    def waves(product):
        angle = (product % samples) * (2.0 * np.pi / samples)
        return np.cos(angle), np.sin(angle)

    count = np.arange(length)
    cosine, sine = waves(RADIX * np.outer(count, count))
    zero = np.concatenate([cosine[:, :half], -sine[:, :half]], axis=1)
    zero[:, half] = 1 - 2 * (count % 2)
    eight = np.concatenate(waves(np.outer(count, RADIX // 2 + RADIX * count[:half])), axis=1)
    eight[:, half:] *= -1
    turn = [wave for cls in CLASSES for wave in waves(cls * count)]
    square = np.stack([cosine, sine, zero, eight]) / samples
    return square.astype(np.float32), np.stack(turn).astype(np.float32)


def put_matrix(ref, at, value, lanes):
    high, low = split(value)
    third = ref.shape[0] // 3
    for block, part in ((0, high), (1, high), (2, low)):
        start = block * third + at
        ref[start : start + value.shape[0], lanes] = part


def put_rows(ref, slot, rows, at, value):
    high, low = split(value)
    past = ref.shape[2] // 2 + at
    ref[slot, rows, at : at + value.shape[1]] = high
    ref[slot, rows, past : past + value.shape[1]] = low


def frequency_weights(psd_ref, wts_ref, samples):
    length = samples // RADIX
    half = length // 2
    power = jnp.concatenate([psd_ref[:, half * i : half * (i + 1)] for i in range(RADIX)], axis=0)
    spread = (iota((RADIX, half), 0) == iota((RADIX, half), 1) >> 3).astype(jnp.bfloat16)
    keep = (iota((half, half), 0) >> 4) == (iota((half, half), 1) & (half // RADIX - 1))
    pick_up = ((iota((RADIX, half), 1) & (RADIX - 1)) == iota((RADIX, half), 0)).astype(jnp.bfloat16)
    pick_down = ((iota((RADIX, half), 1) + iota((RADIX, half), 0)) & (RADIX - 1) == 0).astype(
        jnp.bfloat16
    )
    flip = (iota((half, half), 0) + iota((half, half), 1) == half - 1).astype(jnp.bfloat16)
    up = jnp.zeros((RADIX, half), jnp.float32)
    down = jnp.zeros((RADIX, half), jnp.float32)
    for digits, unit in ((power >> 8, 256.0), (power & 255, 1.0)):
        digits = digits.astype(jnp.float32).astype(jnp.bfloat16)
        moved = lax.dot_general(
            digits, spread, (((0,), (0,)), ((), ())), preferred_element_type=jnp.float32
        )
        moved = jnp.where(keep, moved, 0.0).astype(jnp.bfloat16)
        up = up + unit * jnp.dot(pick_up, moved, preferred_element_type=jnp.float32)
        back = jnp.dot(pick_down, moved, preferred_element_type=jnp.float32).astype(jnp.bfloat16)
        down = down + unit * jnp.dot(back, flip, preferred_element_type=jnp.float32)
    up = 2.0 * (8192.0 / up)
    down = 2.0 * (8192.0 / down)
    last = 8192.0 / psd_ref[:, samples // 2 : samples // 2 + 1].astype(jnp.float32)
    first = iota((1, half), 1) == 0
    wts_ref[0:1, 0:half] = jnp.where(first, 0.5 * up[0:1], up[0:1])
    wts_ref[0:1, half:length] = jnp.where(first, last, up[0:1])
    wts_ref[1:2, 0:half] = up[RADIX // 2 : RADIX // 2 + 1]
    wts_ref[1:2, half:length] = up[RADIX // 2 : RADIX // 2 + 1]
    for slot, cls in enumerate(CLASSES):
        for at in (0, length):
            wts_ref[slot + 2 : slot + 3, at : at + half] = up[cls : cls + 1]
            wts_ref[slot + 2 : slot + 3, at + half : at + length] = down[cls : cls + 1]


def even_classes(d):
    r = math.sqrt(0.5)
    even, alt = [], []
    for q in range(4):
        first, second = d(q) + d(q + 8), d(q + 4) + d(q + 12)
        even.append(first + second)
        alt.append(first - second)
    e02, e13 = even[0] + even[2], even[1] + even[3]
    four = (even[0] - even[2], even[3] - even[1])
    p, q = r * (alt[1] - alt[3]), r * (alt[1] + alt[3])
    two = (alt[0] + p, -(alt[2] + q))
    six = (alt[0] - p, alt[2] - q)
    return (e02 + e13, e02 - e13), (two, four, six)


def odd_classes(d):
    br, bi = [], []
    for q in range(4):
        real, imag = d(q) - d(q + 8), d(q + 12) - d(q + 4)
        c, s = math.cos(math.pi * q / 8), math.sin(math.pi * q / 8)
        if q == 2:
            real, imag = c * (real + imag), c * (imag - real)
        elif q:
            real, imag = c * real + s * imag, c * imag - s * real
        br.append(real)
        bi.append(imag)
    sr, si = br[0] + br[2], bi[0] + bi[2]
    tr, ti = br[1] + br[3], bi[1] + bi[3]
    ur, ui = br[0] - br[2], bi[0] - bi[2]
    vr, vi = br[1] - br[3], bi[1] - bi[3]
    return (sr + tr, si + ti), (ur + vi, ui - vr), (sr - tr, si - ti), (ur - vi, ui + vr)


def kernel(
    devices_tm,
    angles_hbm,
    mask_hbm,
    columns_hbm,
    coeffs_hbm,
    psd_hbm,
    square_hbm,
    twiddle_hbm,
    own_ref,
    other_ref,
    columns_ref,
    coeffs_ref,
    psd_ref,
    orbit,
    flags,
    far_coeffs,
    far_columns,
    coeffs_t,
    column_t,
    basis_a,
    basis_b,
    design,
    real,
    pair_even,
    pair_odd,
    spectra_even,
    mat_real,
    mat,
    square,
    twiddle,
    wts,
    total,
    send_sem,
    recv_sem,
    side_send,
    side_recv,
    load_sem,
):
    block = angles_hbm.shape[1]
    samples = block * devices_tm
    length = samples // RADIX
    half = length // 2
    terms = coeffs_ref.shape[1]
    terms_lat = terms // 2
    columns = coeffs_ref.shape[2]
    rows = own_ref.shape[0]
    everyone = rows + columns
    me = lax.axis_index("tm")
    panel = lax.axis_index("panel")
    comp = lax.axis_index("comp")

    barrier = pltpu.get_barrier_semaphore()
    peers = [lax.rem(me + k, devices_tm) for k in range(1, devices_tm)]
    for peer in peers:
        pl.semaphore_signal(barrier, inc=1, device_id={"tm": peer}, device_id_type=MESH)
    pl.semaphore_signal(barrier, inc=1, device_id={"panel": 1 - panel}, device_id_type=MESH)
    pl.semaphore_signal(barrier, inc=1, device_id={"comp": 1 - comp}, device_id_type=MESH)

    loads = [
        pltpu.make_async_copy(source, held, load_sem.at[i])
        for i, (source, held) in enumerate(
            (
                (angles_hbm, orbit.at[me]),
                (mask_hbm, flags.at[me]),
                (columns_hbm, columns_ref),
                (coeffs_hbm, coeffs_ref),
                (psd_hbm, psd_ref),
                (twiddle_hbm, twiddle),
                (square_hbm, square),
            )
        )
    ]
    for load in loads:
        load.start()
    pl.semaphore_wait(barrier, devices_tm + 1)

    def send_orbit(k, slot, peer):
        return [
            pltpu.make_async_remote_copy(
                src_ref=source,
                dst_ref=held.at[slot],
                send_sem=send_sem.at[i, k],
                recv_sem=recv_sem.at[i, slot],
                device_id={"tm": peer},
                device_id_type=MESH,
            )
            for i, (source, held) in enumerate(((angles_hbm, orbit), (mask_hbm, flags)))
        ]

    for k, peer in enumerate(peers):
        for copy in send_orbit(k, me, peer):
            copy.start()
    first_row = me * rows
    lanes = pl.ds(pl.multiple_of(lax.rem(first_row, columns), rows), rows)
    send_coeffs = pltpu.make_async_remote_copy(
        src_ref=coeffs_hbm.at[0, :, lanes],
        dst_ref=far_coeffs,
        send_sem=side_send.at[0],
        recv_sem=side_recv.at[0],
        device_id={"panel": 1 - panel},
        device_id_type=MESH,
    )
    send_columns = pltpu.make_async_remote_copy(
        src_ref=columns_hbm.at[:, lanes],
        dst_ref=far_columns,
        send_sem=side_send.at[1],
        recv_sem=side_recv.at[1],
        device_id={"panel": 1 - panel},
        device_id_type=MESH,
    )
    send_coeffs.start()
    send_columns.start()

    loads[6].wait()
    left, right = slice(0, length), slice(length, 2 * length)
    put_matrix(mat, 0, square[0], left)
    put_matrix(mat, 0, -square[1], right)
    put_matrix(mat, length, square[1], left)
    put_matrix(mat, length, square[0], right)
    put_matrix(mat_real.at[0], 0, square[2], left)
    put_matrix(mat_real.at[1], 0, square[3], left)
    loads[4].wait()

    def place(at, coeffs, index_rows):
        width = coeffs.shape[1]
        level = iota((terms, width), 0)
        level = jnp.where(level < terms_lat, level, level - terms_lat)
        masked = jnp.where(level <= index_rows[0:1, :], coeffs, 0.0)
        coeffs_t[at : at + width, :] = jnp.transpose(masked).astype(jnp.bfloat16)
        orders = index_rows[1:2, :]
        shift = jnp.where(orders >= 0, 0.0, 0.25)
        norm = 1.0 / jnp.sqrt(index_rows[0:1, :].astype(jnp.float32) + 1.0)
        packed = jnp.concatenate(
            [jnp.abs(orders).astype(jnp.float32), shift]
            + [norm * term for term in SINE_LON]
            + [jnp.zeros((2, width), jnp.float32)],
            axis=0,
        )
        turned = jnp.transpose(packed)
        for i in range(2 + len(SINE_LON)):
            column_t[i, at : at + width, :] = jnp.broadcast_to(turned[:, i : i + 1], (width, 128))

    loads[2].wait()
    loads[3].wait()
    place(0, coeffs_ref[0].astype(jnp.float32), columns_ref[...])
    send_coeffs.wait()
    send_columns.wait()
    mine = first_row // columns == panel
    near = coeffs_ref[0, :, lanes].astype(jnp.float32)
    place(
        columns,
        jnp.where(mine, near, far_coeffs[...].astype(jnp.float32)),
        jnp.where(mine, columns_ref[:, lanes], far_columns[...]),
    )
    loads[0].wait()
    loads[1].wait()
    for k, peer in enumerate(peers):
        for copy in send_orbit(k, me, peer):
            copy.wait_send()
        for copy in send_orbit(k, peer, peer):
            copy.wait_recv()

    per_device = block // length

    def epoch_lanes(chunk):
        at = lax.rem(chunk, per_device) * length
        return chunk // per_device, pl.ds(pl.multiple_of(at, length), length)

    def fill_basis(chunk, basis):
        holder, lanes = epoch_lanes(chunk)
        theta = orbit[holder, 0:1, lanes] * (0.5 / math.pi)
        keep = flags[holder, :, lanes].astype(jnp.float32)
        turns = iota((16, length), 0).astype(jnp.float32) * theta
        cosine, sine = cos_turns(turns) * keep, cos_turns(turns - 0.25) * keep
        step_c, step_s = cos_turns(16.0 * theta), cos_turns(16.0 * theta - 0.25)
        for at in range(0, terms_lat, 16):
            basis[at : at + 16, :] = cosine.astype(jnp.bfloat16)
            basis[terms_lat + at : terms_lat + at + 16, :] = sine.astype(jnp.bfloat16)
            cosine, sine = cosine * step_c - sine * step_s, sine * step_c + cosine * step_s

    def fill_design(chunk, basis):
        holder, lanes = epoch_lanes(chunk)
        longit = orbit[holder, 1:2, lanes] * (0.5 / math.pi)
        latitude = jnp.dot(coeffs_t[...], basis[...], preferred_element_type=jnp.float32)
        terms_lon = [column_t[2 + i] for i in range(len(SINE_LON))]
        for lane in range(0, length, 128):
            where = slice(lane, lane + 128)
            wave = cos_turns(column_t[0] * longit[:, where] - column_t[1], terms_lon)
            design[chunk, :, where] = latitude[:, where] * wave

    fill_basis(0, basis_a)

    def two_chunks(i, carry):
        fill_basis(2 * i + 1, basis_b)
        fill_design(2 * i, basis_a)
        fill_basis(lax.rem(2 * i + 2, RADIX), basis_a)
        fill_design(2 * i + 1, basis_b)
        return carry

    lax.fori_loop(0, RADIX // 2, two_chunks, 0)

    def turn(slot, pair, at, lane, value):
        re, im = value
        c = twiddle[2 * slot : 2 * slot + 1, lane : lane + 128]
        s = twiddle[2 * slot + 1 : 2 * slot + 2, lane : lane + 128]
        place_at = slot if slot < EVEN else slot - EVEN
        put_rows(pair, place_at, at, lane, re * c + im * s)
        put_rows(pair, place_at, at, length + lane, im * c - re * s)

    def fold_even(i, carry):
        at = pl.ds(pl.multiple_of(i * 16, 16), 16)
        for lane in range(0, length, 128):
            plain, pairs = even_classes(lambda q: design[q, at, lane : lane + 128])
            for slot, value in enumerate(plain):
                put_rows(real, slot, at, lane, value)
            for slot, value in enumerate(pairs):
                turn(slot, pair_even, at, lane, value)
        return carry

    def fold_odd(i):
        at = pl.ds(pl.multiple_of(i * 16, 16), 16)
        for lane in range(0, length, 128):
            for slot, value in enumerate(odd_classes(lambda q: design[q, at, lane : lane + 128])):
                turn(EVEN + slot, pair_odd, at, lane, value)

    loads[5].wait()
    lax.fori_loop(0, everyone // 16, fold_even, 0)

    def spectra_of(parts, matrix):
        high = parts[:, : parts.shape[1] // 2]
        return jnp.dot(
            jnp.concatenate([parts, high], axis=1), matrix, preferred_element_type=jnp.float32
        ).astype(jnp.bfloat16)

    def gram(spectra, weight):
        weighted = (spectra[:columns].astype(jnp.float32) * weight).astype(jnp.bfloat16)
        return lax.dot_general(
            spectra[columns:], weighted, (((1,), (1,)), ((), ())), preferred_element_type=jnp.float32
        )

    units = everyone // 16 // EVEN

    def even_step(slot, carry):
        spectra_even[slot] = spectra_of(pair_even[slot], mat[...])
        for unit in range(units):
            fold_odd(slot * units + unit)
        return carry

    lax.fori_loop(0, EVEN, even_step, 0)
    frequency_weights(psd_ref, wts, samples)
    summed = jnp.zeros((rows, columns), jnp.float32)
    for slot in range(len(CLASSES) - EVEN):
        spectra = spectra_of(pair_odd[slot], mat[...])
        summed = summed + gram(spectra, wts[slot + 2 + EVEN : slot + 3 + EVEN, :])
    for slot in range(2):
        spectra = spectra_of(real[slot], mat_real[slot])
        summed = summed + gram(spectra, wts[slot : slot + 1, 0:length])
    for slot in range(EVEN):
        summed = summed + gram(spectra_even[slot], wts[slot + 2 : slot + 3, :])
    total[...] = summed
    swap = pltpu.make_async_remote_copy(
        src_ref=total,
        dst_ref=other_ref,
        send_sem=side_send.at[2],
        recv_sem=side_recv.at[2],
        device_id={"comp": 1 - comp},
        device_id_type=MESH,
    )
    swap.start()
    own_ref[...] = total[...]
    swap.wait()


def fused(orbit_angles, gap_mask, column_index, lat_coeffs, psd_table):
    devices_tm = lax.axis_size("tm")
    block = orbit_angles.shape[1]
    samples = devices_tm * block
    length = samples // RADIX
    terms, columns = lat_coeffs.shape[1:]
    rows = columns * lax.axis_size("panel") // devices_tm
    everyone = rows + columns
    f32, bf16 = jnp.float32, jnp.bfloat16
    vmem = pl.BlockSpec(memory_space=pltpu.VMEM)
    count = len(CLASSES)
    own, other = pl.pallas_call(
        functools.partial(kernel, devices_tm),
        out_shape=[jax.ShapeDtypeStruct((rows, columns), f32)] * 2,
        in_specs=[pl.BlockSpec(memory_space=pltpu.HBM)] * 7,
        out_specs=[vmem] * 2,
        scratch_shapes=[
            pltpu.VMEM(column_index.shape, jnp.int32),
            pltpu.VMEM(lat_coeffs.shape, bf16),
            pltpu.VMEM(psd_table.shape, jnp.int32),
            pltpu.VMEM((devices_tm, 2, block), f32),
            pltpu.VMEM((devices_tm, 1, block), jnp.int32),
            pltpu.VMEM((terms, rows), bf16),
            pltpu.VMEM((2, rows), jnp.int32),
            pltpu.VMEM((everyone, terms), bf16),
            pltpu.VMEM((2 + len(SINE_LON), everyone, 128), f32),
            pltpu.VMEM((terms, length), bf16),
            pltpu.VMEM((terms, length), bf16),
            pltpu.VMEM((RADIX, everyone, length), f32),
            pltpu.VMEM((2, everyone, 2 * length), bf16),
            pltpu.VMEM((EVEN, everyone, 4 * length), bf16),
            pltpu.VMEM((count - EVEN, everyone, 4 * length), bf16),
            pltpu.VMEM((EVEN, everyone, 2 * length), bf16),
            pltpu.VMEM((2, 3 * length, length), bf16),
            pltpu.VMEM((6 * length, 2 * length), bf16),
            pltpu.VMEM((4, length, length), f32),
            pltpu.VMEM((2 * count, length), f32),
            pltpu.VMEM((16, 2 * length), f32),
            pltpu.VMEM((rows, columns), f32),
            pltpu.SemaphoreType.DMA((2, devices_tm)),
            pltpu.SemaphoreType.DMA((2, devices_tm)),
            pltpu.SemaphoreType.DMA((3,)),
            pltpu.SemaphoreType.DMA((3,)),
            pltpu.SemaphoreType.DMA((7,)),
        ],
        compiler_params=pltpu.CompilerParams(
            collective_id=0, has_side_effects=True, vmem_limit_bytes=63 * 1024 * 1024
        ),
    )(orbit_angles, gap_mask.reshape(1, block), column_index, lat_coeffs, psd_table, *tables(length))
    return own + other


def choose(orbit_angles, gap_mask, column_index, lat_coeffs, psd_table):
    devices_tm, panels = lax.axis_size("tm"), lax.axis_size("panel")
    samples = devices_tm * orbit_angles.shape[1]
    columns = lat_coeffs.shape[2]
    rows = columns * panels // devices_tm
    fits = (
        samples == 4096
        and orbit_angles.shape[1] % 256 == 0
        and panels == 2
        and lax.axis_size("comp") == 2
        and rows % 128 == 0
        and columns % rows == 0
        and lat_coeffs.shape[1] % 32 == 0
        and (rows + columns) * lat_coeffs.shape[1] <= 512 * 1024
    )
    step = fused if fits else body
    return step(orbit_angles, gap_mask, column_index, lat_coeffs, psd_table)


def solution(mesh):
    return jax.shard_map(
        choose,
        mesh=mesh,
        in_specs=(
            P(None, ("groups", "tm")),
            P(("groups", "tm")),
            P(None, "panel"),
            P("comp", None, "panel"),
            P("comp", None),
        ),
        out_specs=P(("groups", "tm"), "panel"),
        check_vma=False,
    )
```

```python
import functools
import math

import jax
import jax.numpy as jnp
import numpy as np
from jax import lax
from jax.experimental import pallas as pl
from jax.experimental.pallas import tpu as pltpu
from jax.sharding import PartitionSpec as P

SPLIT = 64


def synthesize(angles, keep_rows, column_index, coeffs):
    terms_lat = coeffs.shape[0] // 2
    colatitude = angles[0]
    longit = angles[1]
    wavenumbers = jnp.arange(terms_lat, dtype=jnp.float32)
    phases = colatitude[:, None] * wavenumbers[None, :]
    basis_rows = jnp.concatenate([jnp.cos(phases), jnp.sin(phases)], axis=1).astype(jnp.bfloat16)
    degree = column_index[0]
    orders = column_index[1]
    levels = jnp.arange(2 * terms_lat, dtype=jnp.int32) % terms_lat
    allowed = levels[:, None] <= degree[None, :]
    masked = jnp.where(allowed, coeffs, jnp.zeros_like(coeffs))
    latitude = jnp.dot(basis_rows, masked, preferred_element_type=jnp.float32)
    lon_phase = longit[:, None] * jnp.abs(orders).astype(jnp.float32)[None, :]
    lon_wave = jnp.where(orders[None, :] >= 0, jnp.cos(lon_phase), jnp.sin(lon_phase))
    norm_scale = 1.0 / jnp.sqrt(degree.astype(jnp.float32) + 1.0)
    return latitude * lon_wave * (keep_rows[:, None] * norm_scale[None, :])


def phase_tables(row_index, col_index, length):
    product = row_index[:, None] * col_index[None, :] % length
    angle_grid = product.astype(jnp.float32) * (2.0 * math.pi / length)
    return (jnp.cos(angle_grid), jnp.sin(angle_grid))


def dft_tables(length):
    indices = jnp.arange(length, dtype=jnp.int32)
    return phase_tables(indices, indices, length)


def rotate(real_part, imag_part, outer_index, inner_index, length):
    index_grid = outer_index[:, None] * inner_index[None, :] % length
    angle_grid = index_grid.astype(jnp.float32) * (2.0 * math.pi / length)
    cosine = jnp.cos(angle_grid)[:, :, None]
    sine_grid = jnp.sin(angle_grid)[:, :, None]
    return (real_part * cosine + imag_part * sine_grid, imag_part * cosine - real_part * sine_grid)


def precise_dot(left_side, right_side):
    return jnp.dot(
        left_side, right_side, precision=lax.Precision.HIGHEST, preferred_element_type=jnp.float32
    )


def transform(cos_table, sin_table, real_part, imag_part):
    new_real = precise_dot(cos_table, real_part) + precise_dot(sin_table, imag_part)
    new_imag = precise_dot(cos_table, imag_part) - precise_dot(sin_table, real_part)
    return (new_real, new_imag)


def four_step(real_in, imag_in, samples):
    length = real_in.shape[0]
    columns = real_in.shape[1]
    outer_count = SPLIT
    inner_count = length // SPLIT
    real_part = real_in.reshape(outer_count, inner_count * columns)
    imag_part = imag_in.reshape(outer_count, inner_count * columns)
    cos_outer, sin_outer = dft_tables(outer_count)
    real_part, imag_part = transform(cos_outer, sin_outer, real_part, imag_part)
    real_part = real_part.reshape(outer_count, inner_count, columns)
    imag_part = imag_part.reshape(outer_count, inner_count, columns)
    real_part, imag_part = rotate(
        real_part,
        imag_part,
        jnp.arange(outer_count, dtype=jnp.int32),
        jnp.arange(inner_count, dtype=jnp.int32),
        length,
    )
    real_part = jnp.transpose(real_part, (1, 0, 2)).reshape(inner_count, outer_count * columns)
    imag_part = jnp.transpose(imag_part, (1, 0, 2)).reshape(inner_count, outer_count * columns)
    cos_inner, sin_inner = dft_tables(inner_count)
    real_part, imag_part = transform(cos_inner, sin_inner, real_part, imag_part)
    return (
        real_part.reshape(length, columns) / samples,
        imag_part.reshape(length, columns) / samples,
    )


def local_transform(received, samples):
    real_part, imag_part = four_step(received[0, 0], received[1, 0], samples)
    return (real_part.astype(jnp.bfloat16), imag_part.astype(jnp.bfloat16))


def noise_weighted(spectra, psd_row, frequency, samples):
    folded = jnp.minimum(frequency, samples - frequency)
    inverse_psd = 8192.0 / jnp.take(psd_row, folded).astype(jnp.float32)
    return (spectra.astype(jnp.float32) * inverse_psd[None, :, None]).astype(jnp.bfloat16)


def settle(partial_value, sum_dim):
    summed = lax.psum_scatter(partial_value, "tm", scatter_dimension=sum_dim, tiled=True)
    return lax.psum(summed, "comp")


def body(orbit_angles, gap_mask, column_index, lat_coeffs, psd_table):
    devices_tm = lax.axis_size("tm")
    epochs = orbit_angles.shape[1]
    block_len = epochs // devices_tm
    samples = epochs * devices_tm
    columns = lat_coeffs.shape[2]
    coeffs = lat_coeffs[0]
    keep_rows = gap_mask.astype(jnp.float32)
    packed = jnp.concatenate([orbit_angles, keep_rows[None]], axis=0)[:, None, :]
    received = lax.all_to_all(packed, "tm", split_axis=2, concat_axis=1, tiled=True)
    flat_orbit = received.reshape(3, devices_tm * block_len)
    spread = synthesize(flat_orbit[0:2], flat_orbit[2], column_index, coeffs).reshape(
        devices_tm, block_len, columns
    )
    position = lax.axis_index("tm")
    local_epoch = position * block_len + jnp.arange(block_len, dtype=jnp.int32)
    cos_outer, sin_outer = dft_tables(devices_tm)
    flat_design = spread.reshape(devices_tm, block_len * columns)
    real_part = precise_dot(cos_outer, flat_design).reshape(devices_tm, block_len, columns)
    imag_part = -precise_dot(sin_outer, flat_design).reshape(devices_tm, block_len, columns)
    real_part, imag_part = rotate(
        real_part, imag_part, jnp.arange(devices_tm, dtype=jnp.int32), local_epoch, samples
    )
    twisted = jnp.stack([real_part, imag_part])
    spec_real, spec_imag = local_transform(
        lax.all_to_all(twisted, "tm", split_axis=1, concat_axis=2, tiled=True), samples
    )
    spectra = jnp.stack([spec_real, spec_imag])
    psd_row = psd_table[0]
    contract = (((0, 1), (0, 1)), ((), ()))
    frequency = position + devices_tm * jnp.arange(epochs, dtype=jnp.int32)
    weighted = noise_weighted(spectra, psd_row, frequency, samples)
    partial_value = lax.dot_general(
        lax.all_gather(spectra, "panel", axis=2, tiled=True),
        weighted,
        contract,
        preferred_element_type=jnp.float32,
    )
    return settle(partial_value, 0)


RADIX = 16
SINE_LON = (6.283164044168851, -41.33714234995496, 81.34076808172247, -70.99342472149007)
SINE_FINE = (
    6.283185160088548,
    -41.3416550311802,
    81.60100405747373,
    -76.54978191007581,
    39.53670300634923,
)
CLASSES = (2, 4, 6, 1, 5, 9, 13)
EVEN = 3
ROUNDER = 1.5 * 2.0**23
MESH = pl.DeviceIdType.MESH


def cos_turns(turns, terms=SINE_FINE):
    offset = turns - ((turns + ROUNDER) - ROUNDER)
    near = 0.25 - jnp.abs(offset)
    square = near * near
    total = terms[-1]
    for term in terms[-2::-1]:
        total = total * square + term
    return total * near


def iota(shape, dim):
    return lax.broadcasted_iota(jnp.int32, shape, dim)


def split(value):
    high = value.astype(jnp.bfloat16)
    return high, (value - high.astype(jnp.float32)).astype(jnp.bfloat16)


def tables(length):
    samples = RADIX * length
    half = length // 2

    def waves(product):
        angle = (product % samples) * (2.0 * np.pi / samples)
        return np.cos(angle), np.sin(angle)

    count = np.arange(length)
    cosine, sine = waves(RADIX * np.outer(count, count))
    zero = np.concatenate([cosine[:, :half], -sine[:, :half]], axis=1)
    zero[:, half] = 1 - 2 * (count % 2)
    eight = np.concatenate(waves(np.outer(count, RADIX // 2 + RADIX * count[:half])), axis=1)
    eight[:, half:] *= -1
    turn = [wave for cls in CLASSES for wave in waves(cls * count)]
    square = np.stack([cosine, sine, zero, eight]) / samples
    return square.astype(np.float32), np.stack(turn).astype(np.float32)


def put_matrix(ref, at, value, lanes):
    high, low = split(value)
    third = ref.shape[0] // 3
    for block, part in ((0, high), (1, high), (2, low)):
        start = block * third + at
        ref[start : start + value.shape[0], lanes] = part


def put_rows(ref, slot, rows, at, value):
    high, low = split(value)
    past = ref.shape[2] // 2 + at
    ref[slot, rows, at : at + value.shape[1]] = high
    ref[slot, rows, past : past + value.shape[1]] = low


def frequency_weights(psd_ref, wts_ref, samples):
    length = samples // RADIX
    half = length // 2
    power = jnp.concatenate([psd_ref[:, half * i : half * (i + 1)] for i in range(RADIX)], axis=0)
    spread = (iota((RADIX, half), 0) == iota((RADIX, half), 1) >> 3).astype(jnp.bfloat16)
    keep = (iota((half, half), 0) >> 4) == (iota((half, half), 1) & (half // RADIX - 1))
    pick_up = ((iota((RADIX, half), 1) & (RADIX - 1)) == iota((RADIX, half), 0)).astype(jnp.bfloat16)
    pick_down = ((iota((RADIX, half), 1) + iota((RADIX, half), 0)) & (RADIX - 1) == 0).astype(
        jnp.bfloat16
    )
    flip = (iota((half, half), 0) + iota((half, half), 1) == half - 1).astype(jnp.bfloat16)
    up = jnp.zeros((RADIX, half), jnp.float32)
    down = jnp.zeros((RADIX, half), jnp.float32)
    for digits, unit in ((power >> 8, 256.0), (power & 255, 1.0)):
        digits = digits.astype(jnp.float32).astype(jnp.bfloat16)
        moved = lax.dot_general(
            digits, spread, (((0,), (0,)), ((), ())), preferred_element_type=jnp.float32
        )
        moved = jnp.where(keep, moved, 0.0).astype(jnp.bfloat16)
        up = up + unit * jnp.dot(pick_up, moved, preferred_element_type=jnp.float32)
        back = jnp.dot(pick_down, moved, preferred_element_type=jnp.float32).astype(jnp.bfloat16)
        down = down + unit * jnp.dot(back, flip, preferred_element_type=jnp.float32)
    up = 2.0 * (8192.0 / up)
    down = 2.0 * (8192.0 / down)
    last = 8192.0 / psd_ref[:, samples // 2 : samples // 2 + 1].astype(jnp.float32)
    first = iota((1, half), 1) == 0
    wts_ref[0:1, 0:half] = jnp.where(first, 0.5 * up[0:1], up[0:1])
    wts_ref[0:1, half:length] = jnp.where(first, last, up[0:1])
    wts_ref[1:2, 0:half] = up[RADIX // 2 : RADIX // 2 + 1]
    wts_ref[1:2, half:length] = up[RADIX // 2 : RADIX // 2 + 1]
    for slot, cls in enumerate(CLASSES):
        for at in (0, length):
            wts_ref[slot + 2 : slot + 3, at : at + half] = up[cls : cls + 1]
            wts_ref[slot + 2 : slot + 3, at + half : at + length] = down[cls : cls + 1]


def even_classes(d):
    r = math.sqrt(0.5)
    even, alt = [], []
    for q in range(4):
        first, second = d(q) + d(q + 8), d(q + 4) + d(q + 12)
        even.append(first + second)
        alt.append(first - second)
    e02, e13 = even[0] + even[2], even[1] + even[3]
    four = (even[0] - even[2], even[3] - even[1])
    p, q = r * (alt[1] - alt[3]), r * (alt[1] + alt[3])
    two = (alt[0] + p, -(alt[2] + q))
    six = (alt[0] - p, alt[2] - q)
    return (e02 + e13, e02 - e13), (two, four, six)


def odd_classes(d):
    br, bi = [], []
    for q in range(4):
        real, imag = d(q) - d(q + 8), d(q + 12) - d(q + 4)
        c, s = math.cos(math.pi * q / 8), math.sin(math.pi * q / 8)
        if q == 2:
            real, imag = c * (real + imag), c * (imag - real)
        elif q:
            real, imag = c * real + s * imag, c * imag - s * real
        br.append(real)
        bi.append(imag)
    sr, si = br[0] + br[2], bi[0] + bi[2]
    tr, ti = br[1] + br[3], bi[1] + bi[3]
    ur, ui = br[0] - br[2], bi[0] - bi[2]
    vr, vi = br[1] - br[3], bi[1] - bi[3]
    return (sr + tr, si + ti), (ur + vi, ui - vr), (sr - tr, si - ti), (ur - vi, ui + vr)


def kernel(
    devices_tm,
    angles_hbm,
    mask_hbm,
    columns_hbm,
    coeffs_hbm,
    psd_hbm,
    square_hbm,
    twiddle_hbm,
    own_ref,
    other_ref,
    columns_ref,
    coeffs_ref,
    psd_ref,
    orbit,
    flags,
    far_coeffs,
    far_columns,
    coeffs_t,
    column_t,
    basis_a,
    basis_b,
    design,
    real,
    pair_even,
    pair_odd,
    spectra_even,
    mat_real,
    mat,
    square,
    twiddle,
    wts,
    total,
    send_sem,
    recv_sem,
    side_send,
    side_recv,
    load_sem,
):
    block = angles_hbm.shape[1]
    samples = block * devices_tm
    length = samples // RADIX
    half = length // 2
    terms = coeffs_ref.shape[1]
    terms_lat = terms // 2
    columns = coeffs_ref.shape[2]
    rows = own_ref.shape[0]
    everyone = rows + columns
    me = lax.axis_index("tm")
    panel = lax.axis_index("panel")
    comp = lax.axis_index("comp")

    barrier = pltpu.get_barrier_semaphore()
    peers = [lax.rem(me + k, devices_tm) for k in range(1, devices_tm)]
    for peer in peers:
        pl.semaphore_signal(barrier, inc=1, device_id={"tm": peer}, device_id_type=MESH)
    pl.semaphore_signal(barrier, inc=1, device_id={"panel": 1 - panel}, device_id_type=MESH)
    pl.semaphore_signal(barrier, inc=1, device_id={"comp": 1 - comp}, device_id_type=MESH)

    loads = [
        pltpu.make_async_copy(source, held, load_sem.at[i])
        for i, (source, held) in enumerate(
            (
                (angles_hbm, orbit.at[me]),
                (mask_hbm, flags.at[me]),
                (columns_hbm, columns_ref),
                (coeffs_hbm, coeffs_ref),
                (psd_hbm, psd_ref),
                (twiddle_hbm, twiddle),
                (square_hbm, square),
            )
        )
    ]
    for load in loads:
        load.start()
    pl.semaphore_wait(barrier, devices_tm + 1)

    def send_orbit(k, slot, peer):
        return [
            pltpu.make_async_remote_copy(
                src_ref=source,
                dst_ref=held.at[slot],
                send_sem=send_sem.at[i, k],
                recv_sem=recv_sem.at[i, slot],
                device_id={"tm": peer},
                device_id_type=MESH,
            )
            for i, (source, held) in enumerate(((angles_hbm, orbit), (mask_hbm, flags)))
        ]

    for k, peer in enumerate(peers):
        for copy in send_orbit(k, me, peer):
            copy.start()
    first_row = me * rows
    lanes = pl.ds(pl.multiple_of(lax.rem(first_row, columns), rows), rows)
    send_coeffs = pltpu.make_async_remote_copy(
        src_ref=coeffs_hbm.at[0, :, lanes],
        dst_ref=far_coeffs,
        send_sem=side_send.at[0],
        recv_sem=side_recv.at[0],
        device_id={"panel": 1 - panel},
        device_id_type=MESH,
    )
    send_columns = pltpu.make_async_remote_copy(
        src_ref=columns_hbm.at[:, lanes],
        dst_ref=far_columns,
        send_sem=side_send.at[1],
        recv_sem=side_recv.at[1],
        device_id={"panel": 1 - panel},
        device_id_type=MESH,
    )
    send_coeffs.start()
    send_columns.start()

    loads[6].wait()
    left, right = slice(0, length), slice(length, 2 * length)
    put_matrix(mat, 0, square[0], left)
    put_matrix(mat, 0, -square[1], right)
    put_matrix(mat, length, square[1], left)
    put_matrix(mat, length, square[0], right)
    put_matrix(mat_real.at[0], 0, square[2], left)
    put_matrix(mat_real.at[1], 0, square[3], left)
    loads[4].wait()

    def place(at, coeffs, index_rows):
        width = coeffs.shape[1]
        level = iota((terms, width), 0)
        level = jnp.where(level < terms_lat, level, level - terms_lat)
        masked = jnp.where(level <= index_rows[0:1, :], coeffs, 0.0)
        coeffs_t[at : at + width, :] = jnp.transpose(masked).astype(jnp.bfloat16)
        orders = index_rows[1:2, :]
        shift = jnp.where(orders >= 0, 0.0, 0.25)
        norm = 1.0 / jnp.sqrt(index_rows[0:1, :].astype(jnp.float32) + 1.0)
        packed = jnp.concatenate(
            [jnp.abs(orders).astype(jnp.float32), shift]
            + [norm * term for term in SINE_LON]
            + [jnp.zeros((2, width), jnp.float32)],
            axis=0,
        )
        turned = jnp.transpose(packed)
        for i in range(2 + len(SINE_LON)):
            column_t[i, at : at + width, :] = jnp.broadcast_to(turned[:, i : i + 1], (width, 128))

    loads[2].wait()
    loads[3].wait()
    place(0, coeffs_ref[0].astype(jnp.float32), columns_ref[...])
    loads[0].wait()
    loads[1].wait()
    per_device = block // length

    def epoch_lanes(chunk):
        at = lax.rem(chunk, per_device) * length
        return chunk // per_device, pl.ds(pl.multiple_of(at, length), length)

    def fill_basis(chunk, basis, slot):
        holder, lanes = epoch_lanes(chunk)
        theta = orbit[holder, 0:1, lanes] * (0.5 / math.pi)
        keep = flags[holder, :, lanes].astype(jnp.float32)
        turns = iota((16, length), 0).astype(jnp.float32) * theta
        cosine, sine = cos_turns(turns) * keep, cos_turns(turns - 0.25) * keep
        step_c, step_s = cos_turns(16.0 * theta), cos_turns(16.0 * theta - 0.25)
        for at in range(0, terms_lat, 16):
            basis[slot, at : at + 16, :] = cosine.astype(jnp.bfloat16)
            basis[slot, terms_lat + at : terms_lat + at + 16, :] = sine.astype(jnp.bfloat16)
            cosine, sine = cosine * step_c - sine * step_s, sine * step_c + cosine * step_s

    def fill_design(chunk, basis, slot, at, width):
        holder, lanes = epoch_lanes(chunk)
        longit = orbit[holder, 1:2, lanes] * (0.5 / math.pi)
        these = slice(at, at + width)
        latitude = jnp.dot(coeffs_t[these, :], basis[slot], preferred_element_type=jnp.float32)
        terms_lon = [column_t[2 + i, these, :] for i in range(len(SINE_LON))]
        for lane in range(0, length, 128):
            where = slice(lane, lane + 128)
            wave = cos_turns(
                column_t[0, these, :] * longit[:, where] - column_t[1, these, :], terms_lon
            )
            design[chunk, these, where] = latitude[:, where] * wave

    own_chunks = me * per_device

    def near_columns(first, last):
        def two_chunks(i, carry):
            chunk = lax.rem(own_chunks + 2 * i, RADIX)
            again = jnp.where(i + 1 < last, i + 1, first)
            fill_basis(chunk + 1, basis_b, i)
            fill_design(chunk, basis_a, i, 0, columns)
            fill_basis(lax.rem(own_chunks + 2 * again, RADIX), basis_a, again)
            fill_design(chunk + 1, basis_b, i, 0, columns)
            return carry

        fill_basis(lax.rem(own_chunks + 2 * first, RADIX), basis_a, first)
        lax.fori_loop(first, last, two_chunks, 0)

    near_columns(0, per_device // 2)
    for k, peer in enumerate(peers):
        for copy in send_orbit(k, me, peer):
            copy.wait_send()
        for copy in send_orbit(k, peer, peer):
            copy.wait_recv()

    near_columns(per_device // 2, RADIX // 2)
    send_coeffs.wait()
    send_columns.wait()
    mine = first_row // columns == panel
    near = coeffs_ref[0, :, lanes].astype(jnp.float32)
    place(
        columns,
        jnp.where(mine, near, far_coeffs[...].astype(jnp.float32)),
        jnp.where(mine, columns_ref[:, lanes], far_columns[...]),
    )

    def far_rows(i, carry):
        chunk = lax.rem(own_chunks + 2 * i, RADIX)
        fill_design(chunk, basis_a, i, columns, rows)
        fill_design(chunk + 1, basis_b, i, columns, rows)
        return carry

    lax.fori_loop(0, RADIX // 2, far_rows, 0)

    def turn(slot, pair, at, lane, value):
        re, im = value
        c = twiddle[2 * slot : 2 * slot + 1, lane : lane + 128]
        s = twiddle[2 * slot + 1 : 2 * slot + 2, lane : lane + 128]
        place_at = slot if slot < EVEN else slot - EVEN
        put_rows(pair, place_at, at, lane, re * c + im * s)
        put_rows(pair, place_at, at, length + lane, im * c - re * s)

    def fold_even(i, carry):
        at = pl.ds(pl.multiple_of(i * 16, 16), 16)
        for lane in range(0, length, 128):
            plain, pairs = even_classes(lambda q: design[q, at, lane : lane + 128])
            for slot, value in enumerate(plain):
                put_rows(real, slot, at, lane, value)
            for slot, value in enumerate(pairs):
                turn(slot, pair_even, at, lane, value)
        return carry

    def fold_odd(i):
        at = pl.ds(pl.multiple_of(i * 16, 16), 16)
        for lane in range(0, length, 128):
            for slot, value in enumerate(odd_classes(lambda q: design[q, at, lane : lane + 128])):
                turn(EVEN + slot, pair_odd, at, lane, value)

    loads[5].wait()
    lax.fori_loop(0, everyone // 16, fold_even, 0)

    def spectra_of(parts, matrix):
        high = parts[:, : parts.shape[1] // 2]
        return jnp.dot(
            jnp.concatenate([parts, high], axis=1), matrix, preferred_element_type=jnp.float32
        ).astype(jnp.bfloat16)

    def gram(spectra, weight):
        weighted = (spectra[:columns].astype(jnp.float32) * weight).astype(jnp.bfloat16)
        return lax.dot_general(
            spectra[columns:], weighted, (((1,), (1,)), ((), ())), preferred_element_type=jnp.float32
        )

    units = everyone // 16 // EVEN

    def even_step(slot, carry):
        spectra_even[slot] = spectra_of(pair_even[slot], mat[...])
        for unit in range(units):
            fold_odd(slot * units + unit)
        return carry

    lax.fori_loop(0, EVEN, even_step, 0)
    frequency_weights(psd_ref, wts, samples)
    summed = jnp.zeros((rows, columns), jnp.float32)
    for slot in range(len(CLASSES) - EVEN):
        spectra = spectra_of(pair_odd[slot], mat[...])
        summed = summed + gram(spectra, wts[slot + 2 + EVEN : slot + 3 + EVEN, :])
    for slot in range(2):
        spectra = spectra_of(real[slot], mat_real[slot])
        summed = summed + gram(spectra, wts[slot : slot + 1, 0:length])
    for slot in range(EVEN):
        summed = summed + gram(spectra_even[slot], wts[slot + 2 : slot + 3, :])
    total[...] = summed
    swap = pltpu.make_async_remote_copy(
        src_ref=total,
        dst_ref=other_ref,
        send_sem=side_send.at[2],
        recv_sem=side_recv.at[2],
        device_id={"comp": 1 - comp},
        device_id_type=MESH,
    )
    swap.start()
    own_ref[...] = total[...]
    swap.wait()


def fused(orbit_angles, gap_mask, column_index, lat_coeffs, psd_table):
    devices_tm = lax.axis_size("tm")
    block = orbit_angles.shape[1]
    samples = devices_tm * block
    length = samples // RADIX
    terms, columns = lat_coeffs.shape[1:]
    rows = columns * lax.axis_size("panel") // devices_tm
    everyone = rows + columns
    f32, bf16 = jnp.float32, jnp.bfloat16
    vmem = pl.BlockSpec(memory_space=pltpu.VMEM)
    count = len(CLASSES)
    own, other = pl.pallas_call(
        functools.partial(kernel, devices_tm),
        out_shape=[jax.ShapeDtypeStruct((rows, columns), f32)] * 2,
        in_specs=[pl.BlockSpec(memory_space=pltpu.HBM)] * 7,
        out_specs=[vmem] * 2,
        scratch_shapes=[
            pltpu.VMEM(column_index.shape, jnp.int32),
            pltpu.VMEM(lat_coeffs.shape, bf16),
            pltpu.VMEM(psd_table.shape, jnp.int32),
            pltpu.VMEM((devices_tm, 2, block), f32),
            pltpu.VMEM((devices_tm, 1, block), jnp.int32),
            pltpu.VMEM((terms, rows), bf16),
            pltpu.VMEM((2, rows), jnp.int32),
            pltpu.VMEM((everyone, terms), bf16),
            pltpu.VMEM((2 + len(SINE_LON), everyone, 128), f32),
            pltpu.VMEM((RADIX // 2, terms, length), bf16),
            pltpu.VMEM((RADIX // 2, terms, length), bf16),
            pltpu.VMEM((RADIX, everyone, length), f32),
            pltpu.VMEM((2, everyone, 2 * length), bf16),
            pltpu.VMEM((EVEN, everyone, 4 * length), bf16),
            pltpu.VMEM((count - EVEN, everyone, 4 * length), bf16),
            pltpu.VMEM((EVEN, everyone, 2 * length), bf16),
            pltpu.VMEM((2, 3 * length, length), bf16),
            pltpu.VMEM((6 * length, 2 * length), bf16),
            pltpu.VMEM((4, length, length), f32),
            pltpu.VMEM((2 * count, length), f32),
            pltpu.VMEM((16, 2 * length), f32),
            pltpu.VMEM((rows, columns), f32),
            pltpu.SemaphoreType.DMA((2, devices_tm)),
            pltpu.SemaphoreType.DMA((2, devices_tm)),
            pltpu.SemaphoreType.DMA((3,)),
            pltpu.SemaphoreType.DMA((3,)),
            pltpu.SemaphoreType.DMA((7,)),
        ],
        compiler_params=pltpu.CompilerParams(
            collective_id=0, has_side_effects=True, vmem_limit_bytes=63 * 1024 * 1024
        ),
    )(orbit_angles, gap_mask.reshape(1, block), column_index, lat_coeffs, psd_table, *tables(length))
    return own + other


def choose(orbit_angles, gap_mask, column_index, lat_coeffs, psd_table):
    devices_tm, panels = lax.axis_size("tm"), lax.axis_size("panel")
    samples = devices_tm * orbit_angles.shape[1]
    columns = lat_coeffs.shape[2]
    rows = columns * panels // devices_tm
    fits = (
        samples == 4096
        and orbit_angles.shape[1] % 512 == 0
        and panels == 2
        and lax.axis_size("comp") == 2
        and rows % 128 == 0
        and columns % rows == 0
        and lat_coeffs.shape[1] % 32 == 0
        and (rows + columns) * lat_coeffs.shape[1] <= 512 * 1024
    )
    step = fused if fits else body
    return step(orbit_angles, gap_mask, column_index, lat_coeffs, psd_table)


def solution(mesh):
    return jax.shard_map(
        choose,
        mesh=mesh,
        in_specs=(
            P(None, ("groups", "tm")),
            P(("groups", "tm")),
            P(None, "panel"),
            P("comp", None, "panel"),
            P("comp", None),
        ),
        out_specs=P(("groups", "tm"), "panel"),
        check_vma=False,
    )
```

```python
import functools
import math

import jax
import jax.numpy as jnp
import numpy as np
from jax import lax
from jax.experimental import pallas as pl
from jax.experimental.pallas import tpu as pltpu
from jax.sharding import PartitionSpec as P

SPLIT = 64


def synthesize(angles, keep_rows, column_index, coeffs):
    terms_lat = coeffs.shape[0] // 2
    colatitude = angles[0]
    longit = angles[1]
    wavenumbers = jnp.arange(terms_lat, dtype=jnp.float32)
    phases = colatitude[:, None] * wavenumbers[None, :]
    basis_rows = jnp.concatenate([jnp.cos(phases), jnp.sin(phases)], axis=1).astype(jnp.bfloat16)
    degree = column_index[0]
    orders = column_index[1]
    levels = jnp.arange(2 * terms_lat, dtype=jnp.int32) % terms_lat
    allowed = levels[:, None] <= degree[None, :]
    masked = jnp.where(allowed, coeffs, jnp.zeros_like(coeffs))
    latitude = jnp.dot(basis_rows, masked, preferred_element_type=jnp.float32)
    lon_phase = longit[:, None] * jnp.abs(orders).astype(jnp.float32)[None, :]
    lon_wave = jnp.where(orders[None, :] >= 0, jnp.cos(lon_phase), jnp.sin(lon_phase))
    norm_scale = 1.0 / jnp.sqrt(degree.astype(jnp.float32) + 1.0)
    return latitude * lon_wave * (keep_rows[:, None] * norm_scale[None, :])


def phase_tables(row_index, col_index, length):
    product = row_index[:, None] * col_index[None, :] % length
    angle_grid = product.astype(jnp.float32) * (2.0 * math.pi / length)
    return (jnp.cos(angle_grid), jnp.sin(angle_grid))


def dft_tables(length):
    indices = jnp.arange(length, dtype=jnp.int32)
    return phase_tables(indices, indices, length)


def rotate(real_part, imag_part, outer_index, inner_index, length):
    index_grid = outer_index[:, None] * inner_index[None, :] % length
    angle_grid = index_grid.astype(jnp.float32) * (2.0 * math.pi / length)
    cosine = jnp.cos(angle_grid)[:, :, None]
    sine_grid = jnp.sin(angle_grid)[:, :, None]
    return (real_part * cosine + imag_part * sine_grid, imag_part * cosine - real_part * sine_grid)


def precise_dot(left_side, right_side):
    return jnp.dot(
        left_side, right_side, precision=lax.Precision.HIGHEST, preferred_element_type=jnp.float32
    )


def transform(cos_table, sin_table, real_part, imag_part):
    new_real = precise_dot(cos_table, real_part) + precise_dot(sin_table, imag_part)
    new_imag = precise_dot(cos_table, imag_part) - precise_dot(sin_table, real_part)
    return (new_real, new_imag)


def four_step(real_in, imag_in, samples):
    length = real_in.shape[0]
    columns = real_in.shape[1]
    outer_count = SPLIT
    inner_count = length // SPLIT
    real_part = real_in.reshape(outer_count, inner_count * columns)
    imag_part = imag_in.reshape(outer_count, inner_count * columns)
    cos_outer, sin_outer = dft_tables(outer_count)
    real_part, imag_part = transform(cos_outer, sin_outer, real_part, imag_part)
    real_part = real_part.reshape(outer_count, inner_count, columns)
    imag_part = imag_part.reshape(outer_count, inner_count, columns)
    real_part, imag_part = rotate(
        real_part,
        imag_part,
        jnp.arange(outer_count, dtype=jnp.int32),
        jnp.arange(inner_count, dtype=jnp.int32),
        length,
    )
    real_part = jnp.transpose(real_part, (1, 0, 2)).reshape(inner_count, outer_count * columns)
    imag_part = jnp.transpose(imag_part, (1, 0, 2)).reshape(inner_count, outer_count * columns)
    cos_inner, sin_inner = dft_tables(inner_count)
    real_part, imag_part = transform(cos_inner, sin_inner, real_part, imag_part)
    return (
        real_part.reshape(length, columns) / samples,
        imag_part.reshape(length, columns) / samples,
    )


def local_transform(received, samples):
    real_part, imag_part = four_step(received[0, 0], received[1, 0], samples)
    return (real_part.astype(jnp.bfloat16), imag_part.astype(jnp.bfloat16))


def noise_weighted(spectra, psd_row, frequency, samples):
    folded = jnp.minimum(frequency, samples - frequency)
    inverse_psd = 8192.0 / jnp.take(psd_row, folded).astype(jnp.float32)
    return (spectra.astype(jnp.float32) * inverse_psd[None, :, None]).astype(jnp.bfloat16)


def settle(partial_value, sum_dim):
    summed = lax.psum_scatter(partial_value, "tm", scatter_dimension=sum_dim, tiled=True)
    return lax.psum(summed, "comp")


def body(orbit_angles, gap_mask, column_index, lat_coeffs, psd_table):
    devices_tm = lax.axis_size("tm")
    epochs = orbit_angles.shape[1]
    block_len = epochs // devices_tm
    samples = epochs * devices_tm
    columns = lat_coeffs.shape[2]
    coeffs = lat_coeffs[0]
    keep_rows = gap_mask.astype(jnp.float32)
    packed = jnp.concatenate([orbit_angles, keep_rows[None]], axis=0)[:, None, :]
    received = lax.all_to_all(packed, "tm", split_axis=2, concat_axis=1, tiled=True)
    flat_orbit = received.reshape(3, devices_tm * block_len)
    spread = synthesize(flat_orbit[0:2], flat_orbit[2], column_index, coeffs).reshape(
        devices_tm, block_len, columns
    )
    position = lax.axis_index("tm")
    local_epoch = position * block_len + jnp.arange(block_len, dtype=jnp.int32)
    cos_outer, sin_outer = dft_tables(devices_tm)
    flat_design = spread.reshape(devices_tm, block_len * columns)
    real_part = precise_dot(cos_outer, flat_design).reshape(devices_tm, block_len, columns)
    imag_part = -precise_dot(sin_outer, flat_design).reshape(devices_tm, block_len, columns)
    real_part, imag_part = rotate(
        real_part, imag_part, jnp.arange(devices_tm, dtype=jnp.int32), local_epoch, samples
    )
    twisted = jnp.stack([real_part, imag_part])
    spec_real, spec_imag = local_transform(
        lax.all_to_all(twisted, "tm", split_axis=1, concat_axis=2, tiled=True), samples
    )
    spectra = jnp.stack([spec_real, spec_imag])
    psd_row = psd_table[0]
    contract = (((0, 1), (0, 1)), ((), ()))
    frequency = position + devices_tm * jnp.arange(epochs, dtype=jnp.int32)
    weighted = noise_weighted(spectra, psd_row, frequency, samples)
    partial_value = lax.dot_general(
        lax.all_gather(spectra, "panel", axis=2, tiled=True),
        weighted,
        contract,
        preferred_element_type=jnp.float32,
    )
    return settle(partial_value, 0)


RADIX = 16
SINE_LON = (6.283164044168851, -41.33714234995496, 81.34076808172247, -70.99342472149007)
SINE_FINE = (
    6.283185160088548,
    -41.3416550311802,
    81.60100405747373,
    -76.54978191007581,
    39.53670300634923,
)
CLASSES = (2, 4, 6, 1, 5, 9, 13)
EVEN = 3
ROUNDER = 1.5 * 2.0**23
MESH = pl.DeviceIdType.MESH


def cos_turns(turns, terms=SINE_FINE):
    offset = turns - ((turns + ROUNDER) - ROUNDER)
    near = 0.25 - jnp.abs(offset)
    square = near * near
    total = terms[-1]
    for term in terms[-2::-1]:
        total = total * square + term
    return total * near


def iota(shape, dim):
    return lax.broadcasted_iota(jnp.int32, shape, dim)


def split(value):
    high = value.astype(jnp.bfloat16)
    return high, (value - high.astype(jnp.float32)).astype(jnp.bfloat16)


def tables(length):
    samples = RADIX * length
    half = length // 2

    def waves(product):
        angle = (product % samples) * (2.0 * np.pi / samples)
        return np.cos(angle), np.sin(angle)

    count = np.arange(length)
    cosine, sine = waves(RADIX * np.outer(count, count))
    zero = np.concatenate([cosine[:, :half], -sine[:, :half]], axis=1)
    zero[:, half] = 1 - 2 * (count % 2)
    eight = np.concatenate(waves(np.outer(count, RADIX // 2 + RADIX * count[:half])), axis=1)
    eight[:, half:] *= -1
    turn = [wave for cls in CLASSES for wave in waves(cls * count)]
    square = np.stack([cosine, sine, zero, eight]) / samples
    return square.astype(np.float32), np.stack(turn).astype(np.float32)


def put_matrix(ref, at, value, lanes):
    high, low = split(value)
    third = ref.shape[0] // 3
    for block, part in ((0, high), (1, high), (2, low)):
        start = block * third + at
        ref[start : start + value.shape[0], lanes] = part


def put_rows(ref, slot, rows, at, value):
    high, low = split(value)
    past = ref.shape[2] // 2 + at
    ref[slot, rows, at : at + value.shape[1]] = high
    ref[slot, rows, past : past + value.shape[1]] = low


def frequency_weights(psd_ref, wts_ref, samples):
    length = samples // RADIX
    half = length // 2
    power = jnp.concatenate([psd_ref[:, half * i : half * (i + 1)] for i in range(RADIX)], axis=0)
    spread = (iota((RADIX, half), 0) == iota((RADIX, half), 1) >> 3).astype(jnp.bfloat16)
    keep = (iota((half, half), 0) >> 4) == (iota((half, half), 1) & (half // RADIX - 1))
    pick_up = ((iota((RADIX, half), 1) & (RADIX - 1)) == iota((RADIX, half), 0)).astype(jnp.bfloat16)
    pick_down = ((iota((RADIX, half), 1) + iota((RADIX, half), 0)) & (RADIX - 1) == 0).astype(
        jnp.bfloat16
    )
    flip = (iota((half, half), 0) + iota((half, half), 1) == half - 1).astype(jnp.bfloat16)
    up = jnp.zeros((RADIX, half), jnp.float32)
    down = jnp.zeros((RADIX, half), jnp.float32)
    for digits, unit in ((power >> 8, 256.0), (power & 255, 1.0)):
        digits = digits.astype(jnp.float32).astype(jnp.bfloat16)
        moved = lax.dot_general(
            digits, spread, (((0,), (0,)), ((), ())), preferred_element_type=jnp.float32
        )
        moved = jnp.where(keep, moved, 0.0).astype(jnp.bfloat16)
        up = up + unit * jnp.dot(pick_up, moved, preferred_element_type=jnp.float32)
        back = jnp.dot(pick_down, moved, preferred_element_type=jnp.float32).astype(jnp.bfloat16)
        down = down + unit * jnp.dot(back, flip, preferred_element_type=jnp.float32)
    up = 2.0 * (8192.0 / up)
    down = 2.0 * (8192.0 / down)
    last = 8192.0 / psd_ref[:, samples // 2 : samples // 2 + 1].astype(jnp.float32)
    first = iota((1, half), 1) == 0
    wts_ref[0:1, 0:half] = jnp.where(first, 0.5 * up[0:1], up[0:1])
    wts_ref[0:1, half:length] = jnp.where(first, last, up[0:1])
    wts_ref[1:2, 0:half] = up[RADIX // 2 : RADIX // 2 + 1]
    wts_ref[1:2, half:length] = up[RADIX // 2 : RADIX // 2 + 1]
    for slot, cls in enumerate(CLASSES):
        for at in (0, length):
            wts_ref[slot + 2 : slot + 3, at : at + half] = up[cls : cls + 1]
            wts_ref[slot + 2 : slot + 3, at + half : at + length] = down[cls : cls + 1]


def even_classes(d):
    r = math.sqrt(0.5)
    even, alt = [], []
    for q in range(4):
        first, second = d(q) + d(q + 8), d(q + 4) + d(q + 12)
        even.append(first + second)
        alt.append(first - second)
    e02, e13 = even[0] + even[2], even[1] + even[3]
    four = (even[0] - even[2], even[3] - even[1])
    p, q = r * (alt[1] - alt[3]), r * (alt[1] + alt[3])
    two = (alt[0] + p, -(alt[2] + q))
    six = (alt[0] - p, alt[2] - q)
    return (e02 + e13, e02 - e13), (two, four, six)


def odd_classes(d):
    br, bi = [], []
    for q in range(4):
        real, imag = d(q) - d(q + 8), d(q + 12) - d(q + 4)
        c, s = math.cos(math.pi * q / 8), math.sin(math.pi * q / 8)
        if q == 2:
            real, imag = c * (real + imag), c * (imag - real)
        elif q:
            real, imag = c * real + s * imag, c * imag - s * real
        br.append(real)
        bi.append(imag)
    sr, si = br[0] + br[2], bi[0] + bi[2]
    tr, ti = br[1] + br[3], bi[1] + bi[3]
    ur, ui = br[0] - br[2], bi[0] - bi[2]
    vr, vi = br[1] - br[3], bi[1] - bi[3]
    return (sr + tr, si + ti), (ur + vi, ui - vr), (sr - tr, si - ti), (ur - vi, ui + vr)


def kernel(
    devices_tm,
    angles_hbm,
    mask_hbm,
    columns_hbm,
    coeffs_hbm,
    psd_hbm,
    square_hbm,
    twiddle_hbm,
    own_ref,
    other_ref,
    columns_ref,
    coeffs_ref,
    psd_ref,
    orbit,
    flags,
    far_coeffs,
    far_columns,
    coeffs_t,
    column_t,
    basis_a,
    basis_b,
    design,
    real,
    pair_even,
    pair_odd,
    spectra_even,
    mat_real,
    mat,
    square,
    twiddle,
    wts,
    total,
    send_sem,
    recv_sem,
    side_send,
    side_recv,
    load_sem,
):
    block = angles_hbm.shape[1]
    samples = block * devices_tm
    length = samples // RADIX
    half = length // 2
    terms = coeffs_ref.shape[1]
    terms_lat = terms // 2
    columns = coeffs_ref.shape[2]
    rows = own_ref.shape[0]
    everyone = rows + columns
    me = lax.axis_index("tm")
    panel = lax.axis_index("panel")
    comp = lax.axis_index("comp")

    barrier = pltpu.get_barrier_semaphore()
    peers = [lax.rem(me + k, devices_tm) for k in range(1, devices_tm)]
    for peer in peers:
        pl.semaphore_signal(barrier, inc=1, device_id={"tm": peer}, device_id_type=MESH)
    pl.semaphore_signal(barrier, inc=1, device_id={"panel": 1 - panel}, device_id_type=MESH)
    pl.semaphore_signal(barrier, inc=1, device_id={"comp": 1 - comp}, device_id_type=MESH)

    loads = [
        pltpu.make_async_copy(source, held, load_sem.at[i])
        for i, (source, held) in enumerate(
            (
                (angles_hbm, orbit.at[me]),
                (mask_hbm, flags.at[me]),
                (columns_hbm, columns_ref),
                (coeffs_hbm, coeffs_ref),
                (psd_hbm, psd_ref),
                (twiddle_hbm, twiddle),
                (square_hbm, square),
            )
        )
    ]
    for load in loads:
        load.start()
    loads[6].wait()
    left, right = slice(0, length), slice(length, 2 * length)
    put_matrix(mat, 0, square[0], left)
    put_matrix(mat, 0, -square[1], right)
    put_matrix(mat, length, square[1], left)
    put_matrix(mat, length, square[0], right)
    put_matrix(mat_real.at[0], 0, square[2], left)
    put_matrix(mat_real.at[1], 0, square[3], left)
    loads[4].wait()

    def place(at, coeffs, index_rows):
        width = coeffs.shape[1]
        level = iota((terms, width), 0)
        level = jnp.where(level < terms_lat, level, level - terms_lat)
        masked = jnp.where(level <= index_rows[0:1, :], coeffs, 0.0)
        coeffs_t[at : at + width, :] = jnp.transpose(masked).astype(jnp.bfloat16)
        orders = index_rows[1:2, :]
        shift = jnp.where(orders >= 0, 0.0, 0.25)
        norm = 1.0 / jnp.sqrt(index_rows[0:1, :].astype(jnp.float32) + 1.0)
        packed = jnp.concatenate(
            [jnp.abs(orders).astype(jnp.float32), shift]
            + [norm * term for term in SINE_LON]
            + [jnp.zeros((2, width), jnp.float32)],
            axis=0,
        )
        turned = jnp.transpose(packed)
        for i in range(2 + len(SINE_LON)):
            column_t[i, at : at + width, :] = jnp.broadcast_to(turned[:, i : i + 1], (width, 128))

    loads[2].wait()
    loads[3].wait()
    place(0, coeffs_ref[0].astype(jnp.float32), columns_ref[...])
    pl.semaphore_wait(barrier, devices_tm + 1)

    def send_orbit(k, slot, peer):
        return [
            pltpu.make_async_remote_copy(
                src_ref=source,
                dst_ref=held.at[slot],
                send_sem=send_sem.at[i, k],
                recv_sem=recv_sem.at[i, slot],
                device_id={"tm": peer},
                device_id_type=MESH,
            )
            for i, (source, held) in enumerate(((angles_hbm, orbit), (mask_hbm, flags)))
        ]

    for k, peer in enumerate(peers):
        for copy in send_orbit(k, me, peer):
            copy.start()
    first_row = me * rows
    lanes = pl.ds(pl.multiple_of(lax.rem(first_row, columns), rows), rows)
    send_coeffs = pltpu.make_async_remote_copy(
        src_ref=coeffs_hbm.at[0, :, lanes],
        dst_ref=far_coeffs,
        send_sem=side_send.at[0],
        recv_sem=side_recv.at[0],
        device_id={"panel": 1 - panel},
        device_id_type=MESH,
    )
    send_columns = pltpu.make_async_remote_copy(
        src_ref=columns_hbm.at[:, lanes],
        dst_ref=far_columns,
        send_sem=side_send.at[1],
        recv_sem=side_recv.at[1],
        device_id={"panel": 1 - panel},
        device_id_type=MESH,
    )
    send_coeffs.start()
    send_columns.start()

    loads[0].wait()
    loads[1].wait()
    per_device = block // length

    def epoch_lanes(chunk):
        at = lax.rem(chunk, per_device) * length
        return chunk // per_device, pl.ds(pl.multiple_of(at, length), length)

    def fill_basis(chunk, basis, slot):
        holder, lanes = epoch_lanes(chunk)
        theta = orbit[holder, 0:1, lanes] * (0.5 / math.pi)
        keep = flags[holder, :, lanes].astype(jnp.float32)
        turns = iota((16, length), 0).astype(jnp.float32) * theta
        cosine, sine = cos_turns(turns) * keep, cos_turns(turns - 0.25) * keep
        step_c, step_s = cos_turns(16.0 * theta), cos_turns(16.0 * theta - 0.25)
        for at in range(0, terms_lat, 16):
            basis[slot, at : at + 16, :] = cosine.astype(jnp.bfloat16)
            basis[slot, terms_lat + at : terms_lat + at + 16, :] = sine.astype(jnp.bfloat16)
            cosine, sine = cosine * step_c - sine * step_s, sine * step_c + cosine * step_s

    def fill_design(chunk, basis, slot, at, width):
        holder, lanes = epoch_lanes(chunk)
        longit = orbit[holder, 1:2, lanes] * (0.5 / math.pi)
        latitude = jnp.dot(
            coeffs_t[at : at + width, :], basis[slot], preferred_element_type=jnp.float32
        )
        for row in range(0, width, 32):
            these = slice(at + row, at + row + 32)
            for lane in range(0, length, 128):
                where = slice(lane, lane + 128)
                wave = cos_turns(
                    column_t[0, these, :] * longit[:, where] - column_t[1, these, :],
                    [column_t[2 + i, these, :] for i in range(len(SINE_LON))],
                )
                design[chunk, these, where] = latitude[row : row + 32, where] * wave

    own_chunks = me * per_device

    def near_columns(first, last):
        def two_chunks(i, carry):
            chunk = lax.rem(own_chunks + 2 * i, RADIX)
            again = jnp.where(i + 1 < last, i + 1, first)
            fill_basis(chunk + 1, basis_b, i)
            fill_design(chunk, basis_a, i, 0, columns)
            fill_basis(lax.rem(own_chunks + 2 * again, RADIX), basis_a, again)
            fill_design(chunk + 1, basis_b, i, 0, columns)
            return carry

        fill_basis(lax.rem(own_chunks + 2 * first, RADIX), basis_a, first)
        lax.fori_loop(first, last, two_chunks, 0)

    near_columns(0, per_device // 2)
    for k, peer in enumerate(peers):
        for copy in send_orbit(k, me, peer):
            copy.wait_send()
        for copy in send_orbit(k, peer, peer):
            copy.wait_recv()

    near_columns(per_device // 2, RADIX // 2)
    send_coeffs.wait()
    send_columns.wait()
    mine = first_row // columns == panel
    near = coeffs_ref[0, :, lanes].astype(jnp.float32)
    place(
        columns,
        jnp.where(mine, near, far_coeffs[...].astype(jnp.float32)),
        jnp.where(mine, columns_ref[:, lanes], far_columns[...]),
    )

    def far_rows(i, carry):
        chunk = lax.rem(own_chunks + 2 * i, RADIX)
        fill_design(chunk, basis_a, i, columns, rows)
        fill_design(chunk + 1, basis_b, i, columns, rows)
        return carry

    lax.fori_loop(0, RADIX // 2, far_rows, 0)

    def turn(slot, pair, at, lane, value):
        re, im = value
        c = twiddle[2 * slot : 2 * slot + 1, lane : lane + 128]
        s = twiddle[2 * slot + 1 : 2 * slot + 2, lane : lane + 128]
        place_at = slot if slot < EVEN else slot - EVEN
        put_rows(pair, place_at, at, lane, re * c + im * s)
        put_rows(pair, place_at, at, length + lane, im * c - re * s)

    def fold_even(i, carry):
        at = pl.ds(pl.multiple_of(i * 16, 16), 16)
        for lane in range(0, length, 128):
            plain, pairs = even_classes(lambda q: design[q, at, lane : lane + 128])
            for slot, value in enumerate(plain):
                put_rows(real, slot, at, lane, value)
            for slot, value in enumerate(pairs):
                turn(slot, pair_even, at, lane, value)
        return carry

    def fold_odd(i):
        at = pl.ds(pl.multiple_of(i * 16, 16), 16)
        for lane in range(0, length, 128):
            for slot, value in enumerate(odd_classes(lambda q: design[q, at, lane : lane + 128])):
                turn(EVEN + slot, pair_odd, at, lane, value)

    loads[5].wait()
    lax.fori_loop(0, everyone // 16, fold_even, 0)

    def spectra_of(parts, matrix):
        high = parts[:, : parts.shape[1] // 2]
        return jnp.dot(
            jnp.concatenate([parts, high], axis=1), matrix, preferred_element_type=jnp.float32
        ).astype(jnp.bfloat16)

    def gram(spectra, weight):
        weighted = (spectra[:columns].astype(jnp.float32) * weight).astype(jnp.bfloat16)
        return lax.dot_general(
            spectra[columns:], weighted, (((1,), (1,)), ((), ())), preferred_element_type=jnp.float32
        )

    units = everyone // 16 // EVEN

    def even_step(slot, carry):
        spectra_even[slot] = spectra_of(pair_even[slot], mat[...])
        for unit in range(units):
            fold_odd(slot * units + unit)
        return carry

    lax.fori_loop(0, EVEN, even_step, 0)
    frequency_weights(psd_ref, wts, samples)
    summed = jnp.zeros((rows, columns), jnp.float32)
    for slot in range(len(CLASSES) - EVEN):
        spectra = spectra_of(pair_odd[slot], mat[...])
        summed = summed + gram(spectra, wts[slot + 2 + EVEN : slot + 3 + EVEN, :])
    for slot in range(2):
        spectra = spectra_of(real[slot], mat_real[slot])
        summed = summed + gram(spectra, wts[slot : slot + 1, 0:length])
    for slot in range(EVEN):
        summed = summed + gram(spectra_even[slot], wts[slot + 2 : slot + 3, :])
    total[...] = summed
    swap = pltpu.make_async_remote_copy(
        src_ref=total,
        dst_ref=other_ref,
        send_sem=side_send.at[2],
        recv_sem=side_recv.at[2],
        device_id={"comp": 1 - comp},
        device_id_type=MESH,
    )
    swap.start()
    own_ref[...] = total[...]
    swap.wait()


def fused(orbit_angles, gap_mask, column_index, lat_coeffs, psd_table):
    devices_tm = lax.axis_size("tm")
    block = orbit_angles.shape[1]
    samples = devices_tm * block
    length = samples // RADIX
    terms, columns = lat_coeffs.shape[1:]
    rows = columns * lax.axis_size("panel") // devices_tm
    everyone = rows + columns
    f32, bf16 = jnp.float32, jnp.bfloat16
    vmem = pl.BlockSpec(memory_space=pltpu.VMEM)
    count = len(CLASSES)
    own, other = pl.pallas_call(
        functools.partial(kernel, devices_tm),
        out_shape=[jax.ShapeDtypeStruct((rows, columns), f32)] * 2,
        in_specs=[pl.BlockSpec(memory_space=pltpu.HBM)] * 7,
        out_specs=[vmem] * 2,
        scratch_shapes=[
            pltpu.VMEM(column_index.shape, jnp.int32),
            pltpu.VMEM(lat_coeffs.shape, bf16),
            pltpu.VMEM(psd_table.shape, jnp.int32),
            pltpu.VMEM((devices_tm, 2, block), f32),
            pltpu.VMEM((devices_tm, 1, block), jnp.int32),
            pltpu.VMEM((terms, rows), bf16),
            pltpu.VMEM((2, rows), jnp.int32),
            pltpu.VMEM((everyone, terms), bf16),
            pltpu.VMEM((2 + len(SINE_LON), everyone, 128), f32),
            pltpu.VMEM((RADIX // 2, terms, length), bf16),
            pltpu.VMEM((RADIX // 2, terms, length), bf16),
            pltpu.VMEM((RADIX, everyone, length), f32),
            pltpu.VMEM((2, everyone, 2 * length), bf16),
            pltpu.VMEM((EVEN, everyone, 4 * length), bf16),
            pltpu.VMEM((count - EVEN, everyone, 4 * length), bf16),
            pltpu.VMEM((EVEN, everyone, 2 * length), bf16),
            pltpu.VMEM((2, 3 * length, length), bf16),
            pltpu.VMEM((6 * length, 2 * length), bf16),
            pltpu.VMEM((4, length, length), f32),
            pltpu.VMEM((2 * count, length), f32),
            pltpu.VMEM((16, 2 * length), f32),
            pltpu.VMEM((rows, columns), f32),
            pltpu.SemaphoreType.DMA((2, devices_tm)),
            pltpu.SemaphoreType.DMA((2, devices_tm)),
            pltpu.SemaphoreType.DMA((3,)),
            pltpu.SemaphoreType.DMA((3,)),
            pltpu.SemaphoreType.DMA((7,)),
        ],
        compiler_params=pltpu.CompilerParams(
            collective_id=0, has_side_effects=True, vmem_limit_bytes=63 * 1024 * 1024
        ),
    )(orbit_angles, gap_mask.reshape(1, block), column_index, lat_coeffs, psd_table, *tables(length))
    return own + other


def choose(orbit_angles, gap_mask, column_index, lat_coeffs, psd_table):
    devices_tm, panels = lax.axis_size("tm"), lax.axis_size("panel")
    samples = devices_tm * orbit_angles.shape[1]
    columns = lat_coeffs.shape[2]
    rows = columns * panels // devices_tm
    fits = (
        samples == 4096
        and orbit_angles.shape[1] % 512 == 0
        and panels == 2
        and lax.axis_size("comp") == 2
        and rows % 128 == 0
        and columns % rows == 0
        and lat_coeffs.shape[1] % 32 == 0
        and (rows + columns) * lat_coeffs.shape[1] <= 512 * 1024
    )
    step = fused if fits else body
    return step(orbit_angles, gap_mask, column_index, lat_coeffs, psd_table)


def solution(mesh):
    return jax.shard_map(
        choose,
        mesh=mesh,
        in_specs=(
            P(None, ("groups", "tm")),
            P(("groups", "tm")),
            P(None, "panel"),
            P("comp", None, "panel"),
            P("comp", None),
        ),
        out_specs=P(("groups", "tm"), "panel"),
        check_vma=False,
    )
```

```python
import functools
import math

import jax
import jax.numpy as jnp
import numpy as np
from jax import lax
from jax.experimental import pallas as pl
from jax.experimental.pallas import tpu as pltpu
from jax.sharding import PartitionSpec as P

SPLIT = 64


def synthesize(angles, keep_rows, column_index, coeffs):
    terms_lat = coeffs.shape[0] // 2
    colatitude = angles[0]
    longit = angles[1]
    wavenumbers = jnp.arange(terms_lat, dtype=jnp.float32)
    phases = colatitude[:, None] * wavenumbers[None, :]
    basis_rows = jnp.concatenate([jnp.cos(phases), jnp.sin(phases)], axis=1).astype(jnp.bfloat16)
    degree = column_index[0]
    orders = column_index[1]
    levels = jnp.arange(2 * terms_lat, dtype=jnp.int32) % terms_lat
    allowed = levels[:, None] <= degree[None, :]
    masked = jnp.where(allowed, coeffs, jnp.zeros_like(coeffs))
    latitude = jnp.dot(basis_rows, masked, preferred_element_type=jnp.float32)
    lon_phase = longit[:, None] * jnp.abs(orders).astype(jnp.float32)[None, :]
    lon_wave = jnp.where(orders[None, :] >= 0, jnp.cos(lon_phase), jnp.sin(lon_phase))
    norm_scale = 1.0 / jnp.sqrt(degree.astype(jnp.float32) + 1.0)
    return latitude * lon_wave * (keep_rows[:, None] * norm_scale[None, :])


def phase_tables(row_index, col_index, length):
    product = row_index[:, None] * col_index[None, :] % length
    angle_grid = product.astype(jnp.float32) * (2.0 * math.pi / length)
    return (jnp.cos(angle_grid), jnp.sin(angle_grid))


def dft_tables(length):
    indices = jnp.arange(length, dtype=jnp.int32)
    return phase_tables(indices, indices, length)


def rotate(real_part, imag_part, outer_index, inner_index, length):
    index_grid = outer_index[:, None] * inner_index[None, :] % length
    angle_grid = index_grid.astype(jnp.float32) * (2.0 * math.pi / length)
    cosine = jnp.cos(angle_grid)[:, :, None]
    sine_grid = jnp.sin(angle_grid)[:, :, None]
    return (real_part * cosine + imag_part * sine_grid, imag_part * cosine - real_part * sine_grid)


def precise_dot(left_side, right_side):
    return jnp.dot(
        left_side, right_side, precision=lax.Precision.HIGHEST, preferred_element_type=jnp.float32
    )


def transform(cos_table, sin_table, real_part, imag_part):
    new_real = precise_dot(cos_table, real_part) + precise_dot(sin_table, imag_part)
    new_imag = precise_dot(cos_table, imag_part) - precise_dot(sin_table, real_part)
    return (new_real, new_imag)


def four_step(real_in, imag_in, samples):
    length = real_in.shape[0]
    columns = real_in.shape[1]
    outer_count = SPLIT
    inner_count = length // SPLIT
    real_part = real_in.reshape(outer_count, inner_count * columns)
    imag_part = imag_in.reshape(outer_count, inner_count * columns)
    cos_outer, sin_outer = dft_tables(outer_count)
    real_part, imag_part = transform(cos_outer, sin_outer, real_part, imag_part)
    real_part = real_part.reshape(outer_count, inner_count, columns)
    imag_part = imag_part.reshape(outer_count, inner_count, columns)
    real_part, imag_part = rotate(
        real_part,
        imag_part,
        jnp.arange(outer_count, dtype=jnp.int32),
        jnp.arange(inner_count, dtype=jnp.int32),
        length,
    )
    real_part = jnp.transpose(real_part, (1, 0, 2)).reshape(inner_count, outer_count * columns)
    imag_part = jnp.transpose(imag_part, (1, 0, 2)).reshape(inner_count, outer_count * columns)
    cos_inner, sin_inner = dft_tables(inner_count)
    real_part, imag_part = transform(cos_inner, sin_inner, real_part, imag_part)
    return (
        real_part.reshape(length, columns) / samples,
        imag_part.reshape(length, columns) / samples,
    )


def local_transform(received, samples):
    real_part, imag_part = four_step(received[0, 0], received[1, 0], samples)
    return (real_part.astype(jnp.bfloat16), imag_part.astype(jnp.bfloat16))


def noise_weighted(spectra, psd_row, frequency, samples):
    folded = jnp.minimum(frequency, samples - frequency)
    inverse_psd = 8192.0 / jnp.take(psd_row, folded).astype(jnp.float32)
    return (spectra.astype(jnp.float32) * inverse_psd[None, :, None]).astype(jnp.bfloat16)


def settle(partial_value, sum_dim):
    summed = lax.psum_scatter(partial_value, "tm", scatter_dimension=sum_dim, tiled=True)
    return lax.psum(summed, "comp")


def body(orbit_angles, gap_mask, column_index, lat_coeffs, psd_table):
    devices_tm = lax.axis_size("tm")
    epochs = orbit_angles.shape[1]
    block_len = epochs // devices_tm
    samples = epochs * devices_tm
    columns = lat_coeffs.shape[2]
    coeffs = lat_coeffs[0]
    keep_rows = gap_mask.astype(jnp.float32)
    packed = jnp.concatenate([orbit_angles, keep_rows[None]], axis=0)[:, None, :]
    received = lax.all_to_all(packed, "tm", split_axis=2, concat_axis=1, tiled=True)
    flat_orbit = received.reshape(3, devices_tm * block_len)
    spread = synthesize(flat_orbit[0:2], flat_orbit[2], column_index, coeffs).reshape(
        devices_tm, block_len, columns
    )
    position = lax.axis_index("tm")
    local_epoch = position * block_len + jnp.arange(block_len, dtype=jnp.int32)
    cos_outer, sin_outer = dft_tables(devices_tm)
    flat_design = spread.reshape(devices_tm, block_len * columns)
    real_part = precise_dot(cos_outer, flat_design).reshape(devices_tm, block_len, columns)
    imag_part = -precise_dot(sin_outer, flat_design).reshape(devices_tm, block_len, columns)
    real_part, imag_part = rotate(
        real_part, imag_part, jnp.arange(devices_tm, dtype=jnp.int32), local_epoch, samples
    )
    twisted = jnp.stack([real_part, imag_part])
    spec_real, spec_imag = local_transform(
        lax.all_to_all(twisted, "tm", split_axis=1, concat_axis=2, tiled=True), samples
    )
    spectra = jnp.stack([spec_real, spec_imag])
    psd_row = psd_table[0]
    contract = (((0, 1), (0, 1)), ((), ()))
    frequency = position + devices_tm * jnp.arange(epochs, dtype=jnp.int32)
    weighted = noise_weighted(spectra, psd_row, frequency, samples)
    partial_value = lax.dot_general(
        lax.all_gather(spectra, "panel", axis=2, tiled=True),
        weighted,
        contract,
        preferred_element_type=jnp.float32,
    )
    return settle(partial_value, 0)


RADIX = 16
SINE_LON = (6.283164044168851, -41.33714234995496, 81.34076808172247, -70.99342472149007)
SINE_FINE = (
    6.283185160088548,
    -41.3416550311802,
    81.60100405747373,
    -76.54978191007581,
    39.53670300634923,
)
CLASSES = (2, 4, 6, 1, 5, 9, 13)
EVEN = 3
ROUNDER = 1.5 * 2.0**23
MESH = pl.DeviceIdType.MESH


def cos_turns(turns, terms=SINE_FINE):
    offset = turns - ((turns + ROUNDER) - ROUNDER)
    near = 0.25 - jnp.abs(offset)
    square = near * near
    total = terms[-1]
    for term in terms[-2::-1]:
        total = total * square + term
    return total * near


def iota(shape, dim):
    return lax.broadcasted_iota(jnp.int32, shape, dim)


def split(value):
    high = value.astype(jnp.bfloat16)
    return high, (value - high.astype(jnp.float32)).astype(jnp.bfloat16)


def tables(length):
    samples = RADIX * length
    half = length // 2

    def waves(product):
        angle = (product % samples) * (2.0 * np.pi / samples)
        return np.cos(angle), np.sin(angle)

    count = np.arange(length)
    cosine, sine = waves(RADIX * np.outer(count, count))
    zero = np.concatenate([cosine[:, :half], -sine[:, :half]], axis=1)
    zero[:, half] = 1 - 2 * (count % 2)
    eight = np.concatenate(waves(np.outer(count, RADIX // 2 + RADIX * count[:half])), axis=1)
    eight[:, half:] *= -1
    turn = [wave for cls in CLASSES for wave in waves(cls * count)]
    square = np.stack([cosine, sine, zero, eight]) / samples
    return square.astype(np.float32), np.stack(turn).astype(np.float32)


def put_matrix(ref, at, value, lanes):
    high, low = split(value)
    third = ref.shape[0] // 3
    for block, part in ((0, high), (1, high), (2, low)):
        start = block * third + at
        ref[start : start + value.shape[0], lanes] = part


def put_rows(ref, slot, rows, at, value):
    high, low = split(value)
    past = ref.shape[2] // 2 + at
    ref[slot, rows, at : at + value.shape[1]] = high
    ref[slot, rows, past : past + value.shape[1]] = low


def frequency_weights(psd_ref, wts_ref, samples):
    length = samples // RADIX
    half = length // 2
    power = jnp.concatenate([psd_ref[:, half * i : half * (i + 1)] for i in range(RADIX)], axis=0)
    spread = (iota((RADIX, half), 0) == iota((RADIX, half), 1) >> 3).astype(jnp.bfloat16)
    keep = (iota((half, half), 0) >> 4) == (iota((half, half), 1) & (half // RADIX - 1))
    pick_up = ((iota((RADIX, half), 1) & (RADIX - 1)) == iota((RADIX, half), 0)).astype(jnp.bfloat16)
    pick_down = ((iota((RADIX, half), 1) + iota((RADIX, half), 0)) & (RADIX - 1) == 0).astype(
        jnp.bfloat16
    )
    flip = (iota((half, half), 0) + iota((half, half), 1) == half - 1).astype(jnp.bfloat16)
    up = jnp.zeros((RADIX, half), jnp.float32)
    down = jnp.zeros((RADIX, half), jnp.float32)
    for digits, unit in ((power >> 8, 256.0), (power & 255, 1.0)):
        digits = digits.astype(jnp.float32).astype(jnp.bfloat16)
        moved = lax.dot_general(
            digits, spread, (((0,), (0,)), ((), ())), preferred_element_type=jnp.float32
        )
        moved = jnp.where(keep, moved, 0.0).astype(jnp.bfloat16)
        up = up + unit * jnp.dot(pick_up, moved, preferred_element_type=jnp.float32)
        back = jnp.dot(pick_down, moved, preferred_element_type=jnp.float32).astype(jnp.bfloat16)
        down = down + unit * jnp.dot(back, flip, preferred_element_type=jnp.float32)
    up = 2.0 * (8192.0 / up)
    down = 2.0 * (8192.0 / down)
    last = 8192.0 / psd_ref[:, samples // 2 : samples // 2 + 1].astype(jnp.float32)
    first = iota((1, half), 1) == 0
    wts_ref[0:1, 0:half] = jnp.where(first, 0.5 * up[0:1], up[0:1])
    wts_ref[0:1, half:length] = jnp.where(first, last, up[0:1])
    wts_ref[1:2, 0:half] = up[RADIX // 2 : RADIX // 2 + 1]
    wts_ref[1:2, half:length] = up[RADIX // 2 : RADIX // 2 + 1]
    for slot, cls in enumerate(CLASSES):
        for at in (0, length):
            wts_ref[slot + 2 : slot + 3, at : at + half] = up[cls : cls + 1]
            wts_ref[slot + 2 : slot + 3, at + half : at + length] = down[cls : cls + 1]


def even_classes(d):
    r = math.sqrt(0.5)
    even, alt = [], []
    for q in range(4):
        first, second = d(q) + d(q + 8), d(q + 4) + d(q + 12)
        even.append(first + second)
        alt.append(first - second)
    e02, e13 = even[0] + even[2], even[1] + even[3]
    four = (even[0] - even[2], even[3] - even[1])
    p, q = r * (alt[1] - alt[3]), r * (alt[1] + alt[3])
    two = (alt[0] + p, -(alt[2] + q))
    six = (alt[0] - p, alt[2] - q)
    return (e02 + e13, e02 - e13), (two, four, six)


def odd_classes(d):
    br, bi = [], []
    for q in range(4):
        real, imag = d(q) - d(q + 8), d(q + 12) - d(q + 4)
        c, s = math.cos(math.pi * q / 8), math.sin(math.pi * q / 8)
        if q == 2:
            real, imag = c * (real + imag), c * (imag - real)
        elif q:
            real, imag = c * real + s * imag, c * imag - s * real
        br.append(real)
        bi.append(imag)
    sr, si = br[0] + br[2], bi[0] + bi[2]
    tr, ti = br[1] + br[3], bi[1] + bi[3]
    ur, ui = br[0] - br[2], bi[0] - bi[2]
    vr, vi = br[1] - br[3], bi[1] - bi[3]
    return (sr + tr, si + ti), (ur + vi, ui - vr), (sr - tr, si - ti), (ur - vi, ui + vr)


def kernel(
    devices_tm,
    angles_hbm,
    mask_hbm,
    columns_hbm,
    coeffs_hbm,
    psd_hbm,
    square_hbm,
    twiddle_hbm,
    own_ref,
    other_ref,
    columns_ref,
    coeffs_ref,
    psd_ref,
    orbit,
    flags,
    far_coeffs,
    far_columns,
    coeffs_t,
    column_t,
    basis_a,
    basis_b,
    design,
    real,
    pair_even,
    pair_odd,
    spectra_even,
    mat_real,
    mat,
    square,
    twiddle,
    wts,
    total,
    send_sem,
    recv_sem,
    side_send,
    side_recv,
    load_sem,
):
    block = angles_hbm.shape[1]
    samples = block * devices_tm
    length = samples // RADIX
    half = length // 2
    terms = coeffs_ref.shape[1]
    terms_lat = terms // 2
    columns = coeffs_ref.shape[2]
    rows = own_ref.shape[0]
    everyone = rows + columns
    me = lax.axis_index("tm")
    panel = lax.axis_index("panel")
    comp = lax.axis_index("comp")

    barrier = pltpu.get_barrier_semaphore()
    peers = [lax.rem(me + k, devices_tm) for k in range(1, devices_tm)]
    for peer in peers:
        pl.semaphore_signal(barrier, inc=1, device_id={"tm": peer}, device_id_type=MESH)
    pl.semaphore_signal(barrier, inc=1, device_id={"panel": 1 - panel}, device_id_type=MESH)
    pl.semaphore_signal(barrier, inc=1, device_id={"comp": 1 - comp}, device_id_type=MESH)

    loads = [
        pltpu.make_async_copy(source, held, load_sem.at[i])
        for i, (source, held) in enumerate(
            (
                (angles_hbm, orbit.at[me]),
                (mask_hbm, flags.at[me]),
                (columns_hbm, columns_ref),
                (coeffs_hbm, coeffs_ref),
                (psd_hbm, psd_ref),
                (twiddle_hbm, twiddle),
                (square_hbm, square),
            )
        )
    ]
    for load in loads:
        load.start()
    pl.semaphore_wait(barrier, devices_tm + 1)

    def send_orbit(k, slot, peer):
        return [
            pltpu.make_async_remote_copy(
                src_ref=source,
                dst_ref=held.at[slot],
                send_sem=send_sem.at[i, k],
                recv_sem=recv_sem.at[i, slot],
                device_id={"tm": peer},
                device_id_type=MESH,
            )
            for i, (source, held) in enumerate(((angles_hbm, orbit), (mask_hbm, flags)))
        ]

    for k, peer in enumerate(peers):
        for copy in send_orbit(k, me, peer):
            copy.start()
    first_row = me * rows
    lanes = pl.ds(pl.multiple_of(lax.rem(first_row, columns), rows), rows)
    send_coeffs = pltpu.make_async_remote_copy(
        src_ref=coeffs_hbm.at[0, :, lanes],
        dst_ref=far_coeffs,
        send_sem=side_send.at[0],
        recv_sem=side_recv.at[0],
        device_id={"panel": 1 - panel},
        device_id_type=MESH,
    )
    send_columns = pltpu.make_async_remote_copy(
        src_ref=columns_hbm.at[:, lanes],
        dst_ref=far_columns,
        send_sem=side_send.at[1],
        recv_sem=side_recv.at[1],
        device_id={"panel": 1 - panel},
        device_id_type=MESH,
    )
    send_coeffs.start()
    send_columns.start()

    loads[6].wait()
    left, right = slice(0, length), slice(length, 2 * length)
    put_matrix(mat, 0, square[0], left)
    put_matrix(mat, 0, -square[1], right)
    put_matrix(mat, length, square[1], left)
    put_matrix(mat, length, square[0], right)
    put_matrix(mat_real.at[0], 0, square[2], left)
    put_matrix(mat_real.at[1], 0, square[3], left)
    loads[4].wait()

    def place(at, coeffs, index_rows):
        width = coeffs.shape[1]
        level = iota((terms, width), 0)
        level = jnp.where(level < terms_lat, level, level - terms_lat)
        masked = jnp.where(level <= index_rows[0:1, :], coeffs, 0.0)
        coeffs_t[at : at + width, :] = jnp.transpose(masked).astype(jnp.bfloat16)
        orders = index_rows[1:2, :]
        shift = jnp.where(orders >= 0, 0.0, 0.25)
        norm = 1.0 / jnp.sqrt(index_rows[0:1, :].astype(jnp.float32) + 1.0)
        packed = jnp.concatenate(
            [jnp.abs(orders).astype(jnp.float32), shift]
            + [norm * term for term in SINE_LON]
            + [jnp.zeros((2, width), jnp.float32)],
            axis=0,
        )
        turned = jnp.transpose(packed)
        for i in range(2 + len(SINE_LON)):
            column_t[i, at : at + width, :] = jnp.broadcast_to(turned[:, i : i + 1], (width, 128))

    loads[2].wait()
    loads[3].wait()
    place(0, coeffs_ref[0].astype(jnp.float32), columns_ref[...])
    loads[0].wait()
    loads[1].wait()
    per_device = block // length

    def epoch_lanes(chunk):
        at = lax.rem(chunk, per_device) * length
        return chunk // per_device, pl.ds(pl.multiple_of(at, length), length)

    def fill_basis(chunk, basis, slot):
        holder, lanes = epoch_lanes(chunk)
        theta = orbit[holder, 0:1, lanes] * (0.5 / math.pi)
        keep = flags[holder, :, lanes].astype(jnp.float32)
        turns = iota((16, length), 0).astype(jnp.float32) * theta
        cosine, sine = cos_turns(turns) * keep, cos_turns(turns - 0.25) * keep
        step_c, step_s = cos_turns(16.0 * theta), cos_turns(16.0 * theta - 0.25)
        for at in range(0, terms_lat, 16):
            basis[slot, at : at + 16, :] = cosine.astype(jnp.bfloat16)
            basis[slot, terms_lat + at : terms_lat + at + 16, :] = sine.astype(jnp.bfloat16)
            cosine, sine = cosine * step_c - sine * step_s, sine * step_c + cosine * step_s

    def fill_design(chunk, basis, slot, at, width):
        holder, lanes = epoch_lanes(chunk)
        longit = orbit[holder, 1:2, lanes] * (0.5 / math.pi)
        these = slice(at, at + width)
        latitude = jnp.dot(coeffs_t[these, :], basis[slot], preferred_element_type=jnp.float32)
        terms_lon = [column_t[2 + i, these, :] for i in range(len(SINE_LON))]
        for lane in range(0, length, 128):
            where = slice(lane, lane + 128)
            wave = cos_turns(
                column_t[0, these, :] * longit[:, where] - column_t[1, these, :], terms_lon
            )
            design[chunk, these, where] = latitude[:, where] * wave

    own_chunks = me * per_device

    def chunks(first, last, width):
        def two_chunks(i, carry):
            chunk = lax.rem(own_chunks + 2 * i, RADIX)
            again = jnp.where(i + 1 < last, i + 1, first)
            fill_basis(chunk + 1, basis_b, i)
            fill_design(chunk, basis_a, i, 0, width)
            fill_basis(lax.rem(own_chunks + 2 * again, RADIX), basis_a, again)
            fill_design(chunk + 1, basis_b, i, 0, width)
            return carry

        fill_basis(lax.rem(own_chunks + 2 * first, RADIX), basis_a, first)
        lax.fori_loop(first, last, two_chunks, 0)

    chunks(0, per_device // 2, columns)
    for k, peer in enumerate(peers):
        for copy in send_orbit(k, me, peer):
            copy.wait_send()
        for copy in send_orbit(k, peer, peer):
            copy.wait_recv()

    send_coeffs.wait()
    send_columns.wait()
    mine = first_row // columns == panel
    near = coeffs_ref[0, :, lanes].astype(jnp.float32)
    place(
        columns,
        jnp.where(mine, near, far_coeffs[...].astype(jnp.float32)),
        jnp.where(mine, columns_ref[:, lanes], far_columns[...]),
    )
    chunks(per_device // 2, RADIX // 2, everyone)

    def far_rows(i, carry):
        chunk = lax.rem(own_chunks + 2 * i, RADIX)
        fill_design(chunk, basis_a, i, columns, rows)
        fill_design(chunk + 1, basis_b, i, columns, rows)
        return carry

    lax.fori_loop(0, per_device // 2, far_rows, 0)

    def turn(slot, pair, at, lane, value):
        re, im = value
        c = twiddle[2 * slot : 2 * slot + 1, lane : lane + 128]
        s = twiddle[2 * slot + 1 : 2 * slot + 2, lane : lane + 128]
        place_at = slot if slot < EVEN else slot - EVEN
        put_rows(pair, place_at, at, lane, re * c + im * s)
        put_rows(pair, place_at, at, length + lane, im * c - re * s)

    def fold_even(i, carry):
        at = pl.ds(pl.multiple_of(i * 16, 16), 16)
        for lane in range(0, length, 128):
            plain, pairs = even_classes(lambda q: design[q, at, lane : lane + 128])
            for slot, value in enumerate(plain):
                put_rows(real, slot, at, lane, value)
            for slot, value in enumerate(pairs):
                turn(slot, pair_even, at, lane, value)
        return carry

    def fold_odd(i):
        at = pl.ds(pl.multiple_of(i * 16, 16), 16)
        for lane in range(0, length, 128):
            for slot, value in enumerate(odd_classes(lambda q: design[q, at, lane : lane + 128])):
                turn(EVEN + slot, pair_odd, at, lane, value)

    loads[5].wait()
    lax.fori_loop(0, everyone // 16, fold_even, 0)

    def spectra_of(parts, matrix):
        high = parts[:, : parts.shape[1] // 2]
        return jnp.dot(
            jnp.concatenate([parts, high], axis=1), matrix, preferred_element_type=jnp.float32
        ).astype(jnp.bfloat16)

    def gram(spectra, weight):
        weighted = (spectra[:columns].astype(jnp.float32) * weight).astype(jnp.bfloat16)
        return lax.dot_general(
            spectra[columns:], weighted, (((1,), (1,)), ((), ())), preferred_element_type=jnp.float32
        )

    units = everyone // 16 // EVEN

    def even_step(slot, carry):
        spectra_even[slot] = spectra_of(pair_even[slot], mat[...])
        for unit in range(units):
            fold_odd(slot * units + unit)
        return carry

    lax.fori_loop(0, EVEN, even_step, 0)
    frequency_weights(psd_ref, wts, samples)
    summed = jnp.zeros((rows, columns), jnp.float32)
    for slot in range(len(CLASSES) - EVEN):
        spectra = spectra_of(pair_odd[slot], mat[...])
        summed = summed + gram(spectra, wts[slot + 2 + EVEN : slot + 3 + EVEN, :])
    for slot in range(2):
        spectra = spectra_of(real[slot], mat_real[slot])
        summed = summed + gram(spectra, wts[slot : slot + 1, 0:length])
    for slot in range(EVEN):
        summed = summed + gram(spectra_even[slot], wts[slot + 2 : slot + 3, :])
    total[...] = summed
    swap = pltpu.make_async_remote_copy(
        src_ref=total,
        dst_ref=other_ref,
        send_sem=side_send.at[2],
        recv_sem=side_recv.at[2],
        device_id={"comp": 1 - comp},
        device_id_type=MESH,
    )
    swap.start()
    own_ref[...] = total[...]
    swap.wait()


def fused(orbit_angles, gap_mask, column_index, lat_coeffs, psd_table):
    devices_tm = lax.axis_size("tm")
    block = orbit_angles.shape[1]
    samples = devices_tm * block
    length = samples // RADIX
    terms, columns = lat_coeffs.shape[1:]
    rows = columns * lax.axis_size("panel") // devices_tm
    everyone = rows + columns
    f32, bf16 = jnp.float32, jnp.bfloat16
    vmem = pl.BlockSpec(memory_space=pltpu.VMEM)
    count = len(CLASSES)
    own, other = pl.pallas_call(
        functools.partial(kernel, devices_tm),
        out_shape=[jax.ShapeDtypeStruct((rows, columns), f32)] * 2,
        in_specs=[pl.BlockSpec(memory_space=pltpu.HBM)] * 7,
        out_specs=[vmem] * 2,
        scratch_shapes=[
            pltpu.VMEM(column_index.shape, jnp.int32),
            pltpu.VMEM(lat_coeffs.shape, bf16),
            pltpu.VMEM(psd_table.shape, jnp.int32),
            pltpu.VMEM((devices_tm, 2, block), f32),
            pltpu.VMEM((devices_tm, 1, block), jnp.int32),
            pltpu.VMEM((terms, rows), bf16),
            pltpu.VMEM((2, rows), jnp.int32),
            pltpu.VMEM((everyone, terms), bf16),
            pltpu.VMEM((2 + len(SINE_LON), everyone, 128), f32),
            pltpu.VMEM((RADIX // 2, terms, length), bf16),
            pltpu.VMEM((RADIX // 2, terms, length), bf16),
            pltpu.VMEM((RADIX, everyone, length), f32),
            pltpu.VMEM((2, everyone, 2 * length), bf16),
            pltpu.VMEM((EVEN, everyone, 4 * length), bf16),
            pltpu.VMEM((count - EVEN, everyone, 4 * length), bf16),
            pltpu.VMEM((EVEN, everyone, 2 * length), bf16),
            pltpu.VMEM((2, 3 * length, length), bf16),
            pltpu.VMEM((6 * length, 2 * length), bf16),
            pltpu.VMEM((4, length, length), f32),
            pltpu.VMEM((2 * count, length), f32),
            pltpu.VMEM((16, 2 * length), f32),
            pltpu.VMEM((rows, columns), f32),
            pltpu.SemaphoreType.DMA((2, devices_tm)),
            pltpu.SemaphoreType.DMA((2, devices_tm)),
            pltpu.SemaphoreType.DMA((3,)),
            pltpu.SemaphoreType.DMA((3,)),
            pltpu.SemaphoreType.DMA((7,)),
        ],
        compiler_params=pltpu.CompilerParams(
            collective_id=0, has_side_effects=True, vmem_limit_bytes=63 * 1024 * 1024
        ),
    )(orbit_angles, gap_mask.reshape(1, block), column_index, lat_coeffs, psd_table, *tables(length))
    return own + other


def choose(orbit_angles, gap_mask, column_index, lat_coeffs, psd_table):
    devices_tm, panels = lax.axis_size("tm"), lax.axis_size("panel")
    samples = devices_tm * orbit_angles.shape[1]
    columns = lat_coeffs.shape[2]
    rows = columns * panels // devices_tm
    fits = (
        samples == 4096
        and orbit_angles.shape[1] % 512 == 0
        and panels == 2
        and lax.axis_size("comp") == 2
        and rows % 128 == 0
        and columns % rows == 0
        and lat_coeffs.shape[1] % 32 == 0
        and (rows + columns) * lat_coeffs.shape[1] <= 512 * 1024
    )
    step = fused if fits else body
    return step(orbit_angles, gap_mask, column_index, lat_coeffs, psd_table)


def solution(mesh):
    return jax.shard_map(
        choose,
        mesh=mesh,
        in_specs=(
            P(None, ("groups", "tm")),
            P(("groups", "tm")),
            P(None, "panel"),
            P("comp", None, "panel"),
            P("comp", None),
        ),
        out_specs=P(("groups", "tm"), "panel"),
        check_vma=False,
    )
```

```python
import functools
import math

import jax
import jax.numpy as jnp
import numpy as np
from jax import lax
from jax.experimental import pallas as pl
from jax.experimental.pallas import tpu as pltpu
from jax.sharding import PartitionSpec as P

SPLIT = 64


def synthesize(angles, keep_rows, column_index, coeffs):
    terms_lat = coeffs.shape[0] // 2
    colatitude = angles[0]
    longit = angles[1]
    wavenumbers = jnp.arange(terms_lat, dtype=jnp.float32)
    phases = colatitude[:, None] * wavenumbers[None, :]
    basis_rows = jnp.concatenate([jnp.cos(phases), jnp.sin(phases)], axis=1).astype(jnp.bfloat16)
    degree = column_index[0]
    orders = column_index[1]
    levels = jnp.arange(2 * terms_lat, dtype=jnp.int32) % terms_lat
    allowed = levels[:, None] <= degree[None, :]
    masked = jnp.where(allowed, coeffs, jnp.zeros_like(coeffs))
    latitude = jnp.dot(basis_rows, masked, preferred_element_type=jnp.float32)
    lon_phase = longit[:, None] * jnp.abs(orders).astype(jnp.float32)[None, :]
    lon_wave = jnp.where(orders[None, :] >= 0, jnp.cos(lon_phase), jnp.sin(lon_phase))
    norm_scale = 1.0 / jnp.sqrt(degree.astype(jnp.float32) + 1.0)
    return latitude * lon_wave * (keep_rows[:, None] * norm_scale[None, :])


def phase_tables(row_index, col_index, length):
    product = row_index[:, None] * col_index[None, :] % length
    angle_grid = product.astype(jnp.float32) * (2.0 * math.pi / length)
    return (jnp.cos(angle_grid), jnp.sin(angle_grid))


def dft_tables(length):
    indices = jnp.arange(length, dtype=jnp.int32)
    return phase_tables(indices, indices, length)


def rotate(real_part, imag_part, outer_index, inner_index, length):
    index_grid = outer_index[:, None] * inner_index[None, :] % length
    angle_grid = index_grid.astype(jnp.float32) * (2.0 * math.pi / length)
    cosine = jnp.cos(angle_grid)[:, :, None]
    sine_grid = jnp.sin(angle_grid)[:, :, None]
    return (real_part * cosine + imag_part * sine_grid, imag_part * cosine - real_part * sine_grid)


def precise_dot(left_side, right_side):
    return jnp.dot(
        left_side, right_side, precision=lax.Precision.HIGHEST, preferred_element_type=jnp.float32
    )


def transform(cos_table, sin_table, real_part, imag_part):
    new_real = precise_dot(cos_table, real_part) + precise_dot(sin_table, imag_part)
    new_imag = precise_dot(cos_table, imag_part) - precise_dot(sin_table, real_part)
    return (new_real, new_imag)


def four_step(real_in, imag_in, samples):
    length = real_in.shape[0]
    columns = real_in.shape[1]
    outer_count = SPLIT
    inner_count = length // SPLIT
    real_part = real_in.reshape(outer_count, inner_count * columns)
    imag_part = imag_in.reshape(outer_count, inner_count * columns)
    cos_outer, sin_outer = dft_tables(outer_count)
    real_part, imag_part = transform(cos_outer, sin_outer, real_part, imag_part)
    real_part = real_part.reshape(outer_count, inner_count, columns)
    imag_part = imag_part.reshape(outer_count, inner_count, columns)
    real_part, imag_part = rotate(
        real_part,
        imag_part,
        jnp.arange(outer_count, dtype=jnp.int32),
        jnp.arange(inner_count, dtype=jnp.int32),
        length,
    )
    real_part = jnp.transpose(real_part, (1, 0, 2)).reshape(inner_count, outer_count * columns)
    imag_part = jnp.transpose(imag_part, (1, 0, 2)).reshape(inner_count, outer_count * columns)
    cos_inner, sin_inner = dft_tables(inner_count)
    real_part, imag_part = transform(cos_inner, sin_inner, real_part, imag_part)
    return (
        real_part.reshape(length, columns) / samples,
        imag_part.reshape(length, columns) / samples,
    )


def local_transform(received, samples):
    real_part, imag_part = four_step(received[0, 0], received[1, 0], samples)
    return (real_part.astype(jnp.bfloat16), imag_part.astype(jnp.bfloat16))


def noise_weighted(spectra, psd_row, frequency, samples):
    folded = jnp.minimum(frequency, samples - frequency)
    inverse_psd = 8192.0 / jnp.take(psd_row, folded).astype(jnp.float32)
    return (spectra.astype(jnp.float32) * inverse_psd[None, :, None]).astype(jnp.bfloat16)


def settle(partial_value, sum_dim):
    summed = lax.psum_scatter(partial_value, "tm", scatter_dimension=sum_dim, tiled=True)
    return lax.psum(summed, "comp")


def body(orbit_angles, gap_mask, column_index, lat_coeffs, psd_table):
    devices_tm = lax.axis_size("tm")
    epochs = orbit_angles.shape[1]
    block_len = epochs // devices_tm
    samples = epochs * devices_tm
    columns = lat_coeffs.shape[2]
    coeffs = lat_coeffs[0]
    keep_rows = gap_mask.astype(jnp.float32)
    packed = jnp.concatenate([orbit_angles, keep_rows[None]], axis=0)[:, None, :]
    received = lax.all_to_all(packed, "tm", split_axis=2, concat_axis=1, tiled=True)
    flat_orbit = received.reshape(3, devices_tm * block_len)
    spread = synthesize(flat_orbit[0:2], flat_orbit[2], column_index, coeffs).reshape(
        devices_tm, block_len, columns
    )
    position = lax.axis_index("tm")
    local_epoch = position * block_len + jnp.arange(block_len, dtype=jnp.int32)
    cos_outer, sin_outer = dft_tables(devices_tm)
    flat_design = spread.reshape(devices_tm, block_len * columns)
    real_part = precise_dot(cos_outer, flat_design).reshape(devices_tm, block_len, columns)
    imag_part = -precise_dot(sin_outer, flat_design).reshape(devices_tm, block_len, columns)
    real_part, imag_part = rotate(
        real_part, imag_part, jnp.arange(devices_tm, dtype=jnp.int32), local_epoch, samples
    )
    twisted = jnp.stack([real_part, imag_part])
    spec_real, spec_imag = local_transform(
        lax.all_to_all(twisted, "tm", split_axis=1, concat_axis=2, tiled=True), samples
    )
    spectra = jnp.stack([spec_real, spec_imag])
    psd_row = psd_table[0]
    contract = (((0, 1), (0, 1)), ((), ()))
    frequency = position + devices_tm * jnp.arange(epochs, dtype=jnp.int32)
    weighted = noise_weighted(spectra, psd_row, frequency, samples)
    partial_value = lax.dot_general(
        lax.all_gather(spectra, "panel", axis=2, tiled=True),
        weighted,
        contract,
        preferred_element_type=jnp.float32,
    )
    return settle(partial_value, 0)


RADIX = 16
SINE_LON = (6.283164044168851, -41.33714234995496, 81.34076808172247, -70.99342472149007)
SINE_FINE = (
    6.283185160088548,
    -41.3416550311802,
    81.60100405747373,
    -76.54978191007581,
    39.53670300634923,
)
CLASSES = (2, 4, 6, 1, 5, 9, 13)
EVEN = 3
ROUNDER = 1.5 * 2.0**23
MESH = pl.DeviceIdType.MESH


def cos_turns(turns, terms=SINE_FINE):
    offset = turns - ((turns + ROUNDER) - ROUNDER)
    near = 0.25 - jnp.abs(offset)
    square = near * near
    total = terms[-1]
    for term in terms[-2::-1]:
        total = total * square + term
    return total * near


def iota(shape, dim):
    return lax.broadcasted_iota(jnp.int32, shape, dim)


def split(value):
    high = value.astype(jnp.bfloat16)
    return high, (value - high.astype(jnp.float32)).astype(jnp.bfloat16)


def tables(length):
    samples = RADIX * length
    half = length // 2

    def waves(product):
        angle = (product % samples) * (2.0 * np.pi / samples)
        return np.cos(angle), np.sin(angle)

    count = np.arange(length)
    cosine, sine = waves(RADIX * np.outer(count, count))
    zero = np.concatenate([cosine[:, :half], -sine[:, :half]], axis=1)
    zero[:, half] = 1 - 2 * (count % 2)
    eight = np.concatenate(waves(np.outer(count, RADIX // 2 + RADIX * count[:half])), axis=1)
    eight[:, half:] *= -1
    turn = [wave for cls in CLASSES for wave in waves(cls * count)]
    square = np.stack([cosine, sine, zero, eight]) / samples
    return square.astype(np.float32), np.stack(turn).astype(np.float32)


def put_matrix(ref, at, value, lanes):
    high, low = split(value)
    third = ref.shape[0] // 3
    for block, part in ((0, high), (1, high), (2, low)):
        start = block * third + at
        ref[start : start + value.shape[0], lanes] = part


def put_rows(ref, slot, rows, at, value):
    high, low = split(value)
    past = ref.shape[2] // 2 + at
    ref[slot, rows, at : at + value.shape[1]] = high
    ref[slot, rows, past : past + value.shape[1]] = low


def frequency_weights(psd_ref, wts_ref, samples):
    length = samples // RADIX
    half = length // 2
    power = jnp.concatenate([psd_ref[:, half * i : half * (i + 1)] for i in range(RADIX)], axis=0)
    spread = (iota((RADIX, half), 0) == iota((RADIX, half), 1) >> 3).astype(jnp.bfloat16)
    keep = (iota((half, half), 0) >> 4) == (iota((half, half), 1) & (half // RADIX - 1))
    pick_up = ((iota((RADIX, half), 1) & (RADIX - 1)) == iota((RADIX, half), 0)).astype(jnp.bfloat16)
    pick_down = ((iota((RADIX, half), 1) + iota((RADIX, half), 0)) & (RADIX - 1) == 0).astype(
        jnp.bfloat16
    )
    flip = (iota((half, half), 0) + iota((half, half), 1) == half - 1).astype(jnp.bfloat16)
    up = jnp.zeros((RADIX, half), jnp.float32)
    down = jnp.zeros((RADIX, half), jnp.float32)
    for digits, unit in ((power >> 8, 256.0), (power & 255, 1.0)):
        digits = digits.astype(jnp.float32).astype(jnp.bfloat16)
        moved = lax.dot_general(
            digits, spread, (((0,), (0,)), ((), ())), preferred_element_type=jnp.float32
        )
        moved = jnp.where(keep, moved, 0.0).astype(jnp.bfloat16)
        up = up + unit * jnp.dot(pick_up, moved, preferred_element_type=jnp.float32)
        back = jnp.dot(pick_down, moved, preferred_element_type=jnp.float32).astype(jnp.bfloat16)
        down = down + unit * jnp.dot(back, flip, preferred_element_type=jnp.float32)
    up = 2.0 * (8192.0 / up)
    down = 2.0 * (8192.0 / down)
    last = 8192.0 / psd_ref[:, samples // 2 : samples // 2 + 1].astype(jnp.float32)
    first = iota((1, half), 1) == 0
    wts_ref[0:1, 0:half] = jnp.where(first, 0.5 * up[0:1], up[0:1])
    wts_ref[0:1, half:length] = jnp.where(first, last, up[0:1])
    wts_ref[1:2, 0:half] = up[RADIX // 2 : RADIX // 2 + 1]
    wts_ref[1:2, half:length] = up[RADIX // 2 : RADIX // 2 + 1]
    for slot, cls in enumerate(CLASSES):
        for at in (0, length):
            wts_ref[slot + 2 : slot + 3, at : at + half] = up[cls : cls + 1]
            wts_ref[slot + 2 : slot + 3, at + half : at + length] = down[cls : cls + 1]


def even_classes(d):
    r = math.sqrt(0.5)
    even, alt = [], []
    for q in range(4):
        first, second = d(q) + d(q + 8), d(q + 4) + d(q + 12)
        even.append(first + second)
        alt.append(first - second)
    e02, e13 = even[0] + even[2], even[1] + even[3]
    four = (even[0] - even[2], even[3] - even[1])
    p, q = r * (alt[1] - alt[3]), r * (alt[1] + alt[3])
    two = (alt[0] + p, -(alt[2] + q))
    six = (alt[0] - p, alt[2] - q)
    return (e02 + e13, e02 - e13), (two, four, six)


def odd_classes(d):
    br, bi = [], []
    for q in range(4):
        real, imag = d(q) - d(q + 8), d(q + 12) - d(q + 4)
        c, s = math.cos(math.pi * q / 8), math.sin(math.pi * q / 8)
        if q == 2:
            real, imag = c * (real + imag), c * (imag - real)
        elif q:
            real, imag = c * real + s * imag, c * imag - s * real
        br.append(real)
        bi.append(imag)
    sr, si = br[0] + br[2], bi[0] + bi[2]
    tr, ti = br[1] + br[3], bi[1] + bi[3]
    ur, ui = br[0] - br[2], bi[0] - bi[2]
    vr, vi = br[1] - br[3], bi[1] - bi[3]
    return (sr + tr, si + ti), (ur + vi, ui - vr), (sr - tr, si - ti), (ur - vi, ui + vr)


def kernel(
    devices_tm,
    angles_hbm,
    mask_hbm,
    columns_hbm,
    coeffs_hbm,
    psd_hbm,
    square_hbm,
    twiddle_hbm,
    own_ref,
    other_ref,
    columns_ref,
    coeffs_ref,
    psd_ref,
    orbit,
    flags,
    far_coeffs,
    far_columns,
    coeffs_t,
    column_t,
    basis_a,
    basis_b,
    design,
    real,
    pair_even,
    pair_odd,
    spectra_even,
    mat_real,
    mat,
    square,
    twiddle,
    wts,
    total,
    send_sem,
    recv_sem,
    side_send,
    side_recv,
    load_sem,
):
    block = angles_hbm.shape[1]
    samples = block * devices_tm
    length = samples // RADIX
    half = length // 2
    terms = coeffs_ref.shape[1]
    terms_lat = terms // 2
    columns = coeffs_ref.shape[2]
    rows = own_ref.shape[0]
    everyone = rows + columns
    me = lax.axis_index("tm")
    panel = lax.axis_index("panel")
    comp = lax.axis_index("comp")

    barrier = pltpu.get_barrier_semaphore()
    peers = [lax.rem(me + k, devices_tm) for k in range(1, devices_tm)]
    for peer in peers:
        pl.semaphore_signal(barrier, inc=1, device_id={"tm": peer}, device_id_type=MESH)
    pl.semaphore_signal(barrier, inc=1, device_id={"panel": 1 - panel}, device_id_type=MESH)
    pl.semaphore_signal(barrier, inc=1, device_id={"comp": 1 - comp}, device_id_type=MESH)

    loads = [
        pltpu.make_async_copy(source, held, load_sem.at[i])
        for i, (source, held) in enumerate(
            (
                (angles_hbm, orbit.at[me]),
                (mask_hbm, flags.at[me]),
                (columns_hbm, columns_ref),
                (coeffs_hbm, coeffs_ref),
                (psd_hbm, psd_ref),
                (twiddle_hbm, twiddle),
                (square_hbm, square),
            )
        )
    ]
    for load in loads:
        load.start()
    pl.semaphore_wait(barrier, devices_tm + 1)

    def send_orbit(k, slot, peer):
        return [
            pltpu.make_async_remote_copy(
                src_ref=source,
                dst_ref=held.at[slot],
                send_sem=send_sem.at[i, k],
                recv_sem=recv_sem.at[i, slot],
                device_id={"tm": peer},
                device_id_type=MESH,
            )
            for i, (source, held) in enumerate(((angles_hbm, orbit), (mask_hbm, flags)))
        ]

    for k, peer in enumerate(peers):
        for copy in send_orbit(k, me, peer):
            copy.start()
    first_row = me * rows
    lanes = pl.ds(pl.multiple_of(lax.rem(first_row, columns), rows), rows)
    send_coeffs = pltpu.make_async_remote_copy(
        src_ref=coeffs_hbm.at[0, :, lanes],
        dst_ref=far_coeffs,
        send_sem=side_send.at[0],
        recv_sem=side_recv.at[0],
        device_id={"panel": 1 - panel},
        device_id_type=MESH,
    )
    send_columns = pltpu.make_async_remote_copy(
        src_ref=columns_hbm.at[:, lanes],
        dst_ref=far_columns,
        send_sem=side_send.at[1],
        recv_sem=side_recv.at[1],
        device_id={"panel": 1 - panel},
        device_id_type=MESH,
    )
    send_coeffs.start()
    send_columns.start()

    loads[4].wait()

    def place(at, coeffs, index_rows):
        width = coeffs.shape[1]
        level = iota((terms, width), 0)
        level = jnp.where(level < terms_lat, level, level - terms_lat)
        masked = jnp.where(level <= index_rows[0:1, :], coeffs, 0.0)
        coeffs_t[at : at + width, :] = jnp.transpose(masked).astype(jnp.bfloat16)
        orders = index_rows[1:2, :]
        shift = jnp.where(orders >= 0, 0.0, 0.25)
        norm = 1.0 / jnp.sqrt(index_rows[0:1, :].astype(jnp.float32) + 1.0)
        packed = jnp.concatenate(
            [jnp.abs(orders).astype(jnp.float32), shift]
            + [norm * term for term in SINE_LON]
            + [jnp.zeros((2, width), jnp.float32)],
            axis=0,
        )
        turned = jnp.transpose(packed)
        for i in range(2 + len(SINE_LON)):
            column_t[i, at : at + width, :] = jnp.broadcast_to(turned[:, i : i + 1], (width, 128))

    loads[2].wait()
    loads[3].wait()
    place(0, coeffs_ref[0].astype(jnp.float32), columns_ref[...])
    loads[0].wait()
    loads[1].wait()
    per_device = block // length

    def epoch_lanes(chunk):
        at = lax.rem(chunk, per_device) * length
        return chunk // per_device, pl.ds(pl.multiple_of(at, length), length)

    def fill_basis(chunk, basis, slot):
        holder, lanes = epoch_lanes(chunk)
        theta = orbit[holder, 0:1, lanes] * (0.5 / math.pi)
        keep = flags[holder, :, lanes].astype(jnp.float32)
        turns = iota((16, length), 0).astype(jnp.float32) * theta
        cosine, sine = cos_turns(turns) * keep, cos_turns(turns - 0.25) * keep
        step_c, step_s = cos_turns(16.0 * theta), cos_turns(16.0 * theta - 0.25)
        for at in range(0, terms_lat, 16):
            basis[slot, at : at + 16, :] = cosine.astype(jnp.bfloat16)
            basis[slot, terms_lat + at : terms_lat + at + 16, :] = sine.astype(jnp.bfloat16)
            cosine, sine = cosine * step_c - sine * step_s, sine * step_c + cosine * step_s

    def fill_design(chunk, basis, slot, at, width):
        holder, lanes = epoch_lanes(chunk)
        longit = orbit[holder, 1:2, lanes] * (0.5 / math.pi)
        these = slice(at, at + width)
        latitude = jnp.dot(coeffs_t[these, :], basis[slot], preferred_element_type=jnp.float32)
        terms_lon = [column_t[2 + i, these, :] for i in range(len(SINE_LON))]
        for lane in range(0, length, 128):
            where = slice(lane, lane + 128)
            wave = cos_turns(
                column_t[0, these, :] * longit[:, where] - column_t[1, these, :], terms_lon
            )
            design[chunk, these, where] = latitude[:, where] * wave

    own_chunks = me * per_device

    def near_columns(first, last):
        def two_chunks(i, carry):
            chunk = lax.rem(own_chunks + 2 * i, RADIX)
            again = jnp.where(i + 1 < last, i + 1, first)
            fill_basis(chunk + 1, basis_b, i)
            fill_design(chunk, basis_a, i, 0, columns)
            fill_basis(lax.rem(own_chunks + 2 * again, RADIX), basis_a, again)
            fill_design(chunk + 1, basis_b, i, 0, columns)
            return carry

        fill_basis(lax.rem(own_chunks + 2 * first, RADIX), basis_a, first)
        lax.fori_loop(first, last, two_chunks, 0)

    near_columns(0, per_device // 2)
    for k, peer in enumerate(peers):
        for copy in send_orbit(k, me, peer):
            copy.wait_send()
        for copy in send_orbit(k, peer, peer):
            copy.wait_recv()

    near_columns(per_device // 2, RADIX // 2)
    loads[6].wait()
    left, right = slice(0, length), slice(length, 2 * length)
    put_matrix(mat, 0, square[0], left)
    put_matrix(mat, 0, -square[1], right)
    put_matrix(mat, length, square[1], left)
    put_matrix(mat, length, square[0], right)
    put_matrix(mat_real.at[0], 0, square[2], left)
    put_matrix(mat_real.at[1], 0, square[3], left)
    send_coeffs.wait()
    send_columns.wait()
    mine = first_row // columns == panel
    near = coeffs_ref[0, :, lanes].astype(jnp.float32)
    place(
        columns,
        jnp.where(mine, near, far_coeffs[...].astype(jnp.float32)),
        jnp.where(mine, columns_ref[:, lanes], far_columns[...]),
    )

    def far_rows(i, carry):
        chunk = lax.rem(own_chunks + 2 * i, RADIX)
        fill_design(chunk, basis_a, i, columns, rows)
        fill_design(chunk + 1, basis_b, i, columns, rows)
        return carry

    lax.fori_loop(0, RADIX // 2, far_rows, 0)

    def turn(slot, pair, at, lane, value):
        re, im = value
        c = twiddle[2 * slot : 2 * slot + 1, lane : lane + 128]
        s = twiddle[2 * slot + 1 : 2 * slot + 2, lane : lane + 128]
        place_at = slot if slot < EVEN else slot - EVEN
        put_rows(pair, place_at, at, lane, re * c + im * s)
        put_rows(pair, place_at, at, length + lane, im * c - re * s)

    def fold_even(i, carry):
        at = pl.ds(pl.multiple_of(i * 16, 16), 16)
        for lane in range(0, length, 128):
            plain, pairs = even_classes(lambda q: design[q, at, lane : lane + 128])
            for slot, value in enumerate(plain):
                put_rows(real, slot, at, lane, value)
            for slot, value in enumerate(pairs):
                turn(slot, pair_even, at, lane, value)
        return carry

    def fold_odd(i):
        at = pl.ds(pl.multiple_of(i * 16, 16), 16)
        for lane in range(0, length, 128):
            for slot, value in enumerate(odd_classes(lambda q: design[q, at, lane : lane + 128])):
                turn(EVEN + slot, pair_odd, at, lane, value)

    loads[5].wait()
    lax.fori_loop(0, everyone // 16, fold_even, 0)

    def spectra_of(parts, matrix):
        high = parts[:, : parts.shape[1] // 2]
        return jnp.dot(
            jnp.concatenate([parts, high], axis=1), matrix, preferred_element_type=jnp.float32
        ).astype(jnp.bfloat16)

    def gram(spectra, weight):
        weighted = (spectra[:columns].astype(jnp.float32) * weight).astype(jnp.bfloat16)
        return lax.dot_general(
            spectra[columns:], weighted, (((1,), (1,)), ((), ())), preferred_element_type=jnp.float32
        )

    units = everyone // 16 // EVEN

    def even_step(slot, carry):
        spectra_even[slot] = spectra_of(pair_even[slot], mat[...])
        for unit in range(units):
            fold_odd(slot * units + unit)
        return carry

    lax.fori_loop(0, EVEN, even_step, 0)
    frequency_weights(psd_ref, wts, samples)
    summed = jnp.zeros((rows, columns), jnp.float32)
    for slot in range(len(CLASSES) - EVEN):
        spectra = spectra_of(pair_odd[slot], mat[...])
        summed = summed + gram(spectra, wts[slot + 2 + EVEN : slot + 3 + EVEN, :])
    for slot in range(2):
        spectra = spectra_of(real[slot], mat_real[slot])
        summed = summed + gram(spectra, wts[slot : slot + 1, 0:length])
    for slot in range(EVEN):
        summed = summed + gram(spectra_even[slot], wts[slot + 2 : slot + 3, :])
    total[...] = summed
    swap = pltpu.make_async_remote_copy(
        src_ref=total,
        dst_ref=other_ref,
        send_sem=side_send.at[2],
        recv_sem=side_recv.at[2],
        device_id={"comp": 1 - comp},
        device_id_type=MESH,
    )
    swap.start()
    own_ref[...] = total[...]
    swap.wait()


def fused(orbit_angles, gap_mask, column_index, lat_coeffs, psd_table):
    devices_tm = lax.axis_size("tm")
    block = orbit_angles.shape[1]
    samples = devices_tm * block
    length = samples // RADIX
    terms, columns = lat_coeffs.shape[1:]
    rows = columns * lax.axis_size("panel") // devices_tm
    everyone = rows + columns
    f32, bf16 = jnp.float32, jnp.bfloat16
    vmem = pl.BlockSpec(memory_space=pltpu.VMEM)
    count = len(CLASSES)
    own, other = pl.pallas_call(
        functools.partial(kernel, devices_tm),
        out_shape=[jax.ShapeDtypeStruct((rows, columns), f32)] * 2,
        in_specs=[pl.BlockSpec(memory_space=pltpu.HBM)] * 7,
        out_specs=[vmem] * 2,
        scratch_shapes=[
            pltpu.VMEM(column_index.shape, jnp.int32),
            pltpu.VMEM(lat_coeffs.shape, bf16),
            pltpu.VMEM(psd_table.shape, jnp.int32),
            pltpu.VMEM((devices_tm, 2, block), f32),
            pltpu.VMEM((devices_tm, 1, block), jnp.int32),
            pltpu.VMEM((terms, rows), bf16),
            pltpu.VMEM((2, rows), jnp.int32),
            pltpu.VMEM((everyone, terms), bf16),
            pltpu.VMEM((2 + len(SINE_LON), everyone, 128), f32),
            pltpu.VMEM((RADIX // 2, terms, length), bf16),
            pltpu.VMEM((RADIX // 2, terms, length), bf16),
            pltpu.VMEM((RADIX, everyone, length), f32),
            pltpu.VMEM((2, everyone, 2 * length), bf16),
            pltpu.VMEM((EVEN, everyone, 4 * length), bf16),
            pltpu.VMEM((count - EVEN, everyone, 4 * length), bf16),
            pltpu.VMEM((EVEN, everyone, 2 * length), bf16),
            pltpu.VMEM((2, 3 * length, length), bf16),
            pltpu.VMEM((6 * length, 2 * length), bf16),
            pltpu.VMEM((4, length, length), f32),
            pltpu.VMEM((2 * count, length), f32),
            pltpu.VMEM((16, 2 * length), f32),
            pltpu.VMEM((rows, columns), f32),
            pltpu.SemaphoreType.DMA((2, devices_tm)),
            pltpu.SemaphoreType.DMA((2, devices_tm)),
            pltpu.SemaphoreType.DMA((3,)),
            pltpu.SemaphoreType.DMA((3,)),
            pltpu.SemaphoreType.DMA((7,)),
        ],
        compiler_params=pltpu.CompilerParams(
            collective_id=0, has_side_effects=True, vmem_limit_bytes=63 * 1024 * 1024
        ),
    )(orbit_angles, gap_mask.reshape(1, block), column_index, lat_coeffs, psd_table, *tables(length))
    return own + other


def choose(orbit_angles, gap_mask, column_index, lat_coeffs, psd_table):
    devices_tm, panels = lax.axis_size("tm"), lax.axis_size("panel")
    samples = devices_tm * orbit_angles.shape[1]
    columns = lat_coeffs.shape[2]
    rows = columns * panels // devices_tm
    fits = (
        samples == 4096
        and orbit_angles.shape[1] % 512 == 0
        and panels == 2
        and lax.axis_size("comp") == 2
        and rows % 128 == 0
        and columns % rows == 0
        and lat_coeffs.shape[1] % 32 == 0
        and (rows + columns) * lat_coeffs.shape[1] <= 512 * 1024
    )
    step = fused if fits else body
    return step(orbit_angles, gap_mask, column_index, lat_coeffs, psd_table)


def solution(mesh):
    return jax.shard_map(
        choose,
        mesh=mesh,
        in_specs=(
            P(None, ("groups", "tm")),
            P(("groups", "tm")),
            P(None, "panel"),
            P("comp", None, "panel"),
            P("comp", None),
        ),
        out_specs=P(("groups", "tm"), "panel"),
        check_vma=False,
    )
```
